128 devices in a mesh: win: 4 (over y), seq: 16 (over z, x), heads: 2 (over core).
Axes of the slice: x: 4, y: 4, z: 4, core: 2. Of those that a mesh axis runs over, the one named last changes fastest.
Arguments:
- tokens: bfloat16 [4, 8192, 768], P('win', ('seq', 'heads')), may hold values from -6 to 6
- first_gain: float32 [768], replicated, may hold values from 0.5 to 1.5
- first_shift: float32 [768], replicated, may hold values from -1.75 to 1.75
- query_weight: bfloat16 [768, 768], P(None, 'heads'), may hold values from -0.5 to 0.5
- query_bias: float32 [768], P('heads'), may hold values from -3 to 3
- keyval_weight: bfloat16 [768, 128], replicated, may hold values from -0.21875 to 0.21875
- value_bias: float32 [64], replicated, may hold values from -1.75 to 1.75
- out_weight: bfloat16 [768, 768], P('heads'), may hold values from -0.4375 to 0.4375
- out_bias: float32 [768], replicated, may hold values from -1.75 to 1.75
- second_gain: float32 [768], replicated, may hold values from 0.5 to 1.5
- second_shift: float32 [768], replicated, may hold values from -1.75 to 1.75
- expand_weight: bfloat16 [768, 3072], P(None, 'heads'), may hold values from -0.21875 to 0.21875
- expand_bias: float32 [3072], P('heads'), may hold values from -1.75 to 1.75
- contract_weight: bfloat16 [3072, 768], P('heads'), may hold values from -0.109375 to 0.109375
- contract_bias: float32 [768], replicated, may hold values from -1.75 to 1.75
- cotangent: bfloat16 [4, 8192, 768], P('win', ('seq', 'heads')), may hold values from -6 to 6
- lengths: int32 [4, 8], P('win'), may hold values from 1 to 8064, 8192 in all within a row
Outputs:
- block_out: bfloat16 [4, 8192, 768], P('win', ('seq', 'heads'))
- tokens_grad: float32 [4, 8192, 768], P('win', ('seq', 'heads'))
- first_gain_grad: float32 [768], replicated
- first_shift_grad: float32 [768], replicated
- query_weight_grad: float32 [768, 768], P(None, 'heads')
- query_bias_grad: float32 [768], P('heads')
- keyval_weight_grad: float32 [768, 128], replicated
- value_bias_grad: float32 [64], replicated
- out_weight_grad: float32 [768, 768], P('heads')
- out_bias_grad: float32 [768], replicated
- second_gain_grad: float32 [768], replicated
- second_shift_grad: float32 [768], replicated
- expand_weight_grad: float32 [768, 3072], P(None, 'heads')
- expand_bias_grad: float32 [3072], P('heads')
- contract_weight_grad: float32 [3072, 768], P('heads')
- contract_bias_grad: float32 [768], replicated
The draws below stay inside these ranges and needn't reach their ends.
Inputs may be any that keep to these rules, and one draw needn't show every extreme that they name: In each window the 8 file lengths add up to 8192, and the longest file has exactly 8064 tokens.
All inputs are finite; a program needn't handle non-finite values.
Results may differ from the reference program's by a relative error of at most 0.018.
Values may be sent and summed in bfloat16 or wider, within the bound.
No kernel may reach another device: no remote copies, remote signals or barrier semaphores. Data moves between devices by JAX's collectives and lax.ppermute only.
A program may use at most 192 MiB of HBM per device.

```python
import math
import jax
import jax.numpy as jnp
import numpy as np
from jax import lax

D = 768
H = 12
DH = 64
FF = 3072
FILES = 8
WINDOWS = 4
WLEN = 8192
RDEV = 256


def block_levels(stream_key, dims, split, smallest, largest):
    loudness, own = 1.0, jax.random.fold_in(stream_key, 6)
    for dim, blocks in split:
        heights = jnp.exp(jax.random.uniform(jax.random.fold_in(own, dim), (blocks,), jnp.float32, smallest / len(split), largest / len(split)))
        loudness = loudness * jnp.repeat(heights, dims[dim] // blocks).reshape([-1 if axis == dim else 1 for axis in range(len(dims))])
    return loudness


def profile(number_of, total, reach, lean):
    loads = [(1 << 20) // math.isqrt(standing ** lean) + 1 for standing in range(2, number_of + 1)]
    spare, holding = total - reach - (number_of - 1), [1] * (number_of - 1)
    while spare > 0:
        movable = [i for i in range(number_of - 1) if holding[i] < reach]
        whole, left = sum([loads[i] for i in movable]), spare
        for i in movable:
            extra = min(reach - holding[i], max(1, left * loads[i] // whole), spare)
            holding[i] = holding[i] + extra
            spare = spare - extra
    return np.array([reach] + holding)


def ragged_sizes(stream_key, count, total, bound, skew):
    if count == 2:
        one = jax.random.randint(stream_key, (), max(1, total - bound), min(bound, total - 1) + 1)
        return jnp.stack([one, total - one])
    sizes = jnp.asarray(profile(count, total, bound, skew), jnp.int32)
    pairs = (count - 1) // 2
    donor, sink = sizes[1:1 + 2 * pairs:2], sizes[2:2 + 2 * pairs:2]
    room = jnp.minimum(donor - 1, bound - sink)
    passed = jax.random.randint(jax.random.fold_in(stream_key, 1), (pairs,), 0, 1 << 20) % (room + 1)
    sizes = sizes.at[1:1 + 2 * pairs:2].set(donor - passed).at[2:2 + 2 * pairs:2].set(sink + passed)
    return sizes[jax.random.permutation(jax.random.fold_in(stream_key, 2), count)]


def gaussian(rng, extent, scale, reach, pieces=(), kind=jnp.bfloat16):
    loudness = block_levels(rng, extent, pieces, -0.22, 0.18) if pieces else 1.0
    array = jax.random.normal(rng, extent, jnp.float32) * scale * loudness
    return jnp.minimum(jnp.maximum(array, -reach), reach).astype(kind)


def setup_inputs(seed: int = 0) -> dict:
    key_list = jax.random.split(jax.random.key(seed), 18)
    return {
        "tokens": gaussian(key_list[0], (WINDOWS, WLEN, D), 1.0, 6.0, ((0, 4), (1, 32))),
        "first_gain": jnp.clip(1.0 + 0.1 * jax.random.normal(key_list[1], (D,), jnp.float32), 0.5, 1.5),
        "first_shift": gaussian(key_list[2], (D,), 0.3, 1.75, (), jnp.float32),
        "query_weight": gaussian(key_list[3], (D, D), (D // 6) ** -0.5, 0.5, ((1, 2),)),
        "query_bias": gaussian(key_list[4], (D,), 0.5, 3.0, ((0, 2),), jnp.float32),
        "keyval_weight": gaussian(key_list[5], (D, 2 * DH), D ** -0.5, 0.21875),
        "value_bias": gaussian(key_list[6], (DH,), 0.3, 1.75, (), jnp.float32),
        "out_weight": gaussian(key_list[7], (D, D), (D // 4) ** -0.5, 0.4375, ((0, 2),)),
        "out_bias": gaussian(key_list[8], (D,), 0.3, 1.75, (), jnp.float32),
        "second_gain": jnp.clip(1.0 + 0.1 * jax.random.normal(key_list[9], (D,), jnp.float32), 0.5, 1.5),
        "second_shift": gaussian(key_list[10], (D,), 0.3, 1.75, (), jnp.float32),
        "expand_weight": gaussian(key_list[11], (D, FF), D ** -0.5, 0.21875, ((1, 2),)),
        "expand_bias": gaussian(key_list[12], (FF,), 0.3, 1.75, ((0, 2),), jnp.float32),
        "contract_weight": gaussian(key_list[13], (FF, D), FF ** -0.5, 0.109375, ((0, 2),)),
        "contract_bias": gaussian(key_list[14], (D,), 0.3, 1.75, (), jnp.float32),
        "cotangent": gaussian(key_list[15], (WINDOWS, WLEN, D), 1.0, 6.0, ((0, 4), (1, 32))),
        "lengths": jax.vmap(lambda own: ragged_sizes(own, FILES, WLEN, WLEN - RDEV // 2, 2))(jax.random.split(key_list[16], WINDOWS)).reshape((WINDOWS, FILES)).astype(jnp.int32),
    }


EPS = 1e-05
NEG = -1e+30

@jax.custom_vjp
def low(v):
    return lax.optimization_barrier(v.astype(jnp.bfloat16)).astype(jnp.float32)

@jax.custom_vjp
def low_back(v):
    return v

def low_keep(v):
    return (low(v), None)

def low_pass(kept, grad):
    return (grad,)

def back_keep(v):
    return (v, None)

def back_low(kept, grad):
    return (low(grad),)
low.defvjp(low_keep, low_pass)
low_back.defvjp(back_keep, back_low)

def matmul(left, right):
    return jnp.dot(left, right, precision=lax.Precision.HIGHEST, preferred_element_type=jnp.float32)

def layer_norm(values, gain, shift):
    center = values - lax.optimization_barrier(jnp.mean(values, axis=-1, keepdims=True))
    spread = lax.optimization_barrier(jnp.mean(center * center, axis=-1, keepdims=True))
    return center * lax.rsqrt(spread + EPS) * gain + shift

def gelu_tanh(values):
    return jax.nn.gelu(values, approximate=True)

def file_ids(lengths, positions):
    bounds = jnp.cumsum(lengths).astype(jnp.int32)
    return lax.optimization_barrier(jnp.sum((positions[:, None] >= bounds[None, :]).astype(jnp.int32), axis=1)).astype(jnp.int32)

def forward(inputs, first_gain, first_shift, query_weight, query_bias, keyval_weight, value_bias, out_weight, out_bias, second_gain, second_shift, expand_weight, expand_bias, contract_weight, contract_bias, allowed):
    length = inputs.shape[0]
    scale = 1.0 / math.sqrt(DH)
    normed = low(layer_norm(inputs, first_gain, first_shift))
    query = low(low_back(matmul(normed, query_weight) + query_bias))
    keyval_shift = jnp.concatenate([jnp.zeros((DH,), jnp.float32), value_bias])
    keyval = low(low_back(matmul(normed, keyval_weight) + keyval_shift))
    keys = keyval[:, :DH]
    values = keyval[:, DH:]
    per_head = query.reshape(length, H, DH).transpose(1, 0, 2)

    def one_head(head_query):
        scores = low_back(matmul(head_query, keys.T) * scale)
        masked = jnp.where(allowed, scores, NEG)
        highest = lax.optimization_barrier(jnp.max(masked, axis=-1, keepdims=True))
        expo = jnp.exp(masked - highest)
        probs = low(expo / lax.optimization_barrier(jnp.sum(expo, axis=-1, keepdims=True)))
        return low(low_back(matmul(probs, values)))
    attended = lax.map(jax.checkpoint(one_head), per_head)
    attended = attended.transpose(1, 0, 2).reshape(length, H * DH)
    middle = inputs + low_back(matmul(attended, out_weight)) + out_bias
    normed2 = low(layer_norm(middle, second_gain, second_shift))
    inner = low_back(matmul(normed2, expand_weight) + expand_bias)
    acts = low(gelu_tanh(inner))
    return middle + low_back(matmul(acts, contract_weight)) + contract_bias

def reference(tokens, first_gain, first_shift, query_weight, query_bias, keyval_weight, value_bias, out_weight, out_bias, second_gain, second_shift, expand_weight, expand_bias, contract_weight, contract_bias, cotangent, lengths):
    params = (first_gain.astype(jnp.float32), first_shift.astype(jnp.float32), query_weight.astype(jnp.float32), query_bias.astype(jnp.float32), keyval_weight.astype(jnp.float32), value_bias.astype(jnp.float32), out_weight.astype(jnp.float32), out_bias.astype(jnp.float32), second_gain.astype(jnp.float32), second_shift.astype(jnp.float32), expand_weight.astype(jnp.float32), expand_bias.astype(jnp.float32), contract_weight.astype(jnp.float32), contract_bias.astype(jnp.float32))
    positions = jnp.arange(WLEN, dtype=jnp.int32)

    def window(carry, packed):
        inputs, grad_out, file_lengths = packed
        files = file_ids(file_lengths, positions)
        allowed = (files[:, None] == files[None, :]) & (positions[None, :] <= positions[:, None])

        def apply_block(inputs_f, *weights):
            return forward(inputs_f, *weights, allowed)
        output, pull = jax.vjp(apply_block, inputs.astype(jnp.float32), *params)
        grads = pull(grad_out.astype(jnp.float32))
        summed = tuple((total + piece for total, piece in zip(carry, grads[1:])))
        return (summed, (output.astype(jnp.bfloat16), grads[0]))
    start = tuple((jnp.zeros_like(param) for param in params))
    sums, (outputs, input_grads) = lax.scan(window, start, (tokens, cotangent, lengths))
    return (outputs, input_grads, sums[0], sums[1], sums[2], sums[3], sums[4], sums[5], sums[6], sums[7], sums[8], sums[9], sums[10], sums[11], sums[12], sums[13])
```

```python
import math
import jax
import jax.numpy as jnp
from jax import lax
from jax.experimental import pallas as pl
from jax.experimental.pallas import tpu as pltpu
from jax.sharding import PartitionSpec as P

DH = 64
NEG = -1e30
TILE = 256
LANES = 256
HALF = 128


def mm(left, right):
    return lax.dot_general(left, right, (((1,), (0,)), ((), ())), preferred_element_type=jnp.float32)


def pieces(row, width):
    high = row.astype(jnp.bfloat16).astype(jnp.float32)
    rest = row - high
    mid = rest.astype(jnp.bfloat16).astype(jnp.float32)
    low = rest - mid
    which = lax.broadcasted_iota(jnp.int32, (16, width), 0)
    block = jnp.where(which == 0, -high, jnp.where(which == 1, -mid, jnp.where(which == 2, -low, 0.0)))
    return block.astype(jnp.bfloat16)


def with_ones(part):
    lane = lax.broadcasted_iota(jnp.int32, (part.shape[0], HALF), 1)
    wide = jnp.concatenate([part, jnp.zeros_like(part)], axis=1)
    return jnp.where((lane >= DH) & (lane < DH + 3), jnp.ones_like(wide), wide)


def allowed_in(tile, chunk_pos, starts):
    key = tile * TILE + lax.broadcasted_iota(jnp.int32, (TILE, LANES), 0)
    lane = lax.broadcasted_iota(jnp.int32, (1, LANES), 1)
    query = chunk_pos + lax.rem(lane, HALF)
    return (key <= query) & (key >= starts)


def block_of(own_ref, peer_ref, place, tile):
    pair = lax.div(tile, 2)
    own = lax.rem(tile, 2) == lax.rem(place, 2)
    return jnp.where(own, own_ref[pair], peer_ref[pair])


def positions(place):
    return (place * 2 * HALF, 63 * HALF - place * 2 * HALF)


def forward_kernel(place_ref, query_ref, own_ref, peer_ref, starts_ref, attended_ref, out_ref, log_ref, kx, vt, qt, acc, high):
    subs = qt.shape[2] // LANES
    chunk_pos = positions(place_ref[0])
    zero = jnp.zeros((16, LANES), jnp.bfloat16)

    def prepare(tile, _):
        rows = pl.ds(pl.multiple_of(tile * TILE, TILE), TILE)
        block = block_of(own_ref, peer_ref, place_ref[0], tile)
        kx[rows, :] = with_ones(block[:, :DH])
        vt[:DH, rows] = block[:, DH:].T
        return 0

    lax.fori_loop(0, jnp.maximum(chunk_pos[0], chunk_pos[1]) // TILE + 1, prepare, 0)
    vt[DH:, :] = jnp.ones_like(vt[DH:, :])

    for c in range(2):
        diag = chunk_pos[c] // TILE
        starts = jnp.concatenate([starts_ref[c], starts_ref[c]], axis=1)
        for s in range(subs):
            cols = slice(s * LANES, (s + 1) * LANES)
            pair = query_ref[c * HALF : (c + 1) * HALF, s * 2 * DH : (s + 1) * 2 * DH].T
            qt[c, :DH, cols] = jnp.concatenate([pair[:DH], pair[DH:]], axis=1)
            qt[c, DH + 16 :, cols] = jnp.zeros_like(qt[c, DH + 16 :, cols])

        def rows_of(tile):
            return pl.ds(pl.multiple_of(tile * TILE, TILE), TILE)

        def set_shift(values, middle):
            for s in range(subs):
                cols = slice(s * LANES, (s + 1) * LANES)
                if values is None:
                    block = zero
                else:
                    row = values[c, :1, cols]
                    if middle:
                        row = jnp.where(starts <= TILE, row, -NEG)
                    block = pieces(row, LANES)
                qt[c, DH : DH + 16, cols] = block

        def scores(tile, s):
            return mm(kx[rows_of(tile), :], qt[c, :, s * LANES : (s + 1) * LANES])

        def take_max(tile, masked, fresh):
            for s in range(subs):
                cols = slice(s * LANES, (s + 1) * LANES)
                st = scores(tile, s)
                if masked:
                    st = jnp.where(allowed_in(tile, chunk_pos[c], starts), st, NEG)
                top = jnp.max(st, axis=0, keepdims=True)
                if not fresh:
                    top = jnp.maximum(top, high[c, :1, cols])
                high[c, :1, cols] = top

        def add(tile, masked, fresh):
            rows = rows_of(tile)
            sts = [scores(tile, s) for s in range(subs)]
            if masked:
                sts = [jnp.where(allowed_in(tile, chunk_pos[c], starts), st, NEG) for st in sts]
            ps = [jnp.exp(st).astype(jnp.bfloat16) for st in sts]
            for s in range(subs):
                cols = slice(s * LANES, (s + 1) * LANES)
                part = mm(vt[:, rows], ps[s])
                if fresh:
                    acc[c, :, cols] = part
                else:
                    acc[c, :, cols] += part

        def sweep():
            set_shift(high, False)
            add(diag, True, True)

            @pl.when(diag > 0)
            def _():
                add(0, True, False)
                set_shift(high, True)

                def step(tile, _):
                    add(tile, False, False)
                    return 0

                lax.fori_loop(1, diag, step, 0)

        set_shift(None, False)
        take_max(diag, True, True)
        sweep()
        total = acc[c, DH : DH + 1, :]

        @pl.when(jnp.logical_not(jnp.max(total) < 1e30))
        def _():
            set_shift(None, False)
            take_max(diag, True, True)

            @pl.when(diag > 0)
            def _():
                take_max(0, True, False)

                def step(tile, _):
                    for s in range(subs):
                        cols = slice(s * LANES, (s + 1) * LANES)
                        st = jnp.where(starts <= TILE, scores(tile, s), NEG)
                        high[c, :1, cols] = jnp.maximum(high[c, :1, cols], jnp.max(st, axis=0, keepdims=True))
                    return 0

                lax.fori_loop(1, diag, step, 0)

            sweep()

        for s in range(subs):
            cols = slice(s * LANES, (s + 1) * LANES)
            total = acc[c, DH : DH + 1, cols]
            result = acc[c, :DH, cols] / total
            out_ref[c, :, cols] = result
            log_ref[c, :, cols] = high[c, :1, cols] + jnp.log(total)
            stacked = jnp.concatenate([result[:, :HALF], result[:, HALF:]], axis=0)
            attended_ref[c * HALF : (c + 1) * HALF, s * 2 * DH : (s + 1) * 2 * DH] = stacked.astype(jnp.bfloat16).T


def backward_kernel(
    place_ref, query_ref, own_ref, peer_ref, starts_ref, grad_ref, out_ref, log_ref,
    dquery_ref, mine_ref, theirs_ref, kx, vx, kt, qt, gt, wq, wg, dq, dkv,
):
    subs = qt.shape[2] // LANES
    place = place_ref[0]
    chunk_pos = positions(place)

    def prepare(tile, _):
        rows = pl.ds(pl.multiple_of(tile * TILE, TILE), TILE)
        block = block_of(own_ref, peer_ref, place, tile)
        kx[rows, :] = with_ones(block[:, :DH])
        vx[rows, :] = with_ones(block[:, DH:])
        kt[:, rows] = block[:, :DH].T
        return 0

    lax.fori_loop(0, jnp.maximum(chunk_pos[0], chunk_pos[1]) // TILE + 1, prepare, 0)
    dkv[...] = jnp.zeros_like(dkv)

    for c in range(2):
        diag = chunk_pos[c] // TILE
        starts = jnp.concatenate([starts_ref[c], starts_ref[c]], axis=1)
        empty = jnp.zeros((HALF, DH), jnp.bfloat16)
        for s in range(subs):
            cols = slice(s * LANES, (s + 1) * LANES)
            q2 = query_ref[c * HALF : (c + 1) * HALF, s * 2 * DH : (s + 1) * 2 * DH]
            g2 = grad_ref[c * HALF : (c + 1) * HALF, s * 2 * DH : (s + 1) * 2 * DH]
            q2t, g2t = q2.T, g2.T
            qt[c, :DH, cols] = jnp.concatenate([q2t[:DH], q2t[DH:]], axis=1)
            grad_t = jnp.concatenate([g2t[:DH], g2t[DH:]], axis=1)
            gt[c, :DH, cols] = grad_t
            qt[c, DH + 16 :, cols] = jnp.zeros_like(qt[c, DH + 16 :, cols])
            gt[c, DH + 16 :, cols] = jnp.zeros_like(gt[c, DH + 16 :, cols])
            delta = jnp.sum(grad_t.astype(jnp.float32) * out_ref[c, :, cols], axis=0, keepdims=True)
            gt[c, DH : DH + 16, cols] = pieces(delta, LANES)
            for h in range(2):
                rows = slice(h * HALF, (h + 1) * HALF)
                wq[c, s, rows, :] = jnp.concatenate([q2[:, h * DH : (h + 1) * DH], empty], axis=1)
                wg[c, s, rows, :] = jnp.concatenate([empty, g2[:, h * DH : (h + 1) * DH]], axis=1)

        def set_shift(middle):
            for s in range(subs):
                cols = slice(s * LANES, (s + 1) * LANES)
                row = log_ref[c, :, cols]
                if middle:
                    row = jnp.where(starts <= TILE, row, -NEG)
                qt[c, DH : DH + 16, cols] = pieces(row, LANES)

        def add(tile, masked, fresh):
            rows = pl.ds(pl.multiple_of(tile * TILE, TILE), TILE)
            total = jnp.zeros((TILE, 2 * DH), jnp.float32)
            for base in range(0, subs, 3):
                group = range(base, base + 3)
                spans = [slice(s * LANES, (s + 1) * LANES) for s in group]
                sts = [mm(kx[rows, :], qt[c, :, cols]) for cols in spans]
                dps = [mm(vx[rows, :], gt[c, :, cols]) for cols in spans]
                if masked:
                    sts = [jnp.where(allowed_in(tile, chunk_pos[c], starts), st, NEG) for st in sts]
                probs = [jnp.exp(st) for st in sts]
                dss = [(p * dp).astype(jnp.bfloat16) for p, dp in zip(probs, dps)]
                lows = [p.astype(jnp.bfloat16) for p in probs]
                for s, ds, low in zip(group, dss, lows):
                    total = total + (mm(ds, wq[c, s]) + mm(low, wg[c, s]))
                for cols, ds in zip(spans, dss):
                    part = mm(kt[:, rows], ds)
                    if fresh:
                        dq[c, :, cols] = part
                    else:
                        dq[c, :, cols] += part
            dkv[rows, :] += total

        set_shift(False)
        add(diag, True, True)

        @pl.when(diag > 0)
        def _():
            add(0, True, False)
            set_shift(True)

            def step(tile, _):
                add(tile, False, False)
                return 0

            lax.fori_loop(1, diag, step, 0)

        for s in range(subs):
            cols = slice(s * LANES, (s + 1) * LANES)
            result = dq[c, :, cols] * 0.125
            stacked = jnp.concatenate([result[:, :HALF], result[:, HALF:]], axis=0)
            dquery_ref[c * HALF : (c + 1) * HALF, s * 2 * DH : (s + 1) * 2 * DH] = stacked.astype(jnp.bfloat16).T

    core = lax.rem(place, 2)

    def give(pair, _):
        for ref, owner in ((mine_ref, 2 * pair + core), (theirs_ref, 2 * pair + 1 - core)):
            for c, pos in enumerate(positions(owner)):
                rows = pl.ds(pl.multiple_of(pos, HALF), HALF)
                ref[pair, c * HALF : (c + 1) * HALF, :] = dkv[rows, :].astype(jnp.bfloat16)
        return 0

    lax.fori_loop(0, mine_ref.shape[0], give, 0)


VM = pl.BlockSpec(memory_space=pltpu.VMEM)
SM = pl.BlockSpec(memory_space=pltpu.SMEM)


def attend(place, query8, own, peer, starts):
    rows, width = query8.shape
    window = 2 * own.shape[0] * own.shape[1]
    lanes = (width // DH) * HALF
    return pl.pallas_call(
        forward_kernel,
        out_shape=(
            jax.ShapeDtypeStruct((rows, width), jnp.bfloat16),
            jax.ShapeDtypeStruct((2, DH, lanes), jnp.float32),
            jax.ShapeDtypeStruct((2, 1, lanes), jnp.float32),
        ),
        in_specs=[SM] + [VM] * 4,
        out_specs=(VM, VM, VM),
        scratch_shapes=[
            pltpu.VMEM((window, HALF), jnp.bfloat16),
            pltpu.VMEM((DH + 16, window), jnp.bfloat16),
            pltpu.VMEM((2, HALF, lanes), jnp.bfloat16),
            pltpu.VMEM((2, DH + 16, lanes), jnp.float32),
            pltpu.VMEM((2, 8, lanes), jnp.float32),
        ],
        compiler_params=pltpu.CompilerParams(vmem_limit_bytes=40 * 2**20),
        name="attend",
    )(place, query8, own, peer, starts)


def attend_back(place, query8, own, peer, starts, grad, out, logs):
    rows, width = query8.shape
    window = 2 * own.shape[0] * own.shape[1]
    lanes = (width // DH) * HALF
    subs = lanes // LANES
    return pl.pallas_call(
        backward_kernel,
        out_shape=(
            jax.ShapeDtypeStruct((rows, width), jnp.bfloat16),
            jax.ShapeDtypeStruct((window // (4 * HALF), 2 * HALF, 2 * DH), jnp.bfloat16),
            jax.ShapeDtypeStruct((window // (4 * HALF), 2 * HALF, 2 * DH), jnp.bfloat16),
        ),
        in_specs=[SM] + [VM] * 7,
        out_specs=(VM, VM, VM),
        scratch_shapes=[
            pltpu.VMEM((window, HALF), jnp.bfloat16),
            pltpu.VMEM((window, HALF), jnp.bfloat16),
            pltpu.VMEM((DH, window), jnp.bfloat16),
            pltpu.VMEM((2, HALF, lanes), jnp.bfloat16),
            pltpu.VMEM((2, HALF, lanes), jnp.bfloat16),
            pltpu.VMEM((2, subs, LANES, HALF), jnp.bfloat16),
            pltpu.VMEM((2, subs, LANES, HALF), jnp.bfloat16),
            pltpu.VMEM((2, DH, lanes), jnp.float32),
            pltpu.VMEM((window, HALF), jnp.float32),
        ],
        compiler_params=pltpu.CompilerParams(vmem_limit_bytes=48 * 2**20),
        name="attend_back",
    )(place, query8, own, peer, starts, grad, out, logs)


EPS = 1e-05
SWAP = ((0, 1), (1, 0))


def layer_norm(values, gain, shift):
    center = values - jnp.mean(values, axis=-1, keepdims=True)
    spread = jnp.mean(center * center, axis=-1, keepdims=True)
    return center * lax.rsqrt(spread + EPS) * gain + shift


def gelu_tanh(values):
    return jax.nn.gelu(values, approximate=True)


def dot_cols(left, right):
    return lax.dot_general(left, right, (((1,), (1,)), ((), ())), preferred_element_type=jnp.float32)


def dot_rows(left, right):
    return lax.dot_general(left, right, (((0,), (0,)), ((), ())), preferred_element_type=jnp.float32)


def low(value):
    return value.astype(jnp.bfloat16)


def swapped(value):
    return lax.ppermute(value, "heads", SWAP)


def opposite(value):
    count = lax.axis_size(("seq", "heads"))
    return lax.ppermute(value, ("seq", "heads"), [(i, count - 1 - i) for i in range(count)])


def exchanged(value):
    half = value.shape[0] // 2
    return jnp.concatenate([value[:half], opposite(value[half:])], axis=0)


def spread_out(blocks, axis):
    return lax.all_to_all(blocks, axis, split_axis=0, concat_axis=0, tiled=True)


def copies(value, axis):
    return spread_out(jnp.broadcast_to(value[None], (lax.axis_size(axis), *value.shape)), axis)


def two_parts(vector):
    high = low(vector)
    return high, low(vector - high.astype(jnp.float32))


def packed_vector(vector, ranks, width):
    share = -(-vector.shape[0] // ranks)
    high, rest = two_parts(jnp.pad(vector, (0, ranks * share - vector.shape[0])))
    row = jnp.concatenate([high.reshape(ranks, share), rest.reshape(ranks, share)], axis=1)
    return jnp.pad(row, ((0, 0), (0, width - 2 * share)))[:, None, :]


def total_of(weights, vector):
    axis = ("win", "seq")
    ranks, rows, width = weights.shape
    share = -(-vector.shape[0] // ranks)
    sent = jnp.concatenate([weights, packed_vector(vector, ranks, width)], axis=1)
    mine = jnp.sum(spread_out(sent, axis).astype(jnp.float32), axis=0)
    piece = mine[rows, :share] + mine[rows, share : 2 * share]
    high, rest = two_parts(piece)
    last = jnp.pad(jnp.concatenate([high, rest]), (0, width - 2 * share))
    full = copies(jnp.concatenate([low(mine[:rows]), last[None]], axis=0), axis)
    both = full[:, rows, : 2 * share].astype(jnp.float32)
    total = (both[:, :share] + both[:, share:]).reshape(-1)[: vector.shape[0]]
    return full[:, :rows].astype(jnp.float32), total


def per_device(
    tokens,
    first_gain,
    first_shift,
    query_weight,
    query_bias,
    keyval_weight,
    value_bias,
    out_weight,
    out_bias,
    second_gain,
    second_shift,
    expand_weight,
    expand_bias,
    contract_weight,
    contract_bias,
    cotangent,
    lengths,
):
    f32 = jnp.float32
    place = lax.axis_index(("seq", "heads"))
    places = place.astype(jnp.int32).reshape(1)
    ranks = lax.axis_size(("win", "seq"))

    own = layer_norm(tokens[0].astype(f32), first_gain, first_shift)
    keyval_shift = jnp.concatenate([jnp.zeros((DH,), f32), value_bias])
    own_keyval = low(jnp.dot(low(own), keyval_weight, preferred_element_type=f32) + keyval_shift)
    own_blocks = copies(own_keyval, "seq")
    peer_blocks = swapped(own_blocks)

    resid = exchanged(tokens[0]).astype(f32)
    grad_low = exchanged(cotangent[0])
    query_pair = (query_weight, swapped(query_weight))
    out_pair = (out_weight, swapped(out_weight))
    expand_pair = (expand_weight, swapped(expand_weight))
    contract_pair = (contract_weight, swapped(contract_weight))
    biases = swapped(jnp.concatenate([query_bias, expand_bias]))
    query_biases = (query_bias, biases[: query_bias.shape[0]])
    expand_biases = (expand_bias, biases[query_bias.shape[0] :])

    bounds = jnp.cumsum(lengths[0])
    first = jnp.stack(positions(place.astype(jnp.int32)))
    position = first[:, None] + jnp.arange(HALF, dtype=jnp.int32)[None, :]
    starts = jnp.max(jnp.where(bounds[None, None, :] <= position[:, :, None], bounds, 0), axis=2)
    starts = starts.astype(jnp.int32).reshape(2, 1, HALF)

    normed, first_pull = jax.vjp(layer_norm, resid, first_gain, first_shift)
    normed_low = low(normed)
    query = [
        low(jnp.dot(normed_low, w, preferred_element_type=f32) + b)
        for w, b in zip(query_pair, query_biases)
    ]
    query8 = jnp.concatenate(query, axis=1) * jnp.bfloat16(0.125)
    attended, out, logs = attend(places, query8, own_blocks, peer_blocks, starts)
    width = query_bias.shape[0]
    attended_pair = (attended[:, :width], attended[:, width:])
    rows = sum(jnp.dot(a, w, preferred_element_type=f32) for a, w in zip(attended_pair, out_pair))
    middle = resid + rows + out_bias
    normed2, second_pull = jax.vjp(layer_norm, middle, second_gain, second_shift)
    normed2_low = low(normed2)
    acts, pulls = [], []
    for w, b in zip(expand_pair, expand_biases):
        inner = jnp.dot(normed2_low, w, preferred_element_type=f32) + b
        act, pull = jax.vjp(gelu_tanh, inner)
        acts.append(low(act))
        pulls.append(pull)
    mlp = sum(jnp.dot(a, w, preferred_element_type=f32) for a, w in zip(acts, contract_pair))
    block_out = exchanged(low(middle + mlp + contract_bias))[None]

    grad_out = grad_low.astype(f32)
    contract_bias_part = jnp.sum(grad_out, axis=0)
    inner_grads = [low(pull(dot_cols(grad_low, w))[0]) for pull, w in zip(pulls, contract_pair)]
    expand_bias_parts = [jnp.sum(g.astype(f32), axis=0) for g in inner_grads]
    normed2_grad = sum(dot_cols(g, w) for g, w in zip(inner_grads, expand_pair))
    middle_from_norm, second_gain_part, second_shift_part = second_pull(normed2_grad)
    middle_grad = grad_out + middle_from_norm
    out_bias_part = jnp.sum(middle_grad, axis=0)
    middle_low = low(middle_grad)
    attended_grad = jnp.concatenate([low(dot_cols(middle_low, w)) for w in out_pair], axis=1)

    def tiles(matrix):
        return matrix.reshape(-1, 48, matrix.shape[1])

    def contract_part(side):
        return jnp.concatenate([tiles(dot_rows(acts[side], grad_low[:, i : i + 384])) for i in (0, 384)])

    def expand_part(side):
        return jnp.concatenate(
            [tiles(dot_rows(normed2_low, inner_grads[side][:, i : i + 384])) for i in range(0, 1536, 384)]
        )

    def out_part(side):
        return jnp.concatenate(
            [dot_rows(attended_pair[side], middle_low[:, i : i + 384]).reshape(-1, 12, 384) for i in (0, 384)]
        )

    def early_part(side):
        return contract_part(side), expand_part(side), out_part(side)

    vectors = jnp.concatenate([contract_bias_part, out_bias_part, second_gain_part, second_shift_part])
    early_vector = jnp.concatenate([vectors, expand_bias_parts[0]]) + swapped(
        jnp.concatenate([vectors, expand_bias_parts[1]])
    )
    early_weights = jnp.concatenate(
        [low(a + swapped(low(b)).astype(f32)) for a, b in zip(early_part(0), early_part(1))], axis=1
    )
    early_full, early_total = total_of(early_weights, early_vector)

    query_grad, mine, theirs = attend_back(
        places, query8, own_blocks, peer_blocks, starts, attended_grad, out, logs
    )
    pair_grad = low(mine.astype(f32) + swapped(theirs).astype(f32))
    keyval_grad = low(jnp.sum(spread_out(pair_grad, "seq").astype(f32), axis=0))
    query_grads = (query_grad[:, :width], query_grad[:, width:])
    query_bias_parts = [jnp.sum(g.astype(f32), axis=0) for g in query_grads]
    normed_grad = sum(dot_cols(g, w) for g, w in zip(query_grads, query_pair))
    normed_grad = normed_grad + dot_cols(keyval_grad, keyval_weight)
    value_bias_part = jnp.sum(keyval_grad[:, DH:].astype(f32), axis=0)
    resid_from_norm, first_gain_part, first_shift_part = first_pull(normed_grad)
    tokens_grad = middle_grad + resid_from_norm
    half = tokens_grad.shape[0] // 2
    tokens_grad = jnp.concatenate(
        [tokens_grad[:half], opposite(low(tokens_grad[half:])).astype(f32)], axis=0
    )[None]
    keyval_part = dot_rows(normed_low, keyval_grad)
    query_parts = [dot_rows(normed_low, g) for g in query_grads]
    vectors = jnp.concatenate([first_gain_part, first_shift_part, value_bias_part])
    late_vector = jnp.concatenate([vectors, query_bias_parts[0]]) + swapped(
        jnp.concatenate([vectors, query_bias_parts[1]])
    )
    late = jnp.concatenate([query_parts[0], keyval_part], axis=1) + swapped(
        low(jnp.concatenate([query_parts[1], keyval_part], axis=1))
    ).astype(f32)
    late_full, late_total = total_of(low(late).reshape(ranks, -1, late.shape[1]), late_vector)
    late_full = late_full.reshape(late.shape)

    def whole(blocks, groups, rows):
        blocks = blocks.reshape(groups, -1, rows, 384)
        return jnp.concatenate([blocks[i].reshape(-1, 384) for i in range(groups)], axis=1)

    features = first_gain.shape[0]
    return (
        block_out,
        tokens_grad,
        late_total[:features],
        late_total[features : 2 * features],
        late_full[:, :width],
        late_total[2 * features + DH :],
        late_full[:, width:],
        late_total[2 * features : 2 * features + DH],
        whole(early_full[:, 96:108], 2, 12),
        early_total[features : 2 * features],
        early_total[2 * features : 3 * features],
        early_total[3 * features : 4 * features],
        whole(early_full[:, 48:96], 4, 48),
        early_total[4 * features :],
        whole(early_full[:, :48], 2, 48),
        early_total[:features],
    )


def solution(mesh):
    return jax.shard_map(
        per_device,
        mesh=mesh,
        in_specs=(
            P("win", ("seq", "heads"), None),
            P(),
            P(),
            P(None, "heads"),
            P("heads"),
            P(),
            P(),
            P("heads", None),
            P(),
            P(),
            P(),
            P(None, "heads"),
            P("heads"),
            P("heads", None),
            P(),
            P("win", ("seq", "heads"), None),
            P("win", None),
        ),
        out_specs=(
            P("win", ("seq", "heads"), None),
            P("win", ("seq", "heads"), None),
            P(),
            P(),
            P(None, "heads"),
            P("heads"),
            P(),
            P(),
            P("heads", None),
            P(),
            P(),
            P(),
            P(None, "heads"),
            P("heads"),
            P("heads", None),
            P(),
        ),
        check_vma=False,
    )
```

```python
import math
import jax
import jax.numpy as jnp
from jax import lax
from jax.experimental import pallas as pl
from jax.experimental.pallas import tpu as pltpu
from jax.sharding import PartitionSpec as P

DH = 64
NEG = -1e30
TILE = 256
LANES = 256
HALF = 128


def mm(left, right):
    return lax.dot_general(left, right, (((1,), (0,)), ((), ())), preferred_element_type=jnp.float32)


def pieces(row, width):
    high = row.astype(jnp.bfloat16).astype(jnp.float32)
    rest = row - high
    mid = rest.astype(jnp.bfloat16).astype(jnp.float32)
    low = rest - mid
    which = lax.broadcasted_iota(jnp.int32, (16, width), 0)
    block = jnp.where(which == 0, -high, jnp.where(which == 1, -mid, jnp.where(which == 2, -low, 0.0)))
    return block.astype(jnp.bfloat16)


def with_ones(part):
    lane = lax.broadcasted_iota(jnp.int32, (part.shape[0], HALF), 1)
    wide = jnp.concatenate([part, jnp.zeros_like(part)], axis=1)
    return jnp.where((lane >= DH) & (lane < DH + 3), jnp.ones_like(wide), wide)


def mask_of(tile, chunk_pos, starts):
    key = tile * TILE + lax.broadcasted_iota(jnp.int32, (TILE, HALF), 0)
    query = chunk_pos + lax.broadcasted_iota(jnp.int32, (TILE, HALF), 1)
    mask = jnp.where((key <= query) & (key >= starts), 0.0, NEG)
    return jnp.concatenate([mask, mask], axis=1)


def in_pairs(first, last, step):
    count = jnp.maximum(last - first, 0)

    def two(i, _):
        step(first + 2 * i, 2)
        return 0

    lax.fori_loop(0, lax.div(count, 2), two, 0)

    @pl.when(lax.rem(count, 2) == 1)
    def _():
        step(last - 1, 1)


def block_of(own_ref, peer_ref, place, tile):
    pair = lax.div(tile, 2)
    own = lax.rem(tile, 2) == lax.rem(place, 2)
    return jnp.where(own, own_ref[pair], peer_ref[pair])


def positions(place):
    return (place * 2 * HALF, 63 * HALF - place * 2 * HALF)


def forward_kernel(place_ref, query_ref, own_ref, peer_ref, starts_ref, attended_ref, out_ref, log_ref, kx, vt, qt, acc, high):
    subs = qt.shape[2] // LANES
    chunk_pos = positions(place_ref[0])

    def prepare(tile, _):
        rows = pl.ds(pl.multiple_of(tile * TILE, TILE), TILE)
        block = block_of(own_ref, peer_ref, place_ref[0], tile)
        kx[rows, :] = with_ones(block[:, :DH])
        vt[:DH, rows] = block[:, DH:].T
        return 0

    lax.fori_loop(0, 2 * own_ref.shape[0], prepare, 0, unroll=4)
    vt[DH:, :] = jnp.ones_like(vt[DH:, :])

    for c in range(2):
        diag = chunk_pos[c] // TILE
        starts = starts_ref[c]
        wide = jnp.concatenate([starts, starts], axis=1)
        spans = [slice(s * LANES, (s + 1) * LANES) for s in range(subs)]
        for s, cols in enumerate(spans):
            pair = query_ref[c * HALF : (c + 1) * HALF, s * 2 * DH : (s + 1) * 2 * DH].T
            qt[c, :DH, cols] = jnp.concatenate([pair[:DH], pair[DH:]], axis=1)
            qt[c, DH:, cols] = jnp.zeros_like(qt[c, DH:, cols])

        def rows_of(tile, count=1):
            return pl.ds(pl.multiple_of(tile * TILE, TILE), count * TILE)

        def scores(tile, count=1):
            return [mm(kx[rows_of(tile, count), :], qt[c, :, cols]) for cols in spans]

        def gather(tile, probs, fresh=False, count=1):
            rows = rows_of(tile, count)
            for cols, prob in zip(spans, probs):
                part = mm(vt[:, rows], prob)
                if fresh:
                    acc[c, :, cols] = part
                else:
                    acc[c, :, cols] += part

        def exps(values):
            return [jnp.exp(v).astype(jnp.bfloat16) for v in values]

        def set_shift(used):
            for cols in spans:
                if used:
                    block = pieces(jnp.where(wide <= TILE, high[c, :1, cols], -NEG), LANES)
                else:
                    block = jnp.zeros((16, LANES), jnp.bfloat16)
                qt[c, DH : DH + 16, cols] = block

        def sweep(again):
            mask = mask_of(diag, chunk_pos[c], starts)
            values = [v + mask for v in scores(diag)]
            if again:
                tops = [high[c, :1, cols] for cols in spans]
            else:
                tops = [jnp.max(v, axis=0, keepdims=True) for v in values]
                for cols, top in zip(spans, tops):
                    high[c, :1, cols] = top
            gather(diag, exps([v - top for v, top in zip(values, tops)]), fresh=True)

            @pl.when(diag > 0)
            def _():
                set_shift(True)
                mask = mask_of(0, chunk_pos[c], starts)
                gather(0, exps([v + mask for v in scores(0)]))
                in_pairs(1, diag, lambda tile, count: gather(tile, exps(scores(tile, count)), count=count))

        sweep(False)

        @pl.when(jnp.logical_not(jnp.max(acc[c, DH : DH + 1, :]) < 1e30))
        def _():
            set_shift(False)

            def raise_to(values):
                for cols, v in zip(spans, values):
                    high[c, :1, cols] = jnp.maximum(high[c, :1, cols], jnp.max(v, axis=0, keepdims=True))

            @pl.when(diag > 0)
            def _():
                mask = mask_of(0, chunk_pos[c], starts)
                raise_to([v + mask for v in scores(0)])

                def step(tile, _):
                    raise_to([jnp.where(wide <= TILE, v, NEG) for v in scores(tile)])
                    return 0

                lax.fori_loop(1, diag, step, 0)

            sweep(True)

        for s, cols in enumerate(spans):
            total = acc[c, DH : DH + 1, cols]
            result = acc[c, :DH, cols] / total
            out_ref[c, :, cols] = result
            log_ref[c, :, cols] = high[c, :1, cols] + jnp.log(total)
            stacked = jnp.concatenate([result[:, :HALF], result[:, HALF:]], axis=0)
            attended_ref[c * HALF : (c + 1) * HALF, s * 2 * DH : (s + 1) * 2 * DH] = stacked.astype(jnp.bfloat16).T


def backward_kernel(
    place_ref, query_ref, own_ref, peer_ref, starts_ref, grad_ref, out_ref, log_ref,
    dquery_ref, mine_ref, theirs_ref, kx, vx, kt, qt, gt, wq, wg, dq, dkv,
):
    subs = qt.shape[2] // LANES
    place = place_ref[0]
    chunk_pos = positions(place)

    def prepare(tile, _):
        rows = pl.ds(pl.multiple_of(tile * TILE, TILE), TILE)
        block = block_of(own_ref, peer_ref, place, tile)
        kx[rows, :] = with_ones(block[:, :DH])
        vx[rows, :] = with_ones(block[:, DH:])
        kt[:, rows] = block[:, :DH].T
        return 0

    lax.fori_loop(0, 2 * own_ref.shape[0], prepare, 0, unroll=4)
    dkv[...] = jnp.zeros_like(dkv)

    for c in range(2):
        diag = chunk_pos[c] // TILE
        starts = jnp.concatenate([starts_ref[c], starts_ref[c]], axis=1)
        empty = jnp.zeros((HALF, DH), jnp.bfloat16)
        for s in range(subs):
            cols = slice(s * LANES, (s + 1) * LANES)
            q2 = query_ref[c * HALF : (c + 1) * HALF, s * 2 * DH : (s + 1) * 2 * DH]
            g2 = grad_ref[c * HALF : (c + 1) * HALF, s * 2 * DH : (s + 1) * 2 * DH]
            q2t, g2t = q2.T, g2.T
            qt[c, :DH, cols] = jnp.concatenate([q2t[:DH], q2t[DH:]], axis=1)
            grad_t = jnp.concatenate([g2t[:DH], g2t[DH:]], axis=1)
            gt[c, :DH, cols] = grad_t
            qt[c, DH:, cols] = jnp.zeros_like(qt[c, DH:, cols])
            gt[c, DH + 16 :, cols] = jnp.zeros_like(gt[c, DH + 16 :, cols])
            delta = jnp.sum(grad_t.astype(jnp.float32) * out_ref[c, :, cols], axis=0, keepdims=True)
            gt[c, DH : DH + 16, cols] = pieces(delta, LANES)
            for h in range(2):
                rows = slice(h * HALF, (h + 1) * HALF)
                wq[c, s, rows, :] = jnp.concatenate([q2[:, h * DH : (h + 1) * DH], empty], axis=1)
                wg[c, s, rows, :] = jnp.concatenate([empty, g2[:, h * DH : (h + 1) * DH]], axis=1)

        def add(tile, mask=None, logs=None, fresh=False, count=1):
            rows = pl.ds(pl.multiple_of(tile * TILE, TILE), count * TILE)
            total = jnp.zeros((count * TILE, 2 * DH), jnp.float32)
            for base in range(0, subs, 3):
                group = range(base, base + 3)
                spans = [slice(s * LANES, (s + 1) * LANES) for s in group]
                sts = [mm(kx[rows, :], qt[c, :, cols]) for cols in spans]
                dps = [mm(vx[rows, :], gt[c, :, cols]) for cols in spans]
                if mask is not None:
                    sts = [st + mask for st in sts]
                if logs is not None:
                    sts = [st - log_ref[c, :, cols] for st, cols in zip(sts, spans)]
                probs = [jnp.exp(st) for st in sts]
                dss = [(p * dp).astype(jnp.bfloat16) for p, dp in zip(probs, dps)]
                lows = [p.astype(jnp.bfloat16) for p in probs]
                for s, ds, low in zip(group, dss, lows):
                    total = total + (mm(ds, wq[c, s]) + mm(low, wg[c, s]))
                for cols, ds in zip(spans, dss):
                    part = mm(kt[:, rows], ds)
                    if fresh:
                        dq[c, :, cols] = part
                    else:
                        dq[c, :, cols] += part
            dkv[rows, :] += total

        add(diag, mask_of(diag, chunk_pos[c], starts_ref[c]), log_ref, fresh=True)

        @pl.when(diag > 0)
        def _():
            for s in range(subs):
                cols = slice(s * LANES, (s + 1) * LANES)
                qt[c, DH : DH + 16, cols] = pieces(jnp.where(starts <= TILE, log_ref[c, :, cols], -NEG), LANES)
            add(0, mask_of(0, chunk_pos[c], starts_ref[c]))

            in_pairs(1, diag, lambda tile, count: add(tile, count=count))

        for s in range(subs):
            cols = slice(s * LANES, (s + 1) * LANES)
            result = dq[c, :, cols] * 0.125
            stacked = jnp.concatenate([result[:, :HALF], result[:, HALF:]], axis=0)
            dquery_ref[c * HALF : (c + 1) * HALF, s * 2 * DH : (s + 1) * 2 * DH] = stacked.astype(jnp.bfloat16).T

    core = lax.rem(place, 2)

    def give(pair, _):
        for ref, owner in ((mine_ref, 2 * pair + core), (theirs_ref, 2 * pair + 1 - core)):
            for c, pos in enumerate(positions(owner)):
                rows = pl.ds(pl.multiple_of(pos, HALF), HALF)
                ref[pair, c * HALF : (c + 1) * HALF, :] = dkv[rows, :].astype(jnp.bfloat16)
        return 0

    lax.fori_loop(0, mine_ref.shape[0], give, 0)


VM = pl.BlockSpec(memory_space=pltpu.VMEM)
SM = pl.BlockSpec(memory_space=pltpu.SMEM)


def attend(place, query8, own, peer, starts):
    rows, width = query8.shape
    window = 2 * own.shape[0] * own.shape[1]
    lanes = (width // DH) * HALF
    return pl.pallas_call(
        forward_kernel,
        out_shape=(
            jax.ShapeDtypeStruct((rows, width), jnp.bfloat16),
            jax.ShapeDtypeStruct((2, DH, lanes), jnp.float32),
            jax.ShapeDtypeStruct((2, 1, lanes), jnp.float32),
        ),
        in_specs=[SM] + [VM] * 4,
        out_specs=(VM, VM, VM),
        scratch_shapes=[
            pltpu.VMEM((window, HALF), jnp.bfloat16),
            pltpu.VMEM((DH + 16, window), jnp.bfloat16),
            pltpu.VMEM((2, HALF, lanes), jnp.bfloat16),
            pltpu.VMEM((2, DH + 16, lanes), jnp.float32),
            pltpu.VMEM((2, 8, lanes), jnp.float32),
        ],
        compiler_params=pltpu.CompilerParams(vmem_limit_bytes=40 * 2**20),
        cost_estimate=pl.CostEstimate(flops=25 * 10**9, bytes_accessed=8 * 2**20, transcendentals=13 * 10**6),
        name="attend",
    )(place, query8, own, peer, starts)


def attend_back(place, query8, own, peer, starts, grad, out, logs):
    rows, width = query8.shape
    window = 2 * own.shape[0] * own.shape[1]
    lanes = (width // DH) * HALF
    subs = lanes // LANES
    return pl.pallas_call(
        backward_kernel,
        out_shape=(
            jax.ShapeDtypeStruct((rows, width), jnp.bfloat16),
            jax.ShapeDtypeStruct((window // (4 * HALF), 2 * HALF, 2 * DH), jnp.bfloat16),
            jax.ShapeDtypeStruct((window // (4 * HALF), 2 * HALF, 2 * DH), jnp.bfloat16),
        ),
        in_specs=[SM] + [VM] * 7,
        out_specs=(VM, VM, VM),
        scratch_shapes=[
            pltpu.VMEM((window, HALF), jnp.bfloat16),
            pltpu.VMEM((window, HALF), jnp.bfloat16),
            pltpu.VMEM((DH, window), jnp.bfloat16),
            pltpu.VMEM((2, HALF, lanes), jnp.bfloat16),
            pltpu.VMEM((2, HALF, lanes), jnp.bfloat16),
            pltpu.VMEM((2, subs, LANES, HALF), jnp.bfloat16),
            pltpu.VMEM((2, subs, LANES, HALF), jnp.bfloat16),
            pltpu.VMEM((2, DH, lanes), jnp.float32),
            pltpu.VMEM((window, HALF), jnp.float32),
        ],
        compiler_params=pltpu.CompilerParams(vmem_limit_bytes=48 * 2**20),
        cost_estimate=pl.CostEstimate(flops=45 * 10**9, bytes_accessed=12 * 2**20, transcendentals=13 * 10**6),
        name="attend_back",
    )(place, query8, own, peer, starts, grad, out, logs)


EPS = 1e-05
CUBE = 0.044715
VECTOR_ROWS = 64
ROOT = math.sqrt(2.0 / math.pi)


def mm_cols(left, right):
    return lax.dot_general(left, right, (((1,), (1,)), ((), ())), preferred_element_type=jnp.float32)


def statistics(values):
    center = values - jnp.mean(values, axis=-1, keepdims=True)
    spread = jnp.mean(center * center, axis=-1, keepdims=True)
    scale = lax.rsqrt(spread + EPS)
    return center * scale, scale


def residual_kernel(
    attended_ref, tokens_ref, mine_ref, theirs_ref, bias_ref, gain_ref, shift_ref, middle_ref, normed_ref
):
    width = mine_ref.shape[0]
    rows = mm(attended_ref[:, :width], mine_ref[...]) + mm(attended_ref[:, width:], theirs_ref[...])
    middle = tokens_ref[...].astype(jnp.float32) + rows + bias_ref[...]
    middle_ref[...] = middle
    normal, _ = statistics(middle)
    normed_ref[...] = (normal * gain_ref[...] + shift_ref[...]).astype(jnp.bfloat16)


def mlp_kernel(
    own_ref, peer_ref, own_grad_ref, peer_grad_ref, expand_ref, bias_ref, contract_ref,
    contract_part_ref, expand_part_ref, bias_part_ref, own_out_ref, peer_out_ref, own_back_ref, peer_back_ref,
    both, turned, grads, out, back,
):
    rows = own_ref.shape[0]
    hidden = expand_ref.shape[1]
    block = hidden // 4
    both[:rows, :] = own_ref[...]
    both[rows:, :] = peer_ref[...]
    grads[:rows, :] = own_grad_ref[...]
    grads[rows:, :] = peer_grad_ref[...]
    turned[...] = both[...].T
    for j in range(hidden // block):
        cols = slice(j * block, (j + 1) * block)
        inner = mm(both[...], expand_ref[:, cols]) + bias_ref[:, cols]
        square = inner * inner
        tanh = jnp.tanh(ROOT * inner * (1.0 + CUBE * square))
        half = 0.5 * (1.0 + tanh)
        acts = (inner * half).astype(jnp.bfloat16)
        slope = half + 0.5 * ROOT * inner * (1.0 - tanh * tanh) * (1.0 + 3.0 * CUBE * square)
        grad = (mm_cols(grads[...], contract_ref[cols, :]) * slope).astype(jnp.bfloat16)
        bias_part_ref[:, cols] = jnp.sum(grad.astype(jnp.float32), axis=0, keepdims=True)
        contract_part_ref[cols, :] = mm(acts.T, grads[...]).astype(jnp.bfloat16)
        expand_part_ref[:, cols] = mm(turned[...], grad).astype(jnp.bfloat16)
        out_part = mm(acts, contract_ref[cols, :])
        back_part = mm_cols(grad, expand_ref[:, cols])
        if j == 0:
            out[...] = out_part
            back[...] = back_part
        else:
            out[...] += out_part
            back[...] += back_part
    own_out_ref[...] = out[:rows, :]
    peer_out_ref[...] = out[rows:, :].astype(jnp.bfloat16)
    own_back_ref[...] = back[:rows, :]
    peer_back_ref[...] = back[rows:, :].astype(jnp.bfloat16)


def residual_back_kernel(
    back_ref, peer_back_ref, grad_ref, middle_ref, gain_ref, mine_ref, theirs_ref,
    middle_grad_ref, low_ref, attended_grad_ref, sums_ref,
):
    width = mine_ref.shape[0]
    back = back_ref[...] + peer_back_ref[...].astype(jnp.float32)
    grad = grad_ref[...].astype(jnp.float32)
    normal, scale = statistics(middle_ref[...])
    weighted = back * gain_ref[...]
    mean = jnp.mean(weighted, axis=-1, keepdims=True)
    along = jnp.mean(weighted * normal, axis=-1, keepdims=True)
    middle_grad = grad + scale * (weighted - mean - normal * along)
    middle_grad_ref[...] = middle_grad
    lowered = middle_grad.astype(jnp.bfloat16)
    low_ref[...] = lowered
    attended_grad_ref[:, :width] = mm_cols(lowered, mine_ref[...]).astype(jnp.bfloat16)
    attended_grad_ref[:, width:] = mm_cols(lowered, theirs_ref[...]).astype(jnp.bfloat16)
    sums_ref[0:1, :] = jnp.sum(middle_grad, axis=0, keepdims=True)
    sums_ref[1:2, :] = jnp.sum(back * normal, axis=0, keepdims=True)
    sums_ref[2:3, :] = jnp.sum(back, axis=0, keepdims=True)
    sums_ref[3:4, :] = jnp.sum(grad, axis=0, keepdims=True)


def query_back_kernel(
    grad_ref, normed_ref, attended_ref, low_ref, mine_ref, theirs_ref,
    normed_grad_ref, mine_part_ref, theirs_part_ref, mine_out_ref, theirs_out_ref, bias_ref,
):
    width = mine_ref.shape[1]
    normed = normed_ref[...].T
    attended = attended_ref[...].T
    mine, theirs = grad_ref[:, :width], grad_ref[:, width:]
    normed_grad_ref[...] = mm_cols(mine, mine_ref[...]) + mm_cols(theirs, theirs_ref[...])
    theirs_part_ref[...] = mm(normed, theirs).astype(jnp.bfloat16)
    theirs_out_ref[...] = mm(attended[width:], low_ref[...]).astype(jnp.bfloat16)
    mine_part_ref[...] = mm(normed, mine)
    mine_out_ref[...] = mm(attended[:width], low_ref[...])
    bias_ref[...] = jnp.sum(grad_ref[...].astype(jnp.float32), axis=0, keepdims=True)


def token_back_kernel(
    arrived_ref, normed_grad_ref, weight_ref, tokens_ref, gain_ref, normed_ref, middle_grad_ref,
    query_ref, peer_query_ref, out_ref, peer_out_ref, middle_sums_ref, query_bias_ref, expand_bias_ref,
    tokens_grad_ref, half_ref, sent_ref, rows_ref,
):
    grad = arrived_ref[0].astype(jnp.float32)
    for i in range(1, arrived_ref.shape[0]):
        grad = grad + arrived_ref[i].astype(jnp.float32)
    grad = grad.astype(jnp.bfloat16)
    back = normed_grad_ref[...] + mm_cols(grad, weight_ref[...])
    normal, scale = statistics(tokens_ref[...].astype(jnp.float32))
    weighted = back * gain_ref[...]
    mean = jnp.mean(weighted, axis=-1, keepdims=True)
    along = jnp.mean(weighted * normal, axis=-1, keepdims=True)
    tokens_grad = middle_grad_ref[...] + scale * (weighted - mean - normal * along)
    half = half_ref.shape[0]
    tokens_grad_ref[...] = tokens_grad[:half]
    half_ref[...] = tokens_grad[half:].astype(jnp.bfloat16)

    place = 0

    def put(values):
        nonlocal place
        depth = values.shape[0]
        sent_ref[place : place + depth, :] = values.astype(jnp.bfloat16)
        place += depth

    for ref, peer in ((query_ref, peer_query_ref), (out_ref, peer_out_ref)):
        for col in range(0, ref.shape[1], HALF):
            span = slice(col, col + HALF)
            put(ref[:, span] + peer[:, span].astype(jnp.float32))
    put(mm(normed_ref[...].T, grad))
    vectors = [middle_sums_ref[i : i + 1, :] for i in range(4)]
    vectors += [jnp.sum(back * normal, axis=0, keepdims=True), jnp.sum(back, axis=0, keepdims=True)]
    vectors += [query_bias_ref[...], jnp.sum(grad.astype(jnp.float32), axis=0, keepdims=True), expand_bias_ref[...]]
    rows_ref[...] = jnp.zeros_like(rows_ref)
    row = 0
    for vector in vectors:
        for col in range(0, vector.shape[1], HALF):
            rows_ref[row : row + 1, :] = vector[:, col : col + HALF]
            row += 1
    rows = rows_ref[...]
    high = rows.astype(jnp.bfloat16)
    put(high)
    put(rows - high.astype(jnp.float32))
    sent_ref[place:, :] = jnp.zeros_like(sent_ref[place:, :])


def unpack_kernel(full_ref, query_ref, out_ref, keyval_ref, rows_ref):
    place = 0
    for ref in (query_ref, out_ref, keyval_ref):
        depth = ref.shape[0]
        for col in range(0, ref.shape[1], HALF):
            ref[:, col : col + HALF] = full_ref[place : place + depth, :].astype(jnp.float32)
            place += depth
    depth = rows_ref.shape[0]
    high = full_ref[place : place + depth, :].astype(jnp.float32)
    rows_ref[...] = high + full_ref[place + depth : place + 2 * depth, :].astype(jnp.float32)


def like(*shape, dtype=jnp.float32):
    return jax.ShapeDtypeStruct(shape, dtype)


def run(kernel, outs, scratch, limit, flops, name, *args):
    return pl.pallas_call(
        kernel,
        out_shape=outs,
        in_specs=[VM] * len(args),
        out_specs=tuple(VM for _ in outs),
        scratch_shapes=scratch,
        compiler_params=pltpu.CompilerParams(vmem_limit_bytes=limit * 2**20),
        cost_estimate=pl.CostEstimate(flops=flops, bytes_accessed=2**20, transcendentals=0),
        name=name,
    )(*args)


def residual(attended, tokens, pair, bias, gain, shift):
    outs = (like(*tokens.shape), like(*tokens.shape, dtype=jnp.bfloat16))
    rows = (bias[None], gain[None], shift[None])
    return run(residual_kernel, outs, [], 24, 10**9, "residual", attended, tokens, *pair, *rows)


def mlp(own, peer, own_grad, peer_grad, expand, bias, contract):
    rows, features = own.shape
    hidden = expand.shape[1]
    b16 = jnp.bfloat16
    outs = (
        like(hidden, features, dtype=b16),
        like(features, hidden, dtype=b16),
        like(1, hidden),
        like(rows, features),
        like(rows, features, dtype=b16),
        like(rows, features),
        like(rows, features, dtype=b16),
    )
    scratch = [
        pltpu.VMEM((2 * rows, features), b16),
        pltpu.VMEM((features, 2 * rows), b16),
        pltpu.VMEM((2 * rows, features), b16),
        pltpu.VMEM((2 * rows, features), jnp.float32),
        pltpu.VMEM((2 * rows, features), jnp.float32),
    ]
    return run(
        mlp_kernel, outs, scratch, 48, 10**10, "mlp", own, peer, own_grad, peer_grad, expand, bias[None], contract
    )


def residual_back(back, peer_back, grad, middle, gain, pair):
    rows, features = grad.shape
    b16 = jnp.bfloat16
    outs = (like(rows, features), like(rows, features, dtype=b16), like(rows, features, dtype=b16), like(8, features))
    return run(
        residual_back_kernel, outs, [], 24, 10**9, "residual_back", back, peer_back, grad, middle, gain[None], *pair
    )


SWAP = ((0, 1), (1, 0))


def query_back(grad, normed, attended, lowered, pair):
    rows, features = grad.shape
    width = pair[0].shape[1]
    b16 = jnp.bfloat16
    outs = (
        like(rows, features),
        like(features, width),
        like(features, width, dtype=b16),
        like(width, features),
        like(width, features, dtype=b16),
        like(1, features),
    )
    return run(query_back_kernel, outs, [], 32, 10**10, "query_back", grad, normed, attended, lowered, *pair)


def token_back(ranks, arrived, normed_grad, weight, tokens, gain, normed, middle_grad, parts, vectors):
    rows, features = normed.shape
    depth = sum(p.size for p in (parts[0], parts[2], weight)) // HALF + 2 * VECTOR_ROWS
    depth += -depth % (8 * ranks)
    outs = (like(rows // 2, features), like(rows // 2, features, dtype=jnp.bfloat16), like(depth, HALF, dtype=jnp.bfloat16))
    return run(
        token_back_kernel, outs, [pltpu.VMEM((VECTOR_ROWS, HALF), jnp.float32)], 32, 10**9, "token_back",
        arrived, normed_grad, weight, tokens, gain[None], normed, middle_grad, *parts, *vectors,
    )


def unpack(full, query_shape, out_shape, keyval_shape):
    outs = (like(*query_shape), like(*out_shape), like(*keyval_shape), like(VECTOR_ROWS, HALF))
    return run(unpack_kernel, outs, [], 32, 10**8, "unpack", full)


def layer_norm(values, gain, shift):
    center = values - jnp.mean(values, axis=-1, keepdims=True)
    spread = jnp.mean(center * center, axis=-1, keepdims=True)
    return center * lax.rsqrt(spread + EPS) * gain + shift


def low(value):
    return value.astype(jnp.bfloat16)


def swapped(value):
    return lax.ppermute(value, "heads", SWAP)


def opposite(value):
    count = lax.axis_size(("seq", "heads"))
    return lax.ppermute(value, ("seq", "heads"), [(i, count - 1 - i) for i in range(count)])


def exchanged(value):
    half = value.shape[0] // 2
    return jnp.concatenate([value[:half], opposite(value[half:])], axis=0)


def spread_out(blocks, axis):
    return lax.all_to_all(blocks, axis, split_axis=0, concat_axis=0, tiled=True)


def copies(value, axis):
    return spread_out(jnp.broadcast_to(value[None], (lax.axis_size(axis), *value.shape)), axis)


def per_device(
    tokens,
    first_gain,
    first_shift,
    query_weight,
    query_bias,
    keyval_weight,
    value_bias,
    out_weight,
    out_bias,
    second_gain,
    second_shift,
    expand_weight,
    expand_bias,
    contract_weight,
    contract_bias,
    cotangent,
    lengths,
):
    f32 = jnp.float32
    place = lax.axis_index(("seq", "heads"))
    places = place.astype(jnp.int32).reshape(1)
    ranks = lax.axis_size(("win", "seq"))

    own = layer_norm(tokens[0].astype(f32), first_gain, first_shift)
    keyval_shift = jnp.concatenate([jnp.zeros((DH,), f32), value_bias])
    own_keyval = low(jnp.dot(low(own), keyval_weight, preferred_element_type=f32) + keyval_shift)

    tokens_half, own_keyval = lax.optimization_barrier((tokens[0], own_keyval))
    own_blocks = copies(own_keyval, "seq")
    peer_blocks = swapped(own_blocks)
    tokens_low = exchanged(tokens_half)
    resid = tokens_low.astype(f32)
    grad_low = exchanged(cotangent[0])
    query_pair = (query_weight, swapped(query_weight))
    out_pair = (out_weight, swapped(out_weight))
    query_biases = (query_bias, swapped(query_bias))
    peer_grad_low = swapped(grad_low)

    bounds = jnp.cumsum(lengths[0])
    first = jnp.stack(positions(place.astype(jnp.int32)))
    position = first[:, None] + jnp.arange(HALF, dtype=jnp.int32)[None, :]
    starts = jnp.max(jnp.where(bounds[None, None, :] <= position[:, :, None], bounds, 0), axis=2)
    starts = starts.astype(jnp.int32).reshape(2, 1, HALF)

    normed_low = low(layer_norm(resid, first_gain, first_shift))
    query = [
        low(jnp.dot(normed_low, w, preferred_element_type=f32) + b)
        for w, b in zip(query_pair, query_biases)
    ]
    query8 = jnp.concatenate(query, axis=1) * jnp.bfloat16(0.125)
    attended, out, logs = attend(places, query8, own_blocks, peer_blocks, starts)
    width = query_bias.shape[0]
    attended_pair = (attended[:, :width], attended[:, width:])
    middle, normed2_low = residual(attended, tokens_low, out_pair, out_bias, second_gain, second_shift)
    contract_part, expand_part, expand_bias_part, mlp_rows, mlp_peer, back_rows, back_peer = mlp(
        normed2_low, swapped(normed2_low), grad_low, peer_grad_low, expand_weight, expand_bias, contract_weight
    )
    contract_total, expand_total = lax.psum((contract_part, expand_part), ("win", "seq"))
    middle_grad, middle_low, attended_grad, middle_sums = residual_back(
        back_rows, swapped(back_peer), grad_low, middle, second_gain, out_pair
    )

    def rest():
        query_grad, mine, theirs = attend_back(
            places, query8, own_blocks, peer_blocks, starts, attended_grad, out, logs
        )
        mlp_out = mlp_rows + swapped(mlp_peer).astype(f32)
        block_out = exchanged(low(middle + mlp_out + contract_bias))
        pair_grad = low(mine.astype(f32) + swapped(theirs).astype(f32))
        arrived = spread_out(pair_grad, "seq")
        from_query, query_part, query_sent, out_part, out_sent, query_bias_part = query_back(
            query_grad, normed_low, attended, middle_low, query_pair
        )
        core = lax.axis_index("heads")
        turned_bias = jnp.concatenate([query_bias_part[:, width:], query_bias_part[:, :width]], axis=1)
        query_bias_part = jnp.where(core == 0, query_bias_part, turned_bias)
        tokens_grad, half, sent = token_back(
            ranks, arrived, from_query, keyval_weight, tokens_low, first_gain, normed_low, middle_grad,
            (query_part, swapped(query_sent), out_part, swapped(out_sent)),
            (middle_sums, query_bias_part, expand_bias_part),
        )
        tokens_grad = jnp.concatenate([tokens_grad, opposite(half).astype(f32)], axis=0)

        blocks = sent.reshape(ranks, -1, HALF)
        depth = blocks.shape[1]
        summed = jnp.sum(spread_out(blocks, ("win", "seq")).astype(f32), axis=0)
        row = lax.axis_index(("win", "seq")) * depth + jnp.arange(depth)[:, None]
        weights = query_weight.size + out_weight.size
        features = first_gain.shape[0]
        vectors = weights + keyval_weight.size
        alone = vectors + 7 * features + HALF
        shared = (row >= weights // HALF) & (row < alone // HALF)
        alone += VECTOR_ROWS * HALF
        shared = shared | ((row >= vectors // HALF + VECTOR_ROWS) & (row < alone // HALF))
        summed = summed + jnp.where(shared, swapped(summed), 0.0)
        full = copies(low(summed), ("win", "seq")).reshape(-1, HALF)
        query_total, out_total, keyval_total, rows = unpack(
            full, query_weight.shape, out_weight.shape, keyval_weight.shape
        )
        rows = rows.reshape(-1)
        sizes = [features] * 7 + [HALF, expand_bias.shape[0]]
        totals = []
        for size in sizes:
            totals.append(rows[:size])
            rows = rows[size:]
        query_bias_total = jnp.where(core == 0, totals[6][:width], totals[6][width:])
        return (
            block_out[None],
            tokens_grad[None],
            totals[4],
            totals[5],
            query_total,
            query_bias_total,
            keyval_total,
            totals[7][DH:],
            out_total,
            totals[0],
            totals[1],
            totals[2],
            totals[8],
            totals[3],
        )

    shapes = jax.eval_shape(rest)

    def nothing():
        return jax.tree.map(lambda s: jnp.zeros(s.shape, s.dtype), shapes)

    outs = lax.cond(lengths[0, 0] > 0, rest, nothing)
    return (
        *outs[:12],
        expand_total.astype(f32),
        outs[12],
        contract_total.astype(f32),
        outs[13],
    )


def solution(mesh):
    return jax.shard_map(
        per_device,
        mesh=mesh,
        in_specs=(
            P("win", ("seq", "heads"), None),
            P(),
            P(),
            P(None, "heads"),
            P("heads"),
            P(),
            P(),
            P("heads", None),
            P(),
            P(),
            P(),
            P(None, "heads"),
            P("heads"),
            P("heads", None),
            P(),
            P("win", ("seq", "heads"), None),
            P("win", None),
        ),
        out_specs=(
            P("win", ("seq", "heads"), None),
            P("win", ("seq", "heads"), None),
            P(),
            P(),
            P(None, "heads"),
            P("heads"),
            P(),
            P(),
            P("heads", None),
            P(),
            P(),
            P(),
            P(None, "heads"),
            P("heads"),
            P("heads", None),
            P(),
        ),
        check_vma=False,
    )
```

```python
import math
import jax
import jax.numpy as jnp
from jax import lax
from jax.experimental import pallas as pl
from jax.experimental.pallas import tpu as pltpu
from jax.sharding import PartitionSpec as P

DH = 64
NEG = -1e30
TILE = 256
LANES = 256
HALF = 128


def mm(left, right):
    return lax.dot_general(left, right, (((1,), (0,)), ((), ())), preferred_element_type=jnp.float32)


def pieces(row, width):
    high = row.astype(jnp.bfloat16).astype(jnp.float32)
    rest = row - high
    mid = rest.astype(jnp.bfloat16).astype(jnp.float32)
    low = rest - mid
    which = lax.broadcasted_iota(jnp.int32, (16, width), 0)
    block = jnp.where(which == 0, -high, jnp.where(which == 1, -mid, jnp.where(which == 2, -low, 0.0)))
    return block.astype(jnp.bfloat16)


def with_ones(part):
    lane = lax.broadcasted_iota(jnp.int32, (part.shape[0], HALF), 1)
    wide = jnp.concatenate([part, jnp.zeros_like(part)], axis=1)
    return jnp.where((lane >= DH) & (lane < DH + 3), jnp.ones_like(wide), wide)


def mask_of(tile, chunk_pos, starts):
    key = tile * TILE + lax.broadcasted_iota(jnp.int32, (TILE, HALF), 0)
    query = chunk_pos + lax.broadcasted_iota(jnp.int32, (TILE, HALF), 1)
    mask = jnp.where((key <= query) & (key >= starts), 0.0, NEG)
    return jnp.concatenate([mask, mask], axis=1)


def in_pairs(first, last, step):
    count = jnp.maximum(last - first, 0)

    def two(i, _):
        step(first + 2 * i, 2)
        return 0

    lax.fori_loop(0, lax.div(count, 2), two, 0)

    @pl.when(lax.rem(count, 2) == 1)
    def _():
        step(last - 1, 1)


def block_of(own_ref, peer_ref, place, tile):
    pair = lax.div(tile, 2)
    own = lax.rem(tile, 2) == lax.rem(place, 2)
    return jnp.where(own, own_ref[pair], peer_ref[pair])


def positions(place):
    return (place * 2 * HALF, 63 * HALF - place * 2 * HALF)


def forward_kernel(place_ref, query_ref, own_ref, peer_ref, starts_ref, attended_ref, out_ref, log_ref, kx, vt, qt, acc, high):
    subs = qt.shape[2] // LANES
    chunk_pos = positions(place_ref[0])

    def prepare(tile, _):
        rows = pl.ds(pl.multiple_of(tile * TILE, TILE), TILE)
        block = block_of(own_ref, peer_ref, place_ref[0], tile)
        kx[rows, :] = with_ones(block[:, :DH])
        vt[:DH, rows] = block[:, DH:].T
        return 0

    lax.fori_loop(0, 2 * own_ref.shape[0], prepare, 0, unroll=4)
    vt[DH:, :] = jnp.ones_like(vt[DH:, :])

    for c in range(2):
        diag = chunk_pos[c] // TILE
        starts = starts_ref[c]
        wide = jnp.concatenate([starts, starts], axis=1)
        spans = [slice(s * LANES, (s + 1) * LANES) for s in range(subs)]
        for s, cols in enumerate(spans):
            pair = query_ref[c * HALF : (c + 1) * HALF, s * 2 * DH : (s + 1) * 2 * DH].T
            qt[c, :DH, cols] = jnp.concatenate([pair[:DH], pair[DH:]], axis=1)
            qt[c, DH:, cols] = jnp.zeros_like(qt[c, DH:, cols])

        def rows_of(tile, count=1):
            return pl.ds(pl.multiple_of(tile * TILE, TILE), count * TILE)

        def scores(tile, count=1):
            return [mm(kx[rows_of(tile, count), :], qt[c, :, cols]) for cols in spans]

        def gather(tile, probs, fresh=False, count=1):
            rows = rows_of(tile, count)
            for cols, prob in zip(spans, probs):
                part = mm(vt[:, rows], prob)
                if fresh:
                    acc[c, :, cols] = part
                else:
                    acc[c, :, cols] += part

        def exps(values):
            return [jnp.exp(v).astype(jnp.bfloat16) for v in values]

        def set_shift(used):
            for cols in spans:
                if used:
                    block = pieces(jnp.where(wide <= TILE, high[c, :1, cols], -NEG), LANES)
                else:
                    block = jnp.zeros((16, LANES), jnp.bfloat16)
                qt[c, DH : DH + 16, cols] = block

        def sweep(again):
            mask = mask_of(diag, chunk_pos[c], starts)
            values = [v + mask for v in scores(diag)]
            if again:
                tops = [high[c, :1, cols] for cols in spans]
            else:
                tops = [jnp.max(v, axis=0, keepdims=True) for v in values]
                for cols, top in zip(spans, tops):
                    high[c, :1, cols] = top
            gather(diag, exps([v - top for v, top in zip(values, tops)]), fresh=True)

            @pl.when(diag > 0)
            def _():
                set_shift(True)
                mask = mask_of(0, chunk_pos[c], starts)
                gather(0, exps([v + mask for v in scores(0)]))
                in_pairs(1, diag, lambda tile, count: gather(tile, exps(scores(tile, count)), count=count))

        sweep(False)

        @pl.when(jnp.logical_not(jnp.max(acc[c, DH : DH + 1, :]) < 1e30))
        def _():
            set_shift(False)

            def raise_to(values):
                for cols, v in zip(spans, values):
                    high[c, :1, cols] = jnp.maximum(high[c, :1, cols], jnp.max(v, axis=0, keepdims=True))

            @pl.when(diag > 0)
            def _():
                mask = mask_of(0, chunk_pos[c], starts)
                raise_to([v + mask for v in scores(0)])

                def step(tile, _):
                    raise_to([jnp.where(wide <= TILE, v, NEG) for v in scores(tile)])
                    return 0

                lax.fori_loop(1, diag, step, 0)

            sweep(True)

        for s, cols in enumerate(spans):
            total = acc[c, DH : DH + 1, cols]
            result = acc[c, :DH, cols] / total
            out_ref[c, :, cols] = result
            log_ref[c, :, cols] = high[c, :1, cols] + jnp.log(total)
            stacked = jnp.concatenate([result[:, :HALF], result[:, HALF:]], axis=0)
            attended_ref[c * HALF : (c + 1) * HALF, s * 2 * DH : (s + 1) * 2 * DH] = stacked.astype(jnp.bfloat16).T


def backward_kernel(
    place_ref, query_ref, own_ref, peer_ref, starts_ref, grad_ref, out_ref, log_ref,
    dquery_ref, mine_ref, theirs_ref, kx, vx, kt, qt, gt, wq, wg, dq, dkv,
):
    subs = qt.shape[2] // LANES
    place = place_ref[0]
    chunk_pos = positions(place)

    def prepare(tile, _):
        rows = pl.ds(pl.multiple_of(tile * TILE, TILE), TILE)
        block = block_of(own_ref, peer_ref, place, tile)
        kx[rows, :] = with_ones(block[:, :DH])
        vx[rows, :] = with_ones(block[:, DH:])
        kt[:, rows] = block[:, :DH].T
        return 0

    lax.fori_loop(0, 2 * own_ref.shape[0], prepare, 0, unroll=4)
    dkv[...] = jnp.zeros_like(dkv)

    for c in range(2):
        diag = chunk_pos[c] // TILE
        starts = jnp.concatenate([starts_ref[c], starts_ref[c]], axis=1)
        empty = jnp.zeros((HALF, DH), jnp.bfloat16)
        for s in range(subs):
            cols = slice(s * LANES, (s + 1) * LANES)
            q2 = query_ref[c * HALF : (c + 1) * HALF, s * 2 * DH : (s + 1) * 2 * DH]
            g2 = grad_ref[c * HALF : (c + 1) * HALF, s * 2 * DH : (s + 1) * 2 * DH]
            q2t, g2t = q2.T, g2.T
            qt[c, :DH, cols] = jnp.concatenate([q2t[:DH], q2t[DH:]], axis=1)
            grad_t = jnp.concatenate([g2t[:DH], g2t[DH:]], axis=1)
            gt[c, :DH, cols] = grad_t
            qt[c, DH:, cols] = jnp.zeros_like(qt[c, DH:, cols])
            gt[c, DH + 16 :, cols] = jnp.zeros_like(gt[c, DH + 16 :, cols])
            delta = jnp.sum(grad_t.astype(jnp.float32) * out_ref[c, :, cols], axis=0, keepdims=True)
            gt[c, DH : DH + 16, cols] = pieces(delta, LANES)
            for h in range(2):
                rows = slice(h * HALF, (h + 1) * HALF)
                wq[c, s, rows, :] = jnp.concatenate([q2[:, h * DH : (h + 1) * DH], empty], axis=1)
                wg[c, s, rows, :] = jnp.concatenate([empty, g2[:, h * DH : (h + 1) * DH]], axis=1)

        def add(tile, mask=None, logs=None, fresh=False, count=1):
            rows = pl.ds(pl.multiple_of(tile * TILE, TILE), count * TILE)
            total = jnp.zeros((count * TILE, 2 * DH), jnp.float32)
            for base in range(0, subs, 3):
                group = range(base, base + 3)
                spans = [slice(s * LANES, (s + 1) * LANES) for s in group]
                sts = [mm(kx[rows, :], qt[c, :, cols]) for cols in spans]
                dps = [mm(vx[rows, :], gt[c, :, cols]) for cols in spans]
                if mask is not None:
                    sts = [st + mask for st in sts]
                if logs is not None:
                    sts = [st - log_ref[c, :, cols] for st, cols in zip(sts, spans)]
                probs = [jnp.exp(st) for st in sts]
                dss = [(p * dp).astype(jnp.bfloat16) for p, dp in zip(probs, dps)]
                lows = [p.astype(jnp.bfloat16) for p in probs]
                for s, ds, low in zip(group, dss, lows):
                    total = total + (mm(ds, wq[c, s]) + mm(low, wg[c, s]))
                for cols, ds in zip(spans, dss):
                    part = mm(kt[:, rows], ds)
                    if fresh:
                        dq[c, :, cols] = part
                    else:
                        dq[c, :, cols] += part
            dkv[rows, :] += total

        add(diag, mask_of(diag, chunk_pos[c], starts_ref[c]), log_ref, fresh=True)

        @pl.when(diag > 0)
        def _():
            for s in range(subs):
                cols = slice(s * LANES, (s + 1) * LANES)
                qt[c, DH : DH + 16, cols] = pieces(jnp.where(starts <= TILE, log_ref[c, :, cols], -NEG), LANES)
            add(0, mask_of(0, chunk_pos[c], starts_ref[c]))

            in_pairs(1, diag, lambda tile, count: add(tile, count=count))

        for s in range(subs):
            cols = slice(s * LANES, (s + 1) * LANES)
            result = dq[c, :, cols] * 0.125
            stacked = jnp.concatenate([result[:, :HALF], result[:, HALF:]], axis=0)
            dquery_ref[c * HALF : (c + 1) * HALF, s * 2 * DH : (s + 1) * 2 * DH] = stacked.astype(jnp.bfloat16).T

    core = lax.rem(place, 2)

    def give(pair, _):
        for ref, owner in ((mine_ref, 2 * pair + core), (theirs_ref, 2 * pair + 1 - core)):
            for c, pos in enumerate(positions(owner)):
                rows = pl.ds(pl.multiple_of(pos, HALF), HALF)
                ref[pair, c * HALF : (c + 1) * HALF, :] = dkv[rows, :].astype(jnp.bfloat16)
        return 0

    lax.fori_loop(0, mine_ref.shape[0], give, 0)


VM = pl.BlockSpec(memory_space=pltpu.VMEM)
SM = pl.BlockSpec(memory_space=pltpu.SMEM)


def attend(place, query8, own, peer, starts):
    rows, width = query8.shape
    window = 2 * own.shape[0] * own.shape[1]
    lanes = (width // DH) * HALF
    return pl.pallas_call(
        forward_kernel,
        out_shape=(
            jax.ShapeDtypeStruct((rows, width), jnp.bfloat16),
            jax.ShapeDtypeStruct((2, DH, lanes), jnp.float32),
            jax.ShapeDtypeStruct((2, 1, lanes), jnp.float32),
        ),
        in_specs=[SM] + [VM] * 4,
        out_specs=(VM, VM, VM),
        scratch_shapes=[
            pltpu.VMEM((window, HALF), jnp.bfloat16),
            pltpu.VMEM((DH + 16, window), jnp.bfloat16),
            pltpu.VMEM((2, HALF, lanes), jnp.bfloat16),
            pltpu.VMEM((2, DH + 16, lanes), jnp.float32),
            pltpu.VMEM((2, 8, lanes), jnp.float32),
        ],
        compiler_params=pltpu.CompilerParams(vmem_limit_bytes=40 * 2**20),
        cost_estimate=pl.CostEstimate(flops=25 * 10**9, bytes_accessed=8 * 2**20, transcendentals=13 * 10**6),
        name="attend",
    )(place, query8, own, peer, starts)


def attend_back(place, query8, own, peer, starts, grad, out, logs):
    rows, width = query8.shape
    window = 2 * own.shape[0] * own.shape[1]
    lanes = (width // DH) * HALF
    subs = lanes // LANES
    return pl.pallas_call(
        backward_kernel,
        out_shape=(
            jax.ShapeDtypeStruct((rows, width), jnp.bfloat16),
            jax.ShapeDtypeStruct((window // (4 * HALF), 2 * HALF, 2 * DH), jnp.bfloat16),
            jax.ShapeDtypeStruct((window // (4 * HALF), 2 * HALF, 2 * DH), jnp.bfloat16),
        ),
        in_specs=[SM] + [VM] * 7,
        out_specs=(VM, VM, VM),
        scratch_shapes=[
            pltpu.VMEM((window, HALF), jnp.bfloat16),
            pltpu.VMEM((window, HALF), jnp.bfloat16),
            pltpu.VMEM((DH, window), jnp.bfloat16),
            pltpu.VMEM((2, HALF, lanes), jnp.bfloat16),
            pltpu.VMEM((2, HALF, lanes), jnp.bfloat16),
            pltpu.VMEM((2, subs, LANES, HALF), jnp.bfloat16),
            pltpu.VMEM((2, subs, LANES, HALF), jnp.bfloat16),
            pltpu.VMEM((2, DH, lanes), jnp.float32),
            pltpu.VMEM((window, HALF), jnp.float32),
        ],
        compiler_params=pltpu.CompilerParams(vmem_limit_bytes=48 * 2**20),
        cost_estimate=pl.CostEstimate(flops=45 * 10**9, bytes_accessed=12 * 2**20, transcendentals=13 * 10**6),
        name="attend_back",
    )(place, query8, own, peer, starts, grad, out, logs)


EPS = 1e-05
CUBE = 0.044715
VECTOR_ROWS = 64
ROOT = math.sqrt(2.0 / math.pi)


def mm_cols(left, right):
    return lax.dot_general(left, right, (((1,), (1,)), ((), ())), preferred_element_type=jnp.float32)


def statistics(values):
    center = values - jnp.mean(values, axis=-1, keepdims=True)
    spread = jnp.mean(center * center, axis=-1, keepdims=True)
    scale = lax.rsqrt(spread + EPS)
    return center * scale, scale


def residual_kernel(
    attended_ref, tokens_ref, mine_ref, theirs_ref, bias_ref, gain_ref, shift_ref, middle_ref, normed_ref
):
    width = mine_ref.shape[0]
    rows = mm(attended_ref[:, :width], mine_ref[...]) + mm(attended_ref[:, width:], theirs_ref[...])
    middle = tokens_ref[...].astype(jnp.float32) + rows + bias_ref[...]
    middle_ref[...] = middle
    normal, _ = statistics(middle)
    normed_ref[...] = (normal * gain_ref[...] + shift_ref[...]).astype(jnp.bfloat16)


def own_kernel(tokens_ref, gain_ref, shift_ref, weight_ref, bias_ref, blocks_ref):
    normal, _ = statistics(tokens_ref[...].astype(jnp.float32))
    normed = (normal * gain_ref[...] + shift_ref[...]).astype(jnp.bfloat16)
    bias = jnp.concatenate([jnp.zeros_like(bias_ref[...]), bias_ref[...]], axis=1)
    keyval = (mm(normed, weight_ref[...]) + bias).astype(jnp.bfloat16)
    for i in range(blocks_ref.shape[0]):
        blocks_ref[i] = keyval


def query_kernel(
    own_ref, half_ref, gain_ref, shift_ref, mine_ref, theirs_ref, mine_bias_ref, theirs_bias_ref,
    tokens_ref, normed_ref, query_ref,
):
    half, width = half_ref.shape[0], mine_ref.shape[1]
    tokens_ref[:half, :] = own_ref[:half, :]
    tokens_ref[half:, :] = half_ref[...]
    normal, _ = statistics(tokens_ref[...].astype(jnp.float32))
    normed = (normal * gain_ref[...] + shift_ref[...]).astype(jnp.bfloat16)
    normed_ref[...] = normed
    mine = (mm(normed, mine_ref[...]) + mine_bias_ref[...]).astype(jnp.bfloat16)
    theirs = (mm(normed, theirs_ref[...]) + theirs_bias_ref[...]).astype(jnp.bfloat16)
    query_ref[:, :width] = mine * jnp.bfloat16(0.125)
    query_ref[:, width:] = theirs * jnp.bfloat16(0.125)


def mlp_kernel(
    own_ref, peer_ref, own_grad_ref, peer_grad_ref, expand_ref, bias_ref, contract_ref,
    contract_part_ref, expand_part_ref, bias_part_ref, own_out_ref, peer_out_ref, own_back_ref, peer_back_ref,
    both, turned, grads, out, back,
):
    rows = own_ref.shape[0]
    hidden = expand_ref.shape[1]
    block = hidden // 4
    both[:rows, :] = own_ref[...]
    both[rows:, :] = peer_ref[...]
    grads[:rows, :] = own_grad_ref[...]
    grads[rows:, :] = peer_grad_ref[...]
    turned[...] = both[...].T
    for j in range(hidden // block):
        cols = slice(j * block, (j + 1) * block)
        inner = mm(both[...], expand_ref[:, cols]) + bias_ref[:, cols]
        square = inner * inner
        tanh = jnp.tanh(ROOT * inner * (1.0 + CUBE * square))
        half = 0.5 * (1.0 + tanh)
        acts = (inner * half).astype(jnp.bfloat16)
        slope = half + 0.5 * ROOT * inner * (1.0 - tanh * tanh) * (1.0 + 3.0 * CUBE * square)
        grad = (mm_cols(grads[...], contract_ref[cols, :]) * slope).astype(jnp.bfloat16)
        bias_part_ref[:, cols] = jnp.sum(grad.astype(jnp.float32), axis=0, keepdims=True)
        contract_part_ref[cols, :] = mm(acts.T, grads[...]).astype(jnp.bfloat16)
        expand_part_ref[:, cols] = mm(turned[...], grad).astype(jnp.bfloat16)
        out_part = mm(acts, contract_ref[cols, :])
        back_part = mm_cols(grad, expand_ref[:, cols])
        if j == 0:
            out[...] = out_part
            back[...] = back_part
        else:
            out[...] += out_part
            back[...] += back_part
    own_out_ref[...] = out[:rows, :]
    peer_out_ref[...] = out[rows:, :].astype(jnp.bfloat16)
    own_back_ref[...] = back[:rows, :]
    peer_back_ref[...] = back[rows:, :].astype(jnp.bfloat16)


def widen_kernel(contract_ref, expand_ref, contract_out_ref, expand_out_ref):
    contract_out_ref[...] = contract_ref[...].astype(jnp.float32)
    expand_out_ref[...] = expand_ref[...].astype(jnp.float32)


def residual_back_kernel(
    back_ref, peer_back_ref, grad_ref, middle_ref, gain_ref, mine_ref, theirs_ref,
    middle_grad_ref, low_ref, attended_grad_ref, sums_ref,
):
    width = mine_ref.shape[0]
    back = back_ref[...] + peer_back_ref[...].astype(jnp.float32)
    grad = grad_ref[...].astype(jnp.float32)
    normal, scale = statistics(middle_ref[...])
    weighted = back * gain_ref[...]
    mean = jnp.mean(weighted, axis=-1, keepdims=True)
    along = jnp.mean(weighted * normal, axis=-1, keepdims=True)
    middle_grad = grad + scale * (weighted - mean - normal * along)
    middle_grad_ref[...] = middle_grad
    lowered = middle_grad.astype(jnp.bfloat16)
    low_ref[...] = lowered
    attended_grad_ref[:, :width] = mm_cols(lowered, mine_ref[...]).astype(jnp.bfloat16)
    attended_grad_ref[:, width:] = mm_cols(lowered, theirs_ref[...]).astype(jnp.bfloat16)
    sums_ref[0:1, :] = jnp.sum(middle_grad, axis=0, keepdims=True)
    sums_ref[1:2, :] = jnp.sum(back * normal, axis=0, keepdims=True)
    sums_ref[2:3, :] = jnp.sum(back, axis=0, keepdims=True)
    sums_ref[3:4, :] = jnp.sum(grad, axis=0, keepdims=True)


def query_back_kernel(
    grad_ref, normed_ref, attended_ref, low_ref, mine_ref, theirs_ref,
    normed_grad_ref, mine_part_ref, theirs_part_ref, mine_out_ref, theirs_out_ref, bias_ref,
):
    width = mine_ref.shape[1]
    normed = normed_ref[...].T
    attended = attended_ref[...].T
    mine, theirs = grad_ref[:, :width], grad_ref[:, width:]
    normed_grad_ref[...] = mm_cols(mine, mine_ref[...]) + mm_cols(theirs, theirs_ref[...])
    theirs_part_ref[...] = mm(normed, theirs).astype(jnp.bfloat16)
    theirs_out_ref[...] = mm(attended[width:], low_ref[...]).astype(jnp.bfloat16)
    mine_part_ref[...] = mm(normed, mine)
    mine_out_ref[...] = mm(attended[:width], low_ref[...])
    bias_ref[...] = jnp.sum(grad_ref[...].astype(jnp.float32), axis=0, keepdims=True)


def token_back_kernel(
    arrived_ref, normed_grad_ref, weight_ref, tokens_ref, gain_ref, normed_ref, middle_grad_ref,
    query_ref, peer_query_ref, out_ref, peer_out_ref, middle_sums_ref, query_bias_ref, expand_bias_ref,
    tokens_grad_ref, half_ref, sent_ref, rows_ref,
):
    grad = arrived_ref[0].astype(jnp.float32)
    for i in range(1, arrived_ref.shape[0]):
        grad = grad + arrived_ref[i].astype(jnp.float32)
    grad = grad.astype(jnp.bfloat16)
    back = normed_grad_ref[...] + mm_cols(grad, weight_ref[...])
    normal, scale = statistics(tokens_ref[...].astype(jnp.float32))
    weighted = back * gain_ref[...]
    mean = jnp.mean(weighted, axis=-1, keepdims=True)
    along = jnp.mean(weighted * normal, axis=-1, keepdims=True)
    tokens_grad = middle_grad_ref[...] + scale * (weighted - mean - normal * along)
    half = half_ref.shape[0]
    tokens_grad_ref[...] = tokens_grad[:half]
    half_ref[...] = tokens_grad[half:].astype(jnp.bfloat16)

    place = 0

    def put(values):
        nonlocal place
        depth = values.shape[0]
        sent_ref[place : place + depth, :] = values.astype(jnp.bfloat16)
        place += depth

    for ref, peer in ((query_ref, peer_query_ref), (out_ref, peer_out_ref)):
        for col in range(0, ref.shape[1], HALF):
            span = slice(col, col + HALF)
            put(ref[:, span] + peer[:, span].astype(jnp.float32))
    put(mm(normed_ref[...].T, grad))
    vectors = [middle_sums_ref[i : i + 1, :] for i in range(4)]
    vectors += [jnp.sum(back * normal, axis=0, keepdims=True), jnp.sum(back, axis=0, keepdims=True)]
    vectors += [query_bias_ref[...], jnp.sum(grad.astype(jnp.float32), axis=0, keepdims=True), expand_bias_ref[...]]
    rows_ref[...] = jnp.zeros_like(rows_ref)
    row = 0
    for vector in vectors:
        for col in range(0, vector.shape[1], HALF):
            rows_ref[row : row + 1, :] = vector[:, col : col + HALF]
            row += 1
    rows = rows_ref[...]
    high = rows.astype(jnp.bfloat16)
    put(high)
    put(rows - high.astype(jnp.float32))
    sent_ref[place:, :] = jnp.zeros_like(sent_ref[place:, :])


def unpack_kernel(full_ref, query_ref, out_ref, keyval_ref, rows_ref):
    place = 0
    for ref in (query_ref, out_ref, keyval_ref):
        depth = ref.shape[0]
        for col in range(0, ref.shape[1], HALF):
            ref[:, col : col + HALF] = full_ref[place : place + depth, :].astype(jnp.float32)
            place += depth
    depth = rows_ref.shape[0]
    high = full_ref[place : place + depth, :].astype(jnp.float32)
    rows_ref[...] = high + full_ref[place + depth : place + 2 * depth, :].astype(jnp.float32)


def like(*shape, dtype=jnp.float32):
    return jax.ShapeDtypeStruct(shape, dtype)


def run(kernel, outs, scratch, limit, flops, name, *args):
    return pl.pallas_call(
        kernel,
        out_shape=outs,
        in_specs=[VM] * len(args),
        out_specs=tuple(VM for _ in outs),
        scratch_shapes=scratch,
        compiler_params=pltpu.CompilerParams(vmem_limit_bytes=limit * 2**20),
        cost_estimate=pl.CostEstimate(flops=flops, bytes_accessed=2**20, transcendentals=0),
        name=name,
    )(*args)


def residual(attended, tokens, pair, bias, gain, shift):
    outs = (like(*tokens.shape), like(*tokens.shape, dtype=jnp.bfloat16))
    rows = (bias[None], gain[None], shift[None])
    return run(residual_kernel, outs, [], 24, 10**9, "residual", attended, tokens, *pair, *rows)


def own_keyval_blocks(tokens, gain, shift, weight, bias, count):
    outs = (like(count, tokens.shape[0], weight.shape[1], dtype=jnp.bfloat16),)
    return run(own_kernel, outs, [], 24, 10**8, "own_keyval", tokens, gain[None], shift[None], weight, bias[None])[0]


def query_rows(own, half, gain, shift, pair, biases):
    low16 = like(*own.shape, dtype=jnp.bfloat16)
    rows = (gain[None], shift[None])
    outs = (low16, low16, low16)
    return run(
        query_kernel, outs, [], 24, 3 * 10**10, "query_rows", own, half, *rows, *pair, biases[0][None], biases[1][None]
    )


def mlp(own, peer, own_grad, peer_grad, expand, bias, contract):
    rows, features = own.shape
    hidden = expand.shape[1]
    b16 = jnp.bfloat16
    outs = (
        like(hidden, features, dtype=b16),
        like(features, hidden, dtype=b16),
        like(1, hidden),
        like(rows, features),
        like(rows, features, dtype=b16),
        like(rows, features),
        like(rows, features, dtype=b16),
    )
    scratch = [
        pltpu.VMEM((2 * rows, features), b16),
        pltpu.VMEM((features, 2 * rows), b16),
        pltpu.VMEM((2 * rows, features), b16),
        pltpu.VMEM((2 * rows, features), jnp.float32),
        pltpu.VMEM((2 * rows, features), jnp.float32),
    ]
    return run(
        mlp_kernel, outs, scratch, 48, 10**10, "mlp", own, peer, own_grad, peer_grad, expand, bias[None], contract
    )


def widen(contract, expand):
    steps = 8

    def spec(array):
        return pl.BlockSpec((array.shape[0] // steps, array.shape[1]), lambda i: (i, 0))

    return pl.pallas_call(
        widen_kernel,
        grid=(steps,),
        out_shape=(like(*contract.shape), like(*expand.shape)),
        in_specs=[spec(contract), spec(expand)],
        out_specs=(spec(contract), spec(expand)),
        compiler_params=pltpu.CompilerParams(vmem_limit_bytes=60 * 2**20),
        name="widen",
    )(contract, expand)


def residual_back(back, peer_back, grad, middle, gain, pair):
    rows, features = grad.shape
    b16 = jnp.bfloat16
    outs = (like(rows, features), like(rows, features, dtype=b16), like(rows, features, dtype=b16), like(8, features))
    return run(
        residual_back_kernel, outs, [], 24, 10**9, "residual_back", back, peer_back, grad, middle, gain[None], *pair
    )


SWAP = ((0, 1), (1, 0))


def query_back(grad, normed, attended, lowered, pair):
    rows, features = grad.shape
    width = pair[0].shape[1]
    b16 = jnp.bfloat16
    outs = (
        like(rows, features),
        like(features, width),
        like(features, width, dtype=b16),
        like(width, features),
        like(width, features, dtype=b16),
        like(1, features),
    )
    return run(query_back_kernel, outs, [], 32, 10**10, "query_back", grad, normed, attended, lowered, *pair)


def token_back(ranks, arrived, normed_grad, weight, tokens, gain, normed, middle_grad, parts, vectors):
    rows, features = normed.shape
    depth = sum(p.size for p in (parts[0], parts[2], weight)) // HALF + 2 * VECTOR_ROWS
    depth += -depth % (8 * ranks)
    outs = (like(rows // 2, features), like(rows // 2, features, dtype=jnp.bfloat16), like(depth, HALF, dtype=jnp.bfloat16))
    return run(
        token_back_kernel, outs, [pltpu.VMEM((VECTOR_ROWS, HALF), jnp.float32)], 32, 10**9, "token_back",
        arrived, normed_grad, weight, tokens, gain[None], normed, middle_grad, *parts, *vectors,
    )


def unpack(full, query_shape, out_shape, keyval_shape):
    outs = (like(*query_shape), like(*out_shape), like(*keyval_shape), like(VECTOR_ROWS, HALF))
    return run(unpack_kernel, outs, [], 32, 10**8, "unpack", full)


def low(value):
    return value.astype(jnp.bfloat16)


def swapped(value):
    return lax.ppermute(value, "heads", SWAP)


def opposite(value):
    count = lax.axis_size(("seq", "heads"))
    return lax.ppermute(value, ("seq", "heads"), [(i, count - 1 - i) for i in range(count)])


def exchanged(value):
    half = value.shape[0] // 2
    return jnp.concatenate([value[:half], opposite(value[half:])], axis=0)


def spread_out(blocks, axis):
    return lax.all_to_all(blocks, axis, split_axis=0, concat_axis=0, tiled=True)


def copies(value, axis):
    return spread_out(jnp.broadcast_to(value[None], (lax.axis_size(axis), *value.shape)), axis)


def per_device(
    tokens,
    first_gain,
    first_shift,
    query_weight,
    query_bias,
    keyval_weight,
    value_bias,
    out_weight,
    out_bias,
    second_gain,
    second_shift,
    expand_weight,
    expand_bias,
    contract_weight,
    contract_bias,
    cotangent,
    lengths,
):
    f32 = jnp.float32
    place = lax.axis_index(("seq", "heads"))
    places = place.astype(jnp.int32).reshape(1)
    ranks = lax.axis_size(("win", "seq"))

    received = opposite(jnp.concatenate([tokens[0, HALF:], cotangent[0, HALF:]]))
    tokens_half = received[:HALF]
    grad_low = jnp.concatenate([cotangent[0, :HALF], received[HALF:]])
    own_blocks = own_keyval_blocks(
        tokens[0], first_gain, first_shift, keyval_weight, value_bias, lax.axis_size("seq")
    )
    own_blocks = spread_out(own_blocks, "seq")
    query_pair = (query_weight, swapped(query_weight))
    out_pair = (out_weight, swapped(out_weight))
    query_biases = (query_bias, swapped(query_bias))

    bounds = jnp.cumsum(lengths[0])
    first = jnp.stack(positions(place.astype(jnp.int32)))
    position = first[:, None] + jnp.arange(HALF, dtype=jnp.int32)[None, :]
    starts = jnp.max(jnp.where(bounds[None, None, :] <= position[:, :, None], bounds, 0), axis=2)
    starts = starts.astype(jnp.int32).reshape(2, 1, HALF)

    tokens_low, normed_low, query8 = query_rows(
        tokens[0], tokens_half, first_gain, first_shift, query_pair, query_biases
    )
    own_blocks, query8 = lax.optimization_barrier((own_blocks, query8))
    peer_blocks = swapped(own_blocks)
    attended, out, logs = attend(places, query8, own_blocks, peer_blocks, starts)
    width = query_bias.shape[0]
    middle, normed2_low = residual(attended, tokens_low, out_pair, out_bias, second_gain, second_shift)
    peer_grad_low = swapped(grad_low)
    contract_part, expand_part, expand_bias_part, out_rows, peer_out, back_rows, peer_back = mlp(
        normed2_low, swapped(normed2_low), grad_low, peer_grad_low, expand_weight, expand_bias, contract_weight
    )
    contract_total, expand_total = lax.psum((contract_part, expand_part), ("win", "seq"))
    middle_grad, middle_low, attended_grad, middle_sums = residual_back(
        back_rows, swapped(peer_back), grad_low, middle, second_gain, out_pair
    )

    def rest():
        query_grad, mine, theirs = attend_back(
            places, query8, own_blocks, peer_blocks, starts, attended_grad, out, logs
        )
        mlp_out = out_rows + swapped(peer_out).astype(f32)
        block_out = exchanged(low(middle + mlp_out + contract_bias))
        pair_grad = low(mine.astype(f32) + swapped(theirs).astype(f32))
        arrived = spread_out(pair_grad, "seq")
        from_query, query_part, query_sent, out_part, out_sent, query_bias_part = query_back(
            query_grad, normed_low, attended, middle_low, query_pair
        )
        core = lax.axis_index("heads")
        turned_bias = jnp.concatenate([query_bias_part[:, width:], query_bias_part[:, :width]], axis=1)
        query_bias_part = jnp.where(core == 0, query_bias_part, turned_bias)
        tokens_grad, half, sent = token_back(
            ranks, arrived, from_query, keyval_weight, tokens_low, first_gain, normed_low, middle_grad,
            (query_part, swapped(query_sent), out_part, swapped(out_sent)),
            (middle_sums, query_bias_part, expand_bias_part),
        )
        tokens_grad = jnp.concatenate([tokens_grad, opposite(half).astype(f32)], axis=0)

        blocks = sent.reshape(ranks, -1, HALF)
        depth = blocks.shape[1]
        wins = lax.axis_size("win")
        summed = spread_out(blocks.reshape(wins, -1, depth, HALF), "win")
        summed = low(jnp.sum(summed.astype(f32), axis=0))
        summed = jnp.sum(spread_out(summed, "seq").astype(f32), axis=0)
        row = lax.axis_index(("win", "seq")) * depth + jnp.arange(depth)[:, None]
        weights = query_weight.size + out_weight.size
        features = first_gain.shape[0]
        vectors = weights + keyval_weight.size
        alone = vectors + 7 * features + HALF
        shared = (row >= weights // HALF) & (row < alone // HALF)
        alone += VECTOR_ROWS * HALF
        shared = shared | ((row >= vectors // HALF + VECTOR_ROWS) & (row < alone // HALF))
        summed = summed + jnp.where(shared, swapped(summed), 0.0)
        full = copies(copies(low(summed), "seq"), "win").reshape(-1, HALF)
        query_total, out_total, keyval_total, rows = unpack(
            full, query_weight.shape, out_weight.shape, keyval_weight.shape
        )
        rows = rows.reshape(-1)
        sizes = [features] * 7 + [HALF, expand_bias.shape[0]]
        totals = []
        for size in sizes:
            totals.append(rows[:size])
            rows = rows[size:]
        query_bias_total = jnp.where(core == 0, totals[6][:width], totals[6][width:])
        return (
            block_out[None],
            tokens_grad[None],
            totals[4],
            totals[5],
            query_total,
            query_bias_total,
            keyval_total,
            totals[7][DH:],
            out_total,
            totals[0],
            totals[1],
            totals[2],
            totals[8],
            totals[3],
        )

    shapes = jax.eval_shape(rest)

    def nothing():
        return jax.tree.map(lambda s: jnp.zeros(s.shape, s.dtype), shapes)

    outs = lax.cond(lengths[0, 0] > 0, rest, nothing)
    contract_total, expand_total = widen(contract_total, expand_total)
    return (
        *outs[:12],
        expand_total,
        outs[12],
        contract_total,
        outs[13],
    )


def solution(mesh):
    return jax.shard_map(
        per_device,
        mesh=mesh,
        in_specs=(
            P("win", ("seq", "heads"), None),
            P(),
            P(),
            P(None, "heads"),
            P("heads"),
            P(),
            P(),
            P("heads", None),
            P(),
            P(),
            P(),
            P(None, "heads"),
            P("heads"),
            P("heads", None),
            P(),
            P("win", ("seq", "heads"), None),
            P("win", None),
        ),
        out_specs=(
            P("win", ("seq", "heads"), None),
            P("win", ("seq", "heads"), None),
            P(),
            P(),
            P(None, "heads"),
            P("heads"),
            P(),
            P(),
            P("heads", None),
            P(),
            P(),
            P(),
            P(None, "heads"),
            P("heads"),
            P("heads", None),
            P(),
        ),
        check_vma=False,
    )
```

```python
import math
import jax
import jax.numpy as jnp
from jax import lax
from jax.experimental import pallas as pl
from jax.experimental.pallas import tpu as pltpu
from jax.sharding import PartitionSpec as P

DH = 64
NEG = -1e30
TILE = 256
LANES = 256
HALF = 128


def mm(left, right):
    return lax.dot_general(left, right, (((1,), (0,)), ((), ())), preferred_element_type=jnp.float32)


def pieces(row, width):
    high = row.astype(jnp.bfloat16).astype(jnp.float32)
    rest = row - high
    mid = rest.astype(jnp.bfloat16).astype(jnp.float32)
    low = rest - mid
    which = lax.broadcasted_iota(jnp.int32, (16, width), 0)
    block = jnp.where(which == 0, -high, jnp.where(which == 1, -mid, jnp.where(which == 2, -low, 0.0)))
    return block.astype(jnp.bfloat16)


def with_ones(part):
    lane = lax.broadcasted_iota(jnp.int32, (part.shape[0], HALF), 1)
    wide = jnp.concatenate([part, jnp.zeros_like(part)], axis=1)
    return jnp.where((lane >= DH) & (lane < DH + 3), jnp.ones_like(wide), wide)


def mask_of(tile, chunk_pos, starts):
    key = tile * TILE + lax.broadcasted_iota(jnp.int32, (TILE, HALF), 0)
    query = chunk_pos + lax.broadcasted_iota(jnp.int32, (TILE, HALF), 1)
    mask = jnp.where((key <= query) & (key >= starts), 0.0, NEG)
    return jnp.concatenate([mask, mask], axis=1)


def in_pairs(first, last, step):
    count = jnp.maximum(last - first, 0)

    def two(i, _):
        step(first + 2 * i, 2)
        return 0

    lax.fori_loop(0, lax.div(count, 2), two, 0)

    @pl.when(lax.rem(count, 2) == 1)
    def _():
        step(last - 1, 1)


def block_of(own_ref, peer_ref, place, tile):
    pair = lax.div(tile, 2)
    own = lax.rem(tile, 2) == lax.rem(place, 2)
    return jnp.where(own, own_ref[pair], peer_ref[pair])


def positions(place):
    return (place * 2 * HALF, 63 * HALF - place * 2 * HALF)


def forward_kernel(place_ref, query_ref, own_ref, peer_ref, starts_ref, attended_ref, out_ref, log_ref, kx, vt, qt, acc, high):
    subs = qt.shape[2] // LANES
    chunk_pos = positions(place_ref[0])

    def prepare(tile, _):
        rows = pl.ds(pl.multiple_of(tile * TILE, TILE), TILE)
        block = block_of(own_ref, peer_ref, place_ref[0], tile)
        kx[rows, :] = with_ones(block[:, :DH])
        vt[:DH, rows] = block[:, DH:].T
        return 0

    lax.fori_loop(0, 2 * own_ref.shape[0], prepare, 0, unroll=4)
    vt[DH:, :] = jnp.ones_like(vt[DH:, :])

    def chunk(c, _):
        first = jnp.where(c == 0, chunk_pos[0], chunk_pos[1])
        diag = lax.div(first, TILE)
        lines = pl.ds(pl.multiple_of(c * HALF, HALF), HALF)
        starts = starts_ref[c]
        wide = jnp.concatenate([starts, starts], axis=1)
        spans = [slice(s * LANES, (s + 1) * LANES) for s in range(subs)]
        for s, cols in enumerate(spans):
            pair = query_ref[lines, s * 2 * DH : (s + 1) * 2 * DH].T
            qt[c, :DH, cols] = jnp.concatenate([pair[:DH], pair[DH:]], axis=1)
            qt[c, DH:, cols] = jnp.zeros_like(qt[c, DH:, cols])

        def rows_of(tile, count=1):
            return pl.ds(pl.multiple_of(tile * TILE, TILE), count * TILE)

        def scores(tile, count=1):
            return [mm(kx[rows_of(tile, count), :], qt[c, :, cols]) for cols in spans]

        def gather(tile, probs, fresh=False, count=1):
            rows = rows_of(tile, count)
            for cols, prob in zip(spans, probs):
                part = mm(vt[:, rows], prob)
                if fresh:
                    acc[c, :, cols] = part
                else:
                    acc[c, :, cols] += part

        def exps(values):
            return [jnp.exp(v).astype(jnp.bfloat16) for v in values]

        def set_shift(used):
            for cols in spans:
                if used:
                    block = pieces(jnp.where(wide <= TILE, high[c, :1, cols], -NEG), LANES)
                else:
                    block = jnp.zeros((16, LANES), jnp.bfloat16)
                qt[c, DH : DH + 16, cols] = block

        def sweep(again):
            mask = mask_of(diag, first, starts)
            values = [v + mask for v in scores(diag)]
            if again:
                tops = [high[c, :1, cols] for cols in spans]
            else:
                tops = [jnp.max(v, axis=0, keepdims=True) for v in values]
                for cols, top in zip(spans, tops):
                    high[c, :1, cols] = top
            gather(diag, exps([v - top for v, top in zip(values, tops)]), fresh=True)

            @pl.when(diag > 0)
            def _():
                set_shift(True)
                mask = mask_of(0, first, starts)
                gather(0, exps([v + mask for v in scores(0)]))
                in_pairs(1, diag, lambda tile, count: gather(tile, exps(scores(tile, count)), count=count))

        sweep(False)

        @pl.when(jnp.logical_not(jnp.max(acc[c, DH : DH + 1, :]) < 1e30))
        def _():
            set_shift(False)

            def raise_to(values):
                for cols, v in zip(spans, values):
                    high[c, :1, cols] = jnp.maximum(high[c, :1, cols], jnp.max(v, axis=0, keepdims=True))

            @pl.when(diag > 0)
            def _():
                mask = mask_of(0, first, starts)
                raise_to([v + mask for v in scores(0)])

                def step(tile, _):
                    raise_to([jnp.where(wide <= TILE, v, NEG) for v in scores(tile)])
                    return 0

                lax.fori_loop(1, diag, step, 0)

            sweep(True)

        for s, cols in enumerate(spans):
            total = acc[c, DH : DH + 1, cols]
            result = acc[c, :DH, cols] / total
            out_ref[c, :, cols] = result
            log_ref[c, :, cols] = high[c, :1, cols] + jnp.log(total)
            stacked = jnp.concatenate([result[:, :HALF], result[:, HALF:]], axis=0)
            attended_ref[lines, s * 2 * DH : (s + 1) * 2 * DH] = stacked.astype(jnp.bfloat16).T
        return 0

    lax.fori_loop(0, 2, chunk, 0)


def backward_kernel(
    place_ref, query_ref, own_ref, peer_ref, starts_ref, grad_ref, out_ref, log_ref,
    dquery_ref, mine_ref, theirs_ref, kx, vx, kt, qt, gt, wq, wg, dq, dkv,
):
    subs = qt.shape[2] // LANES
    place = place_ref[0]
    chunk_pos = positions(place)

    def prepare(tile, _):
        rows = pl.ds(pl.multiple_of(tile * TILE, TILE), TILE)
        block = block_of(own_ref, peer_ref, place, tile)
        kx[rows, :] = with_ones(block[:, :DH])
        vx[rows, :] = with_ones(block[:, DH:])
        kt[:, rows] = block[:, :DH].T
        return 0

    lax.fori_loop(0, 2 * own_ref.shape[0], prepare, 0, unroll=4)
    dkv[...] = jnp.zeros_like(dkv)

    def chunk(c, _):
        first = jnp.where(c == 0, chunk_pos[0], chunk_pos[1])
        diag = lax.div(first, TILE)
        lines = pl.ds(pl.multiple_of(c * HALF, HALF), HALF)
        starts = jnp.concatenate([starts_ref[c], starts_ref[c]], axis=1)
        empty = jnp.zeros((HALF, DH), jnp.bfloat16)
        for s in range(subs):
            cols = slice(s * LANES, (s + 1) * LANES)
            q2 = query_ref[lines, s * 2 * DH : (s + 1) * 2 * DH]
            g2 = grad_ref[lines, s * 2 * DH : (s + 1) * 2 * DH]
            q2t, g2t = q2.T, g2.T
            qt[c, :DH, cols] = jnp.concatenate([q2t[:DH], q2t[DH:]], axis=1)
            grad_t = jnp.concatenate([g2t[:DH], g2t[DH:]], axis=1)
            gt[c, :DH, cols] = grad_t
            qt[c, DH:, cols] = jnp.zeros_like(qt[c, DH:, cols])
            gt[c, DH + 16 :, cols] = jnp.zeros_like(gt[c, DH + 16 :, cols])
            delta = jnp.sum(grad_t.astype(jnp.float32) * out_ref[c, :, cols], axis=0, keepdims=True)
            gt[c, DH : DH + 16, cols] = pieces(delta, LANES)
            for h in range(2):
                rows = slice(h * HALF, (h + 1) * HALF)
                wq[c, s, rows, :] = jnp.concatenate([q2[:, h * DH : (h + 1) * DH], empty], axis=1)
                wg[c, s, rows, :] = jnp.concatenate([empty, g2[:, h * DH : (h + 1) * DH]], axis=1)

        def add(tile, mask=None, logs=None, fresh=False, count=1):
            rows = pl.ds(pl.multiple_of(tile * TILE, TILE), count * TILE)
            total = jnp.zeros((count * TILE, 2 * DH), jnp.float32)
            for base in range(0, subs, 3):
                group = range(base, base + 3)
                spans = [slice(s * LANES, (s + 1) * LANES) for s in group]
                sts = [mm(kx[rows, :], qt[c, :, cols]) for cols in spans]
                dps = [mm(vx[rows, :], gt[c, :, cols]) for cols in spans]
                if mask is not None:
                    sts = [st + mask for st in sts]
                if logs is not None:
                    sts = [st - log_ref[c, :, cols] for st, cols in zip(sts, spans)]
                probs = [jnp.exp(st) for st in sts]
                dss = [(p * dp).astype(jnp.bfloat16) for p, dp in zip(probs, dps)]
                lows = [p.astype(jnp.bfloat16) for p in probs]
                for s, ds, low in zip(group, dss, lows):
                    total = total + (mm(ds, wq[c, s]) + mm(low, wg[c, s]))
                for cols, ds in zip(spans, dss):
                    part = mm(kt[:, rows], ds)
                    if fresh:
                        dq[c, :, cols] = part
                    else:
                        dq[c, :, cols] += part
            dkv[rows, :] += total

        add(diag, mask_of(diag, first, starts_ref[c]), log_ref, fresh=True)

        @pl.when(diag > 0)
        def _():
            for s in range(subs):
                cols = slice(s * LANES, (s + 1) * LANES)
                qt[c, DH : DH + 16, cols] = pieces(jnp.where(starts <= TILE, log_ref[c, :, cols], -NEG), LANES)
            add(0, mask_of(0, first, starts_ref[c]))

            in_pairs(1, diag, lambda tile, count: add(tile, count=count))

        for s in range(subs):
            cols = slice(s * LANES, (s + 1) * LANES)
            result = dq[c, :, cols] * 0.125
            stacked = jnp.concatenate([result[:, :HALF], result[:, HALF:]], axis=0)
            dquery_ref[lines, s * 2 * DH : (s + 1) * 2 * DH] = stacked.astype(jnp.bfloat16).T
        return 0

    lax.fori_loop(0, 2, chunk, 0)

    core = lax.rem(place, 2)

    def give(pair, _):
        for ref, owner in ((mine_ref, 2 * pair + core), (theirs_ref, 2 * pair + 1 - core)):
            for c, pos in enumerate(positions(owner)):
                rows = pl.ds(pl.multiple_of(pos, HALF), HALF)
                ref[pair, c * HALF : (c + 1) * HALF, :] = dkv[rows, :].astype(jnp.bfloat16)
        return 0

    lax.fori_loop(0, mine_ref.shape[0], give, 0)


VM = pl.BlockSpec(memory_space=pltpu.VMEM)
SM = pl.BlockSpec(memory_space=pltpu.SMEM)


def attend(place, query8, own, peer, starts):
    rows, width = query8.shape
    window = 2 * own.shape[0] * own.shape[1]
    lanes = (width // DH) * HALF
    return pl.pallas_call(
        forward_kernel,
        out_shape=(
            jax.ShapeDtypeStruct((rows, width), jnp.bfloat16),
            jax.ShapeDtypeStruct((2, DH, lanes), jnp.float32),
            jax.ShapeDtypeStruct((2, 1, lanes), jnp.float32),
        ),
        in_specs=[SM] + [VM] * 4,
        out_specs=(VM, VM, VM),
        scratch_shapes=[
            pltpu.VMEM((window, HALF), jnp.bfloat16),
            pltpu.VMEM((DH + 16, window), jnp.bfloat16),
            pltpu.VMEM((2, HALF, lanes), jnp.bfloat16),
            pltpu.VMEM((2, DH + 16, lanes), jnp.float32),
            pltpu.VMEM((2, 8, lanes), jnp.float32),
        ],
        compiler_params=pltpu.CompilerParams(vmem_limit_bytes=16 * 2**20),
        cost_estimate=pl.CostEstimate(flops=25 * 10**9, bytes_accessed=8 * 2**20, transcendentals=13 * 10**6),
        name="attend",
    )(place, query8, own, peer, starts)


def attend_back(place, query8, own, peer, starts, grad, out, logs):
    rows, width = query8.shape
    window = 2 * own.shape[0] * own.shape[1]
    lanes = (width // DH) * HALF
    subs = lanes // LANES
    return pl.pallas_call(
        backward_kernel,
        out_shape=(
            jax.ShapeDtypeStruct((rows, width), jnp.bfloat16),
            jax.ShapeDtypeStruct((window // (4 * HALF), 2 * HALF, 2 * DH), jnp.bfloat16),
            jax.ShapeDtypeStruct((window // (4 * HALF), 2 * HALF, 2 * DH), jnp.bfloat16),
        ),
        in_specs=[SM] + [VM] * 7,
        out_specs=(VM, VM, VM),
        scratch_shapes=[
            pltpu.VMEM((window, HALF), jnp.bfloat16),
            pltpu.VMEM((window, HALF), jnp.bfloat16),
            pltpu.VMEM((DH, window), jnp.bfloat16),
            pltpu.VMEM((2, HALF, lanes), jnp.bfloat16),
            pltpu.VMEM((2, HALF, lanes), jnp.bfloat16),
            pltpu.VMEM((2, subs, LANES, HALF), jnp.bfloat16),
            pltpu.VMEM((2, subs, LANES, HALF), jnp.bfloat16),
            pltpu.VMEM((2, DH, lanes), jnp.float32),
            pltpu.VMEM((window, HALF), jnp.float32),
        ],
        compiler_params=pltpu.CompilerParams(vmem_limit_bytes=26 * 2**20),
        cost_estimate=pl.CostEstimate(flops=45 * 10**9, bytes_accessed=12 * 2**20, transcendentals=13 * 10**6),
        name="attend_back",
    )(place, query8, own, peer, starts, grad, out, logs)


EPS = 1e-05
CUBE = 0.044715
VECTOR_ROWS = 64
BLOCKS = 6
ROOT = math.sqrt(2.0 / math.pi)


def mm_cols(left, right):
    return lax.dot_general(left, right, (((1,), (1,)), ((), ())), preferred_element_type=jnp.float32)


def statistics(values):
    center = values - jnp.mean(values, axis=-1, keepdims=True)
    spread = jnp.mean(center * center, axis=-1, keepdims=True)
    scale = lax.rsqrt(spread + EPS)
    return center * scale, scale


def residual_kernel(
    attended_ref, tokens_ref, mine_ref, theirs_ref, bias_ref, gain_ref, shift_ref, middle_ref, normed_ref
):
    width = mine_ref.shape[0]
    rows = mm(attended_ref[:, :width], mine_ref[...]) + mm(attended_ref[:, width:], theirs_ref[...])
    middle = tokens_ref[...].astype(jnp.float32) + rows + bias_ref[...]
    middle_ref[...] = middle
    normal, _ = statistics(middle)
    normed_ref[...] = (normal * gain_ref[...] + shift_ref[...]).astype(jnp.bfloat16)


def own_kernel(tokens_ref, gain_ref, shift_ref, weight_ref, bias_ref, blocks_ref):
    normal, _ = statistics(tokens_ref[...].astype(jnp.float32))
    normed = (normal * gain_ref[...] + shift_ref[...]).astype(jnp.bfloat16)
    bias = jnp.concatenate([jnp.zeros_like(bias_ref[...]), bias_ref[...]], axis=1)
    keyval = (mm(normed, weight_ref[...]) + bias).astype(jnp.bfloat16)
    for i in range(blocks_ref.shape[0]):
        blocks_ref[i] = keyval


def query_kernel(
    own_ref, half_ref, gain_ref, shift_ref, mine_ref, theirs_ref, mine_bias_ref, theirs_bias_ref,
    tokens_ref, normed_ref, query_ref,
):
    half, width = half_ref.shape[0], mine_ref.shape[1]
    tokens_ref[:half, :] = own_ref[:half, :]
    tokens_ref[half:, :] = half_ref[...]
    normal, _ = statistics(tokens_ref[...].astype(jnp.float32))
    normed = (normal * gain_ref[...] + shift_ref[...]).astype(jnp.bfloat16)
    normed_ref[...] = normed
    mine = (mm(normed, mine_ref[...]) + mine_bias_ref[...]).astype(jnp.bfloat16)
    theirs = (mm(normed, theirs_ref[...]) + theirs_bias_ref[...]).astype(jnp.bfloat16)
    query_ref[:, :width] = mine * jnp.bfloat16(0.125)
    query_ref[:, width:] = theirs * jnp.bfloat16(0.125)


def mlp_kernel(
    own_ref, peer_ref, own_grad_ref, peer_grad_ref, expand_ref, bias_ref, contract_ref,
    contract_part_ref, expand_part_ref, bias_part_ref, own_out_ref, peer_out_ref, own_back_ref, peer_back_ref,
    both, turned, grads, acts_all, grad_all,
):
    rows = own_ref.shape[0]
    hidden = expand_ref.shape[1]
    block = hidden // BLOCKS
    both[:rows, :] = own_ref[...]
    both[rows:, :] = peer_ref[...]
    grads[:rows, :] = own_grad_ref[...]
    grads[rows:, :] = peer_grad_ref[...]
    spans = [slice(j * block, (j + 1) * block) for j in range(BLOCKS)]

    def products(cols):
        return mm(both[...], expand_ref[:, cols]), mm_cols(grads[...], contract_ref[cols, :])

    def activate(cols, inner, acts_grad):
        inner = inner + bias_ref[:, cols]
        square = inner * inner
        tanh = jnp.tanh(inner * (ROOT + ROOT * CUBE * square))
        half = 0.5 + 0.5 * tanh
        acts_all[:, cols] = (inner * half).astype(jnp.bfloat16)
        slope = half + inner * (0.5 - 0.5 * tanh * tanh) * (ROOT + 3.0 * ROOT * CUBE * square)
        grad = (acts_grad * slope).astype(jnp.bfloat16)
        grad_all[:, cols] = grad
        bias_part_ref[:, cols] = jnp.sum(grad.astype(jnp.float32), axis=0, keepdims=True)

    def weights(cols):
        contract_part_ref[cols, :] = mm(acts_all[:, cols].T, grads[...]).astype(jnp.bfloat16)
        expand_part_ref[:, cols] = mm(turned[...], grad_all[:, cols]).astype(jnp.bfloat16)

    turned[...] = both[...].T
    held = products(spans[0])
    for j, cols in enumerate(spans):
        later = products(spans[j + 1]) if j + 1 < BLOCKS else None
        activate(cols, *held)
        held = later
    for cols in spans:
        weights(cols)
    out = mm(acts_all[...], contract_ref[...])
    own_out_ref[...] = out[:rows, :]
    peer_out_ref[...] = out[rows:, :].astype(jnp.bfloat16)
    back = mm_cols(grad_all[...], expand_ref[...])
    own_back_ref[...] = back[:rows, :]
    peer_back_ref[...] = back[rows:, :].astype(jnp.bfloat16)


def widen_kernel(contract_ref, expand_ref, contract_out_ref, expand_out_ref):
    contract_out_ref[...] = contract_ref[...].astype(jnp.float32)
    expand_out_ref[...] = expand_ref[...].astype(jnp.float32)


def residual_back_kernel(
    back_ref, peer_back_ref, grad_ref, middle_ref, gain_ref, mine_ref, theirs_ref,
    middle_grad_ref, low_ref, attended_grad_ref, sums_ref,
):
    width = mine_ref.shape[0]
    back = back_ref[...] + peer_back_ref[...].astype(jnp.float32)
    grad = grad_ref[...].astype(jnp.float32)
    normal, scale = statistics(middle_ref[...])
    weighted = back * gain_ref[...]
    mean = jnp.mean(weighted, axis=-1, keepdims=True)
    along = jnp.mean(weighted * normal, axis=-1, keepdims=True)
    middle_grad = grad + scale * (weighted - mean - normal * along)
    middle_grad_ref[...] = middle_grad
    lowered = middle_grad.astype(jnp.bfloat16)
    low_ref[...] = lowered
    attended_grad_ref[:, :width] = mm_cols(lowered, mine_ref[...]).astype(jnp.bfloat16)
    attended_grad_ref[:, width:] = mm_cols(lowered, theirs_ref[...]).astype(jnp.bfloat16)
    sums_ref[0:1, :] = jnp.sum(middle_grad, axis=0, keepdims=True)
    sums_ref[1:2, :] = jnp.sum(back * normal, axis=0, keepdims=True)
    sums_ref[2:3, :] = jnp.sum(back, axis=0, keepdims=True)
    sums_ref[3:4, :] = jnp.sum(grad, axis=0, keepdims=True)


def query_back_kernel(
    grad_ref, normed_ref, attended_ref, low_ref, mine_ref, theirs_ref,
    normed_grad_ref, mine_part_ref, theirs_part_ref, mine_out_ref, theirs_out_ref, bias_ref,
):
    width = mine_ref.shape[1]
    normed = normed_ref[...].T
    attended = attended_ref[...].T
    mine, theirs = grad_ref[:, :width], grad_ref[:, width:]
    normed_grad_ref[...] = mm_cols(mine, mine_ref[...]) + mm_cols(theirs, theirs_ref[...])
    theirs_part_ref[...] = mm(normed, theirs).astype(jnp.bfloat16)
    theirs_out_ref[...] = mm(attended[width:], low_ref[...]).astype(jnp.bfloat16)
    mine_part_ref[...] = mm(normed, mine)
    mine_out_ref[...] = mm(attended[:width], low_ref[...])
    bias_ref[...] = jnp.sum(grad_ref[...].astype(jnp.float32), axis=0, keepdims=True)


def token_back_kernel(
    arrived_ref, normed_grad_ref, weight_ref, tokens_ref, gain_ref, normed_ref, middle_grad_ref,
    middle_sums_ref, query_bias_ref, expand_bias_ref,
    tokens_grad_ref, half_ref, sent_ref, rows_ref,
):
    grad = arrived_ref[0].astype(jnp.float32)
    for i in range(1, arrived_ref.shape[0]):
        grad = grad + arrived_ref[i].astype(jnp.float32)
    grad = grad.astype(jnp.bfloat16)
    back = normed_grad_ref[...] + mm_cols(grad, weight_ref[...])
    normal, scale = statistics(tokens_ref[...].astype(jnp.float32))
    weighted = back * gain_ref[...]
    mean = jnp.mean(weighted, axis=-1, keepdims=True)
    along = jnp.mean(weighted * normal, axis=-1, keepdims=True)
    tokens_grad = middle_grad_ref[...] + scale * (weighted - mean - normal * along)
    half = half_ref.shape[0]
    tokens_grad_ref[...] = tokens_grad[:half]
    half_ref[...] = tokens_grad[half:].astype(jnp.bfloat16)

    place = 0

    def put(values):
        nonlocal place
        depth = values.shape[0]
        sent_ref[place : place + depth, :] = values.astype(jnp.bfloat16)
        place += depth

    put(mm(normed_ref[...].T, grad))
    vectors = [middle_sums_ref[i : i + 1, :] for i in range(4)]
    vectors += [jnp.sum(back * normal, axis=0, keepdims=True), jnp.sum(back, axis=0, keepdims=True)]
    vectors += [query_bias_ref[...], jnp.sum(grad.astype(jnp.float32), axis=0, keepdims=True), expand_bias_ref[...]]
    rows_ref[...] = jnp.zeros_like(rows_ref)
    row = 0
    for vector in vectors:
        for col in range(0, vector.shape[1], HALF):
            rows_ref[row : row + 1, :] = vector[:, col : col + HALF]
            row += 1
    rows = rows_ref[...]
    high = rows.astype(jnp.bfloat16)
    put(high)
    put(rows - high.astype(jnp.float32))
    sent_ref[place:, :] = jnp.zeros_like(sent_ref[place:, :])


def pack_kernel(
    win_ref, query_ref, peer_query_ref, out_ref, peer_out_ref, own_ref, first_ref, second_ref, third_ref, packed
):
    place = 0
    for ref, peer in ((query_ref, peer_query_ref), (out_ref, peer_out_ref)):
        depth = ref.shape[0]
        for col in range(0, ref.shape[1], HALF):
            span = slice(col, col + HALF)
            packed[place : place + depth, :] = ref[:, span] + peer[:, span].astype(jnp.float32)
            place += depth
    depth = own_ref.shape[0]
    count = place // depth
    for shift, ref in enumerate((own_ref, first_ref, second_ref, third_ref)):
        to = lax.rem(win_ref[0] + shift, count)
        rows = pl.ds(pl.multiple_of(to * depth, HALF), depth)
        ref[...] = packed[rows, :].astype(ref.dtype)


def unpack_kernel(weights_ref, rest_ref, query_ref, out_ref, keyval_ref, rows_ref):
    place = 0
    for ref in (query_ref, out_ref):
        depth = ref.shape[0]
        for col in range(0, ref.shape[1], HALF):
            ref[:, col : col + HALF] = weights_ref[place : place + depth, :].astype(jnp.float32)
            place += depth
    place = keyval_ref.shape[0]
    keyval_ref[...] = rest_ref[:place, :].astype(jnp.float32)
    depth = rows_ref.shape[0]
    high = rest_ref[place : place + depth, :].astype(jnp.float32)
    rows_ref[...] = high + rest_ref[place + depth : place + 2 * depth, :].astype(jnp.float32)


def like(*shape, dtype=jnp.float32):
    return jax.ShapeDtypeStruct(shape, dtype)


def run(kernel, outs, scratch, limit, flops, name, *args):
    return pl.pallas_call(
        kernel,
        out_shape=outs,
        in_specs=[VM] * len(args),
        out_specs=tuple(VM for _ in outs),
        scratch_shapes=scratch,
        compiler_params=pltpu.CompilerParams(vmem_limit_bytes=limit * 2**20),
        cost_estimate=pl.CostEstimate(flops=flops, bytes_accessed=2**20, transcendentals=0),
        name=name,
    )(*args)


def residual(attended, tokens, pair, bias, gain, shift):
    outs = (like(*tokens.shape), like(*tokens.shape, dtype=jnp.bfloat16))
    rows = (bias[None], gain[None], shift[None])
    return run(residual_kernel, outs, [], 12, 10**9, "residual", attended, tokens, *pair, *rows)


def own_keyval_blocks(tokens, gain, shift, weight, bias, count):
    outs = (like(count, tokens.shape[0], weight.shape[1], dtype=jnp.bfloat16),)
    return run(own_kernel, outs, [], 8, 10**8, "own_keyval", tokens, gain[None], shift[None], weight, bias[None])[0]


def query_rows(own, half, gain, shift, pair, biases):
    low16 = like(*own.shape, dtype=jnp.bfloat16)
    rows = (gain[None], shift[None])
    outs = (low16, low16, low16)
    return run(
        query_kernel, outs, [], 12, 3 * 10**10, "query_rows", own, half, *rows, *pair, biases[0][None], biases[1][None]
    )


def mlp(own, peer, own_grad, peer_grad, expand, bias, contract):
    rows, features = own.shape
    hidden = expand.shape[1]
    b16 = jnp.bfloat16
    outs = (
        like(hidden, features, dtype=b16),
        like(features, hidden, dtype=b16),
        like(1, hidden),
        like(rows, features),
        like(rows, features, dtype=b16),
        like(rows, features),
        like(rows, features, dtype=b16),
    )
    scratch = [
        pltpu.VMEM((2 * rows, features), b16),
        pltpu.VMEM((features, 2 * rows), b16),
        pltpu.VMEM((2 * rows, features), b16),
        pltpu.VMEM((2 * rows, hidden), b16),
        pltpu.VMEM((2 * rows, hidden), b16),
    ]
    return run(
        mlp_kernel, outs, scratch, 32, 10**10, "mlp", own, peer, own_grad, peer_grad, expand, bias[None], contract
    )


def widen(contract, expand):
    steps = 2

    def spec(array):
        return pl.BlockSpec((array.shape[0] // steps, array.shape[1]), lambda i: (i, 0))

    return pl.pallas_call(
        widen_kernel,
        grid=(steps,),
        out_shape=(like(*contract.shape), like(*expand.shape)),
        in_specs=[spec(contract), spec(expand)],
        out_specs=(spec(contract), spec(expand)),
        compiler_params=pltpu.CompilerParams(vmem_limit_bytes=60 * 2**20),
        name="widen",
    )(contract, expand)


def residual_back(back, peer_back, grad, middle, gain, pair):
    rows, features = grad.shape
    b16 = jnp.bfloat16
    outs = (like(rows, features), like(rows, features, dtype=b16), like(rows, features, dtype=b16), like(8, features))
    return run(
        residual_back_kernel, outs, [], 12, 10**9, "residual_back", back, peer_back, grad, middle, gain[None], *pair
    )


SWAP = ((0, 1), (1, 0))


def query_back(grad, normed, attended, lowered, pair):
    rows, features = grad.shape
    width = pair[0].shape[1]
    b16 = jnp.bfloat16
    outs = (
        like(rows, features),
        like(features, width),
        like(features, width, dtype=b16),
        like(width, features),
        like(width, features, dtype=b16),
        like(1, features),
    )
    return run(query_back_kernel, outs, [], 16, 10**10, "query_back", grad, normed, attended, lowered, *pair)


def token_back(ranks, arrived, normed_grad, weight, tokens, gain, normed, middle_grad, vectors):
    rows, features = normed.shape
    depth = weight.shape[0] + 2 * VECTOR_ROWS
    depth += -depth % (16 * ranks)
    outs = (like(rows // 2, features), like(rows // 2, features, dtype=jnp.bfloat16), like(depth, HALF, dtype=jnp.bfloat16))
    return run(
        token_back_kernel, outs, [pltpu.VMEM((VECTOR_ROWS, HALF), jnp.float32)], 12, 10**9, "token_back",
        arrived, normed_grad, weight, tokens, gain[None], normed, middle_grad, *vectors,
    )


def pack(win, query_part, peer_query, out_part, peer_out):
    depth = (query_part.size + out_part.size) // HALF // 4
    outs = (like(depth, HALF), *(like(depth, HALF, dtype=jnp.bfloat16) for _ in range(3)))
    return pl.pallas_call(
        pack_kernel,
        out_shape=outs,
        in_specs=[SM] + [VM] * 4,
        out_specs=(VM,) * 4,
        scratch_shapes=[pltpu.VMEM((4 * depth, HALF), jnp.float32)],
        compiler_params=pltpu.CompilerParams(vmem_limit_bytes=16 * 2**20),
        name="pack",
    )(win, query_part, peer_query, out_part, peer_out)


def unpack(weights, rest, query_shape, out_shape, keyval_shape):
    outs = (like(*query_shape), like(*out_shape), like(*keyval_shape), like(VECTOR_ROWS, HALF))
    return run(unpack_kernel, outs, [], 12, 10**8, "unpack", weights, rest)


def low(value):
    return value.astype(jnp.bfloat16)


def swapped(value):
    return lax.ppermute(value, "heads", SWAP)


def opposite(value):
    count = lax.axis_size(("seq", "heads"))
    return lax.ppermute(value, ("seq", "heads"), [(i, count - 1 - i) for i in range(count)])


def exchanged(value):
    half = value.shape[0] // 2
    return jnp.concatenate([value[:half], opposite(value[half:])], axis=0)


def spread_out(blocks, axis):
    return lax.all_to_all(blocks, axis, split_axis=0, concat_axis=0, tiled=True)


def copies(value, axis):
    return spread_out(jnp.broadcast_to(value[None], (lax.axis_size(axis), *value.shape)), axis)


def per_device(
    tokens,
    first_gain,
    first_shift,
    query_weight,
    query_bias,
    keyval_weight,
    value_bias,
    out_weight,
    out_bias,
    second_gain,
    second_shift,
    expand_weight,
    expand_bias,
    contract_weight,
    contract_bias,
    cotangent,
    lengths,
):
    f32 = jnp.float32
    place = lax.axis_index(("seq", "heads"))
    places = place.astype(jnp.int32).reshape(1)
    ranks = lax.axis_size(("win", "seq"))

    received = opposite(jnp.concatenate([tokens[0, HALF:], cotangent[0, HALF:]]))
    tokens_half = received[:HALF]
    grad_low = jnp.concatenate([cotangent[0, :HALF], received[HALF:]])
    own_blocks = own_keyval_blocks(
        tokens[0], first_gain, first_shift, keyval_weight, value_bias, lax.axis_size("seq")
    )
    own_blocks = spread_out(own_blocks, "seq")
    query_pair = (query_weight, swapped(query_weight))
    out_pair = (out_weight, swapped(out_weight))
    query_biases = (query_bias, swapped(query_bias))

    bounds = jnp.cumsum(lengths[0])
    first = jnp.stack(positions(place.astype(jnp.int32)))
    position = first[:, None] + jnp.arange(HALF, dtype=jnp.int32)[None, :]
    starts = jnp.max(jnp.where(bounds[None, None, :] <= position[:, :, None], bounds, 0), axis=2)
    starts = starts.astype(jnp.int32).reshape(2, 1, HALF)

    tokens_low, normed_low, query8 = query_rows(
        tokens[0], tokens_half, first_gain, first_shift, query_pair, query_biases
    )
    own_blocks, query8 = lax.optimization_barrier((own_blocks, query8))
    peer_blocks = swapped(own_blocks)
    attended, out, logs = attend(places, query8, own_blocks, peer_blocks, starts)
    width = query_bias.shape[0]
    middle, normed2_low = residual(attended, tokens_low, out_pair, out_bias, second_gain, second_shift)
    peer_grad_low = swapped(grad_low)
    contract_part, expand_part, expand_bias_part, out_rows, peer_out, back_rows, peer_back = mlp(
        normed2_low, swapped(normed2_low), grad_low, peer_grad_low, expand_weight, expand_bias, contract_weight
    )
    contract_total, expand_total = lax.psum((contract_part, expand_part), ("win", "seq"))
    middle_grad, middle_low, attended_grad, middle_sums = residual_back(
        back_rows, swapped(peer_back), grad_low, middle, second_gain, out_pair
    )

    def rest():
        query_grad, mine, theirs = attend_back(
            places, query8, own_blocks, peer_blocks, starts, attended_grad, out, logs
        )
        mlp_out = out_rows + swapped(peer_out).astype(f32)
        block_out = exchanged(low(middle + mlp_out + contract_bias))
        pair_grad = low(mine.astype(f32) + swapped(theirs).astype(f32))
        arrived = spread_out(pair_grad, "seq")
        from_query, query_part, query_sent, out_part, out_sent, query_bias_part = query_back(
            query_grad, normed_low, attended, middle_low, query_pair
        )
        core = lax.axis_index("heads")
        turned_bias = jnp.concatenate([query_bias_part[:, width:], query_bias_part[:, :width]], axis=1)
        query_bias_part = jnp.where(core == 0, query_bias_part, turned_bias)
        wins, seqs = lax.axis_size("win"), lax.axis_size("seq")
        win = lax.axis_index("win").astype(jnp.int32)
        kept, *given = pack(win.reshape(1), query_part, swapped(query_sent), out_part, swapped(out_sent))
        taken = [
            lax.ppermute(g, "win", [(i, (i + shift) % wins) for i in range(wins)]) for shift, g in enumerate(given, 1)
        ]
        tokens_grad, half, sent = token_back(
            ranks, arrived, from_query, keyval_weight, tokens_low, first_gain, normed_low, middle_grad,
            (middle_sums, query_bias_part, expand_bias_part),
        )
        tokens_grad = jnp.concatenate([tokens_grad, opposite(half).astype(f32)], axis=0)

        sent, taken = lax.optimization_barrier((sent, taken))
        rest = spread_out(sent.reshape(wins, -1, HALF), "win")
        rest = low(jnp.sum(rest.astype(f32), axis=0)).reshape(seqs, -1, HALF)
        weights = low(kept + sum(t.astype(f32) for t in taken)).reshape(seqs, -1, HALF)
        depth = weights.shape[1]
        summed = jnp.sum(spread_out(jnp.concatenate([weights, rest], axis=1), "seq").astype(f32), axis=0)
        rest = summed[depth:]
        features = first_gain.shape[0]
        row = lax.axis_index(("win", "seq")) * rest.shape[0] + jnp.arange(rest.shape[0])[:, None]
        vectors = keyval_weight.shape[0]
        common = 7 * features // HALF + 1
        shared = row < vectors + common
        shared = shared | ((row >= vectors + VECTOR_ROWS) & (row < vectors + VECTOR_ROWS + common))
        rest = rest + jnp.where(shared, swapped(rest), 0.0)
        full = low(jnp.concatenate([summed[:depth], rest]))
        full = copies(copies(full, "seq"), "win")
        query_total, out_total, keyval_total, rows = unpack(
            full[:, :, :depth].reshape(-1, HALF),
            full[:, :, depth:].reshape(-1, HALF),
            query_weight.shape,
            out_weight.shape,
            keyval_weight.shape,
        )
        rows = rows.reshape(-1)
        sizes = [features] * 7 + [HALF, expand_bias.shape[0]]
        totals = []
        for size in sizes:
            totals.append(rows[:size])
            rows = rows[size:]
        query_bias_total = jnp.where(core == 0, totals[6][:width], totals[6][width:])
        return (
            block_out[None],
            tokens_grad[None],
            totals[4],
            totals[5],
            query_total,
            query_bias_total,
            keyval_total,
            totals[7][DH:],
            out_total,
            totals[0],
            totals[1],
            totals[2],
            totals[8],
            totals[3],
        )

    shapes = jax.eval_shape(rest)

    def nothing():
        return jax.tree.map(lambda s: jnp.zeros(s.shape, s.dtype), shapes)

    outs = lax.cond(lengths[0, 0] > 0, rest, nothing)
    contract_total, expand_total = widen(contract_total, expand_total)
    return (
        *outs[:12],
        expand_total,
        outs[12],
        contract_total,
        outs[13],
    )


def solution(mesh):
    return jax.shard_map(
        per_device,
        mesh=mesh,
        in_specs=(
            P("win", ("seq", "heads"), None),
            P(),
            P(),
            P(None, "heads"),
            P("heads"),
            P(),
            P(),
            P("heads", None),
            P(),
            P(),
            P(),
            P(None, "heads"),
            P("heads"),
            P("heads", None),
            P(),
            P("win", ("seq", "heads"), None),
            P("win", None),
        ),
        out_specs=(
            P("win", ("seq", "heads"), None),
            P("win", ("seq", "heads"), None),
            P(),
            P(),
            P(None, "heads"),
            P("heads"),
            P(),
            P(),
            P("heads", None),
            P(),
            P(),
            P(),
            P(None, "heads"),
            P("heads"),
            P("heads", None),
            P(),
        ),
        check_vma=False,
    )
```

```python
import math
import jax
import jax.numpy as jnp
from jax import lax
from jax.experimental import pallas as pl
from jax.experimental.pallas import tpu as pltpu
from jax.sharding import PartitionSpec as P

DH = 64
NEG = -1e30
TILE = 256
LANES = 256
HALF = 128


def mm(left, right):
    return lax.dot_general(left, right, (((1,), (0,)), ((), ())), preferred_element_type=jnp.float32)


def pieces(row, width):
    high = row.astype(jnp.bfloat16).astype(jnp.float32)
    rest = row - high
    mid = rest.astype(jnp.bfloat16).astype(jnp.float32)
    low = rest - mid
    which = lax.broadcasted_iota(jnp.int32, (16, width), 0)
    block = jnp.where(which == 0, -high, jnp.where(which == 1, -mid, jnp.where(which == 2, -low, 0.0)))
    return block.astype(jnp.bfloat16)


def with_ones(part):
    lane = lax.broadcasted_iota(jnp.int32, (part.shape[0], HALF), 1)
    wide = jnp.concatenate([part, jnp.zeros_like(part)], axis=1)
    return jnp.where((lane >= DH) & (lane < DH + 3), jnp.ones_like(wide), wide)


def mask_of(tile, chunk_pos, starts):
    key = tile * TILE + lax.broadcasted_iota(jnp.int32, (TILE, HALF), 0)
    query = chunk_pos + lax.broadcasted_iota(jnp.int32, (TILE, HALF), 1)
    mask = jnp.where((key <= query) & (key >= starts), 0.0, NEG)
    return jnp.concatenate([mask, mask], axis=1)


def in_pairs(first, last, step):
    count = jnp.maximum(last - first, 0)

    def two(i, _):
        step(first + 2 * i, 2)
        return 0

    lax.fori_loop(0, lax.div(count, 2), two, 0)

    @pl.when(lax.rem(count, 2) == 1)
    def _():
        step(last - 1, 1)


def block_of(own_ref, peer_ref, place, tile):
    pair = lax.div(tile, 2)
    own = lax.rem(tile, 2) == lax.rem(place, 2)
    return jnp.where(own, own_ref[pair], peer_ref[pair])


def positions(place):
    return (place * 2 * HALF, 63 * HALF - place * 2 * HALF)


def forward_kernel(place_ref, query_ref, own_ref, peer_ref, starts_ref, attended_ref, out_ref, log_ref, kx, vt, qt, acc, high):
    subs = qt.shape[2] // LANES
    chunk_pos = positions(place_ref[0])

    def prepare(tile, _):
        rows = pl.ds(pl.multiple_of(tile * TILE, TILE), TILE)
        block = block_of(own_ref, peer_ref, place_ref[0], tile)
        kx[rows, :] = with_ones(block[:, :DH])
        vt[:DH, rows] = block[:, DH:].T
        return 0

    lax.fori_loop(0, 2 * own_ref.shape[0], prepare, 0, unroll=4)
    vt[DH:, :] = jnp.ones_like(vt[DH:, :])

    def chunk(c, _):
        first = jnp.where(c == 0, chunk_pos[0], chunk_pos[1])
        diag = lax.div(first, TILE)
        lines = pl.ds(pl.multiple_of(c * HALF, HALF), HALF)
        starts = starts_ref[c]
        wide = jnp.concatenate([starts, starts], axis=1)
        spans = [slice(s * LANES, (s + 1) * LANES) for s in range(subs)]
        for s, cols in enumerate(spans):
            pair = query_ref[lines, s * 2 * DH : (s + 1) * 2 * DH].T
            qt[c, :DH, cols] = jnp.concatenate([pair[:DH], pair[DH:]], axis=1)
            qt[c, DH:, cols] = jnp.zeros_like(qt[c, DH:, cols])

        def rows_of(tile, count=1):
            return pl.ds(pl.multiple_of(tile * TILE, TILE), count * TILE)

        def scores(tile, count=1):
            return [mm(kx[rows_of(tile, count), :], qt[c, :, cols]) for cols in spans]

        def gather(tile, probs, fresh=False, count=1):
            rows = rows_of(tile, count)
            for cols, prob in zip(spans, probs):
                part = mm(vt[:, rows], prob)
                if fresh:
                    acc[c, :, cols] = part
                else:
                    acc[c, :, cols] += part

        def exps(values):
            return [jnp.exp(v).astype(jnp.bfloat16) for v in values]

        def set_shift(used):
            for cols in spans:
                if used:
                    block = pieces(jnp.where(wide <= TILE, high[c, :1, cols], -NEG), LANES)
                else:
                    block = jnp.zeros((16, LANES), jnp.bfloat16)
                qt[c, DH : DH + 16, cols] = block

        def sweep(again):
            mask = mask_of(diag, first, starts)
            values = [v + mask for v in scores(diag)]
            if again:
                tops = [high[c, :1, cols] for cols in spans]
            else:
                tops = [jnp.max(v, axis=0, keepdims=True) for v in values]
                for cols, top in zip(spans, tops):
                    high[c, :1, cols] = top
            gather(diag, exps([v - top for v, top in zip(values, tops)]), fresh=True)

            @pl.when(diag > 0)
            def _():
                set_shift(True)
                mask = mask_of(0, first, starts)
                gather(0, exps([v + mask for v in scores(0)]))
                in_pairs(1, diag, lambda tile, count: gather(tile, exps(scores(tile, count)), count=count))

        sweep(False)

        @pl.when(jnp.logical_not(jnp.max(acc[c, DH : DH + 1, :]) < 1e30))
        def _():
            set_shift(False)

            def raise_to(values):
                for cols, v in zip(spans, values):
                    high[c, :1, cols] = jnp.maximum(high[c, :1, cols], jnp.max(v, axis=0, keepdims=True))

            @pl.when(diag > 0)
            def _():
                mask = mask_of(0, first, starts)
                raise_to([v + mask for v in scores(0)])

                def step(tile, _):
                    raise_to([jnp.where(wide <= TILE, v, NEG) for v in scores(tile)])
                    return 0

                lax.fori_loop(1, diag, step, 0)

            sweep(True)

        for s, cols in enumerate(spans):
            total = acc[c, DH : DH + 1, cols]
            result = acc[c, :DH, cols] / total
            out_ref[c, :, cols] = result
            log_ref[c, :, cols] = high[c, :1, cols] + jnp.log(total)
            stacked = jnp.concatenate([result[:, :HALF], result[:, HALF:]], axis=0)
            attended_ref[lines, s * 2 * DH : (s + 1) * 2 * DH] = stacked.astype(jnp.bfloat16).T
        return 0

    lax.fori_loop(0, 2, chunk, 0)


def backward_kernel(
    place_ref, query_ref, own_ref, peer_ref, starts_ref, grad_ref, out_ref, log_ref,
    dquery_ref, mine_ref, theirs_ref, kx, vx, kt, qt, gt, wq, wg, dq, dkv,
):
    subs = qt.shape[2] // LANES
    place = place_ref[0]
    chunk_pos = positions(place)

    def prepare(tile, _):
        rows = pl.ds(pl.multiple_of(tile * TILE, TILE), TILE)
        block = block_of(own_ref, peer_ref, place, tile)
        kx[rows, :] = with_ones(block[:, :DH])
        vx[rows, :] = with_ones(block[:, DH:])
        kt[:, rows] = block[:, :DH].T
        return 0

    lax.fori_loop(0, 2 * own_ref.shape[0], prepare, 0, unroll=4)
    dkv[...] = jnp.zeros_like(dkv)

    def chunk(c, _):
        first = jnp.where(c == 0, chunk_pos[0], chunk_pos[1])
        diag = lax.div(first, TILE)
        lines = pl.ds(pl.multiple_of(c * HALF, HALF), HALF)
        starts = jnp.concatenate([starts_ref[c], starts_ref[c]], axis=1)
        empty = jnp.zeros((HALF, DH), jnp.bfloat16)
        for s in range(subs):
            cols = slice(s * LANES, (s + 1) * LANES)
            q2 = query_ref[lines, s * 2 * DH : (s + 1) * 2 * DH]
            g2 = grad_ref[lines, s * 2 * DH : (s + 1) * 2 * DH]
            q2t, g2t = q2.T, g2.T
            qt[c, :DH, cols] = jnp.concatenate([q2t[:DH], q2t[DH:]], axis=1)
            grad_t = jnp.concatenate([g2t[:DH], g2t[DH:]], axis=1)
            gt[c, :DH, cols] = grad_t
            qt[c, DH:, cols] = jnp.zeros_like(qt[c, DH:, cols])
            gt[c, DH + 16 :, cols] = jnp.zeros_like(gt[c, DH + 16 :, cols])
            delta = jnp.sum(grad_t.astype(jnp.float32) * out_ref[c, :, cols], axis=0, keepdims=True)
            gt[c, DH : DH + 16, cols] = pieces(delta, LANES)
            for h in range(2):
                rows = slice(h * HALF, (h + 1) * HALF)
                wq[c, s, rows, :] = jnp.concatenate([q2[:, h * DH : (h + 1) * DH], empty], axis=1)
                wg[c, s, rows, :] = jnp.concatenate([empty, g2[:, h * DH : (h + 1) * DH]], axis=1)

        def add(tile, mask=None, logs=None, fresh=False, count=1):
            rows = pl.ds(pl.multiple_of(tile * TILE, TILE), count * TILE)
            total = jnp.zeros((count * TILE, 2 * DH), jnp.float32)
            for base in range(0, subs, 3):
                group = range(base, base + 3)
                spans = [slice(s * LANES, (s + 1) * LANES) for s in group]
                sts = [mm(kx[rows, :], qt[c, :, cols]) for cols in spans]
                dps = [mm(vx[rows, :], gt[c, :, cols]) for cols in spans]
                if mask is not None:
                    sts = [st + mask for st in sts]
                if logs is not None:
                    sts = [st - log_ref[c, :, cols] for st, cols in zip(sts, spans)]
                probs = [jnp.exp(st) for st in sts]
                dss = [(p * dp).astype(jnp.bfloat16) for p, dp in zip(probs, dps)]
                lows = [p.astype(jnp.bfloat16) for p in probs]
                for s, ds, low in zip(group, dss, lows):
                    total = total + (mm(ds, wq[c, s]) + mm(low, wg[c, s]))
                for cols, ds in zip(spans, dss):
                    part = mm(kt[:, rows], ds)
                    if fresh:
                        dq[c, :, cols] = part
                    else:
                        dq[c, :, cols] += part
            dkv[rows, :] += total

        add(diag, mask_of(diag, first, starts_ref[c]), log_ref, fresh=True)

        @pl.when(diag > 0)
        def _():
            for s in range(subs):
                cols = slice(s * LANES, (s + 1) * LANES)
                qt[c, DH : DH + 16, cols] = pieces(jnp.where(starts <= TILE, log_ref[c, :, cols], -NEG), LANES)
            add(0, mask_of(0, first, starts_ref[c]))

            in_pairs(1, diag, lambda tile, count: add(tile, count=count))

        for s in range(subs):
            cols = slice(s * LANES, (s + 1) * LANES)
            result = dq[c, :, cols] * 0.125
            stacked = jnp.concatenate([result[:, :HALF], result[:, HALF:]], axis=0)
            dquery_ref[lines, s * 2 * DH : (s + 1) * 2 * DH] = stacked.astype(jnp.bfloat16).T
        return 0

    lax.fori_loop(0, 2, chunk, 0)

    core = lax.rem(place, 2)

    def give(pair, _):
        for ref, owner in ((mine_ref, 2 * pair + core), (theirs_ref, 2 * pair + 1 - core)):
            for c, pos in enumerate(positions(owner)):
                rows = pl.ds(pl.multiple_of(pos, HALF), HALF)
                ref[pair, c * HALF : (c + 1) * HALF, :] = dkv[rows, :].astype(jnp.bfloat16)
        return 0

    lax.fori_loop(0, mine_ref.shape[0], give, 0)


VM = pl.BlockSpec(memory_space=pltpu.VMEM)
SM = pl.BlockSpec(memory_space=pltpu.SMEM)


def attend(place, query8, own, peer, starts):
    rows, width = query8.shape
    window = 2 * own.shape[0] * own.shape[1]
    lanes = (width // DH) * HALF
    return pl.pallas_call(
        forward_kernel,
        out_shape=(
            jax.ShapeDtypeStruct((rows, width), jnp.bfloat16),
            jax.ShapeDtypeStruct((2, DH, lanes), jnp.float32),
            jax.ShapeDtypeStruct((2, 1, lanes), jnp.float32),
        ),
        in_specs=[SM] + [VM] * 4,
        out_specs=(VM, VM, VM),
        scratch_shapes=[
            pltpu.VMEM((window, HALF), jnp.bfloat16),
            pltpu.VMEM((DH + 16, window), jnp.bfloat16),
            pltpu.VMEM((2, HALF, lanes), jnp.bfloat16),
            pltpu.VMEM((2, DH + 16, lanes), jnp.float32),
            pltpu.VMEM((2, 8, lanes), jnp.float32),
        ],
        compiler_params=pltpu.CompilerParams(vmem_limit_bytes=16 * 2**20),
        cost_estimate=pl.CostEstimate(flops=25 * 10**9, bytes_accessed=8 * 2**20, transcendentals=13 * 10**6),
        name="attend",
    )(place, query8, own, peer, starts)


def attend_back(place, query8, own, peer, starts, grad, out, logs):
    rows, width = query8.shape
    window = 2 * own.shape[0] * own.shape[1]
    lanes = (width // DH) * HALF
    subs = lanes // LANES
    return pl.pallas_call(
        backward_kernel,
        out_shape=(
            jax.ShapeDtypeStruct((rows, width), jnp.bfloat16),
            jax.ShapeDtypeStruct((window // (4 * HALF), 2 * HALF, 2 * DH), jnp.bfloat16),
            jax.ShapeDtypeStruct((window // (4 * HALF), 2 * HALF, 2 * DH), jnp.bfloat16),
        ),
        in_specs=[SM] + [VM] * 7,
        out_specs=(VM, VM, VM),
        scratch_shapes=[
            pltpu.VMEM((window, HALF), jnp.bfloat16),
            pltpu.VMEM((window, HALF), jnp.bfloat16),
            pltpu.VMEM((DH, window), jnp.bfloat16),
            pltpu.VMEM((2, HALF, lanes), jnp.bfloat16),
            pltpu.VMEM((2, HALF, lanes), jnp.bfloat16),
            pltpu.VMEM((2, subs, LANES, HALF), jnp.bfloat16),
            pltpu.VMEM((2, subs, LANES, HALF), jnp.bfloat16),
            pltpu.VMEM((2, DH, lanes), jnp.float32),
            pltpu.VMEM((window, HALF), jnp.float32),
        ],
        compiler_params=pltpu.CompilerParams(vmem_limit_bytes=26 * 2**20),
        cost_estimate=pl.CostEstimate(flops=45 * 10**9, bytes_accessed=12 * 2**20, transcendentals=13 * 10**6),
        name="attend_back",
    )(place, query8, own, peer, starts, grad, out, logs)


EPS = 1e-05
CUBE = 0.044715
VECTOR_ROWS = 64
BLOCKS = 6
ROOT = math.sqrt(2.0 / math.pi)


def mm_cols(left, right):
    return lax.dot_general(left, right, (((1,), (1,)), ((), ())), preferred_element_type=jnp.float32)


def line(ref):
    return ref[...].reshape(1, ref.shape[0])


def statistics(values):
    center = values - jnp.mean(values, axis=-1, keepdims=True)
    spread = jnp.mean(center * center, axis=-1, keepdims=True)
    scale = lax.rsqrt(spread + EPS)
    return center * scale, scale


def residual_kernel(
    attended_ref, tokens_ref, mine_ref, theirs_ref, bias_ref, gain_ref, shift_ref, middle_ref, normed_ref
):
    width = mine_ref.shape[0]
    rows = mm(attended_ref[:, :width], mine_ref[...]) + mm(attended_ref[:, width:], theirs_ref[...])
    middle = tokens_ref[...].astype(jnp.float32) + rows + line(bias_ref)
    middle_ref[...] = middle
    normal, _ = statistics(middle)
    normed_ref[...] = (normal * line(gain_ref) + line(shift_ref)).astype(jnp.bfloat16)


def own_kernel(tokens_ref, cotangent_ref, gain_ref, shift_ref, weight_ref, bias_ref, blocks_ref, halves_ref):
    half = tokens_ref.shape[0] // 2
    halves_ref[:half, :] = tokens_ref[half:, :]
    halves_ref[half:, :] = cotangent_ref[half:, :]
    normal, _ = statistics(tokens_ref[...].astype(jnp.float32))
    normed = (normal * line(gain_ref) + line(shift_ref)).astype(jnp.bfloat16)
    bias = jnp.concatenate([jnp.zeros_like(line(bias_ref)), line(bias_ref)], axis=1)
    keyval = (mm(normed, weight_ref[...]) + bias).astype(jnp.bfloat16)
    for i in range(blocks_ref.shape[0]):
        blocks_ref[i] = keyval


def query_kernel(
    own_ref, received_ref, gain_ref, shift_ref, mine_ref, theirs_ref, mine_bias_ref, theirs_bias_ref,
    tokens_ref, normed_ref, query_ref,
):
    half, width = received_ref.shape[0] // 2, mine_ref.shape[1]
    tokens_ref[:half, :] = own_ref[:half, :]
    tokens_ref[half:, :] = received_ref[:half, :]
    normal, _ = statistics(tokens_ref[...].astype(jnp.float32))
    normed = (normal * line(gain_ref) + line(shift_ref)).astype(jnp.bfloat16)
    normed_ref[...] = normed
    mine = (mm(normed, mine_ref[...]) + line(mine_bias_ref)).astype(jnp.bfloat16)
    theirs = (mm(normed, theirs_ref[...]) + line(theirs_bias_ref)).astype(jnp.bfloat16)
    query_ref[:, :width] = mine * jnp.bfloat16(0.125)
    query_ref[:, width:] = theirs * jnp.bfloat16(0.125)


def mlp_kernel(
    own_ref, peer_ref, own_grad_ref, peer_grad_ref, expand_ref, bias_ref, contract_ref,
    contract_part_ref, expand_part_ref, bias_part_ref, own_out_ref, peer_out_ref, own_back_ref, peer_back_ref,
    both, turned, grads, acts_all, grad_all,
):
    rows = own_ref.shape[0]
    hidden = expand_ref.shape[1]
    block = hidden // BLOCKS
    both[:rows, :] = own_ref[...]
    both[rows:, :] = peer_ref[...]
    grads[:rows, :] = own_grad_ref[...]
    grads[rows:, :] = peer_grad_ref[...]
    spans = [slice(j * block, (j + 1) * block) for j in range(BLOCKS)]

    def products(cols):
        return mm(both[...], expand_ref[:, cols]), mm_cols(grads[...], contract_ref[cols, :])

    bias = line(bias_ref)

    def activate(cols, inner, acts_grad):
        inner = inner + bias[:, cols]
        square = inner * inner
        tanh = jnp.tanh(inner * (ROOT + ROOT * CUBE * square))
        half = 0.5 + 0.5 * tanh
        acts_all[:, cols] = (inner * half).astype(jnp.bfloat16)
        slope = half + inner * (0.5 - 0.5 * tanh * tanh) * (ROOT + 3.0 * ROOT * CUBE * square)
        grad = (acts_grad * slope).astype(jnp.bfloat16)
        grad_all[:, cols] = grad
        bias_part_ref[:, cols] = jnp.sum(grad.astype(jnp.float32), axis=0, keepdims=True)

    def weights(cols):
        contract_part_ref[cols, :] = mm(acts_all[:, cols].T, grads[...]).astype(jnp.bfloat16)
        expand_part_ref[:, cols] = mm(turned[...], grad_all[:, cols]).astype(jnp.bfloat16)

    turned[...] = both[...].T
    held = products(spans[0])
    for j, cols in enumerate(spans):
        later = products(spans[j + 1]) if j + 1 < BLOCKS else None
        activate(cols, *held)
        held = later
    for cols in spans:
        weights(cols)
    out = mm(acts_all[...], contract_ref[...])
    own_out_ref[...] = out[:rows, :]
    peer_out_ref[...] = out[rows:, :].astype(jnp.bfloat16)
    back = mm_cols(grad_all[...], expand_ref[...])
    own_back_ref[...] = back[:rows, :]
    peer_back_ref[...] = back[rows:, :].astype(jnp.bfloat16)


def widen_kernel(contract_ref, expand_ref, contract_out_ref, expand_out_ref):
    contract_out_ref[...] = contract_ref[...].astype(jnp.float32)
    expand_out_ref[...] = expand_ref[...].astype(jnp.float32)


def residual_back_kernel(
    back_ref, peer_back_ref, grad_ref, middle_ref, gain_ref, mine_ref, theirs_ref,
    middle_grad_ref, low_ref, attended_grad_ref, sums_ref,
):
    width = mine_ref.shape[0]
    back = back_ref[...] + peer_back_ref[...].astype(jnp.float32)
    grad = grad_ref[...].astype(jnp.float32)
    normal, scale = statistics(middle_ref[...])
    weighted = back * line(gain_ref)
    mean = jnp.mean(weighted, axis=-1, keepdims=True)
    along = jnp.mean(weighted * normal, axis=-1, keepdims=True)
    middle_grad = grad + scale * (weighted - mean - normal * along)
    middle_grad_ref[...] = middle_grad
    lowered = middle_grad.astype(jnp.bfloat16)
    low_ref[...] = lowered
    attended_grad_ref[:, :width] = mm_cols(lowered, mine_ref[...]).astype(jnp.bfloat16)
    attended_grad_ref[:, width:] = mm_cols(lowered, theirs_ref[...]).astype(jnp.bfloat16)
    sums_ref[0:1, :] = jnp.sum(middle_grad, axis=0, keepdims=True)
    sums_ref[1:2, :] = jnp.sum(back * normal, axis=0, keepdims=True)
    sums_ref[2:3, :] = jnp.sum(back, axis=0, keepdims=True)
    sums_ref[3:4, :] = jnp.sum(grad, axis=0, keepdims=True)


def query_back_kernel(
    grad_ref, normed_ref, attended_ref, low_ref, mine_ref, theirs_ref,
    normed_grad_ref, mine_part_ref, theirs_part_ref, bias_ref,
):
    width = mine_ref.shape[1]
    normed = normed_ref[...].T
    attended = attended_ref[...].T
    mine, theirs = grad_ref[:, :width], grad_ref[:, width:]
    normed_grad_ref[...] = mm_cols(mine, mine_ref[...]) + mm_cols(theirs, theirs_ref[...])

    def put(ref, *parts):
        place = 0
        for part in parts:
            for col in range(0, part.shape[1], HALF):
                ref[place : place + part.shape[0], :] = part[:, col : col + HALF].astype(ref.dtype)
                place += part.shape[0]

    put(theirs_part_ref, mm(normed, theirs), mm(attended[width:], low_ref[...]))
    put(mine_part_ref, mm(normed, mine), mm(attended[:width], low_ref[...]))
    bias_ref[...] = jnp.sum(grad_ref[...].astype(jnp.float32), axis=0, keepdims=True)


def token_back_kernel(
    arrived_ref, normed_grad_ref, weight_ref, tokens_ref, gain_ref, normed_ref, middle_grad_ref,
    middle_sums_ref, query_bias_ref, expand_bias_ref,
    tokens_grad_ref, half_ref, sent_ref, rows_ref,
):
    grad = arrived_ref[0].astype(jnp.float32)
    for i in range(1, arrived_ref.shape[0]):
        grad = grad + arrived_ref[i].astype(jnp.float32)
    grad = grad.astype(jnp.bfloat16)
    back = normed_grad_ref[...] + mm_cols(grad, weight_ref[...])
    normal, scale = statistics(tokens_ref[...].astype(jnp.float32))
    weighted = back * line(gain_ref)
    mean = jnp.mean(weighted, axis=-1, keepdims=True)
    along = jnp.mean(weighted * normal, axis=-1, keepdims=True)
    tokens_grad = middle_grad_ref[...] + scale * (weighted - mean - normal * along)
    half = half_ref.shape[0]
    tokens_grad_ref[...] = tokens_grad[:half]
    half_ref[...] = tokens_grad[half:].astype(jnp.bfloat16)

    place = 0

    def put(values):
        nonlocal place
        depth = values.shape[0]
        sent_ref[place : place + depth, :] = values.astype(jnp.bfloat16)
        place += depth

    put(mm(normed_ref[...].T, grad))
    vectors = [middle_sums_ref[i : i + 1, :] for i in range(4)]
    vectors += [jnp.sum(back * normal, axis=0, keepdims=True), jnp.sum(back, axis=0, keepdims=True)]
    vectors += [query_bias_ref[...], jnp.sum(grad.astype(jnp.float32), axis=0, keepdims=True), expand_bias_ref[...]]
    rows_ref[...] = jnp.zeros_like(rows_ref)
    row = 0
    for vector in vectors:
        for col in range(0, vector.shape[1], HALF):
            rows_ref[row : row + 1, :] = vector[:, col : col + HALF]
            row += 1
    rows = rows_ref[...]
    high = rows.astype(jnp.bfloat16)
    put(high)
    put(rows - high.astype(jnp.float32))
    sent_ref[place:, :] = jnp.zeros_like(sent_ref[place:, :])


def pack_kernel(win_ref, part_ref, peer_ref, own_ref, first_ref, second_ref, third_ref):
    depth = own_ref.shape[0]
    count = part_ref.shape[0] // depth
    for shift, ref in enumerate((own_ref, first_ref, second_ref, third_ref)):
        to = lax.rem(win_ref[0] + shift, count)
        rows = pl.ds(pl.multiple_of(to * depth, HALF), depth)
        ref[...] = (part_ref[rows, :] + peer_ref[rows, :].astype(jnp.float32)).astype(ref.dtype)


def unpack_kernel(
    win_ref, own_ref, first_ref, second_ref, third_ref, query_ref, out_ref, keyval_ref, rows_ref, weights_ref, rest_ref
):
    pieces_of = (own_ref, first_ref, second_ref, third_ref)
    count = own_ref.shape[0]
    depth = weights_ref.shape[0] // len(pieces_of) // count
    spare = rest_ref.shape[0] // len(pieces_of) // count
    for shift, ref in enumerate(pieces_of):
        start = lax.rem(win_ref[0] + len(pieces_of) - shift, len(pieces_of)) * count
        for i in range(count):
            piece = ref[i].astype(jnp.float32)
            weights_ref[pl.ds(pl.multiple_of((start + i) * depth, 8), depth), :] = piece[:depth]
            rest_ref[pl.ds(pl.multiple_of((start + i) * spare, 8), spare), :] = piece[depth:]
    place = 0
    for ref in (query_ref, out_ref):
        depth = ref.shape[0]
        for col in range(0, ref.shape[1], HALF):
            ref[:, col : col + HALF] = weights_ref[place : place + depth, :]
            place += depth
    place = keyval_ref.shape[0]
    keyval_ref[...] = rest_ref[:place, :]
    depth = rows_ref.shape[0]
    rows_ref[...] = rest_ref[place : place + depth, :] + rest_ref[place + depth : place + 2 * depth, :]


def like(*shape, dtype=jnp.float32):
    return jax.ShapeDtypeStruct(shape, dtype)


def run(kernel, outs, scratch, limit, flops, name, *args):
    return pl.pallas_call(
        kernel,
        out_shape=outs,
        in_specs=[VM] * len(args),
        out_specs=tuple(VM for _ in outs),
        scratch_shapes=scratch,
        compiler_params=pltpu.CompilerParams(vmem_limit_bytes=limit * 2**20),
        cost_estimate=pl.CostEstimate(flops=flops, bytes_accessed=2**20, transcendentals=0),
        name=name,
    )(*args)


def residual(attended, tokens, pair, bias, gain, shift):
    outs = (like(*tokens.shape), like(*tokens.shape, dtype=jnp.bfloat16))
    return run(residual_kernel, outs, [], 12, 10**9, "residual", attended, tokens, *pair, bias, gain, shift)


def own_keyval_blocks(tokens, cotangent, gain, shift, weight, bias, count):
    outs = (
        like(count, tokens.shape[0], weight.shape[1], dtype=jnp.bfloat16),
        like(*tokens.shape, dtype=jnp.bfloat16),
    )
    return run(own_kernel, outs, [], 60, 10**8, "own_keyval", tokens, cotangent, gain, shift, weight, bias)


def query_rows(own, received, gain, shift, pair, biases):
    low16 = like(*own.shape, dtype=jnp.bfloat16)
    outs = (low16, low16, low16)
    return run(
        query_kernel, outs, [], 12, 3 * 10**10, "query_rows", own, received, gain, shift, *pair, *biases
    )


def mlp(own, peer, own_grad, peer_grad, expand, bias, contract):
    rows, features = own.shape
    hidden = expand.shape[1]
    b16 = jnp.bfloat16
    outs = (
        like(hidden, features, dtype=b16),
        like(features, hidden, dtype=b16),
        like(1, hidden),
        like(rows, features),
        like(rows, features, dtype=b16),
        like(rows, features),
        like(rows, features, dtype=b16),
    )
    scratch = [
        pltpu.VMEM((2 * rows, features), b16),
        pltpu.VMEM((features, 2 * rows), b16),
        pltpu.VMEM((2 * rows, features), b16),
        pltpu.VMEM((2 * rows, hidden), b16),
        pltpu.VMEM((2 * rows, hidden), b16),
    ]
    return run(
        mlp_kernel, outs, scratch, 32, 10**10, "mlp", own, peer, own_grad, peer_grad, expand, bias, contract
    )


def widen(contract, expand):
    steps = 2

    def spec(array):
        return pl.BlockSpec((array.shape[0] // steps, array.shape[1]), lambda i: (i, 0))

    return pl.pallas_call(
        widen_kernel,
        grid=(steps,),
        out_shape=(like(*contract.shape), like(*expand.shape)),
        in_specs=[spec(contract), spec(expand)],
        out_specs=(spec(contract), spec(expand)),
        compiler_params=pltpu.CompilerParams(vmem_limit_bytes=60 * 2**20),
        name="widen",
    )(contract, expand)


def residual_back(back, peer_back, grad, middle, gain, pair):
    rows, features = grad.shape
    b16 = jnp.bfloat16
    outs = (like(rows, features), like(rows, features, dtype=b16), like(rows, features, dtype=b16), like(8, features))
    return run(
        residual_back_kernel, outs, [], 12, 10**9, "residual_back", back, peer_back, grad, middle, gain, *pair
    )


SWAP = ((0, 1), (1, 0))


def query_back(grad, normed, attended, lowered, pair):
    rows, features = grad.shape
    width = pair[0].shape[1]
    b16 = jnp.bfloat16
    outs = (
        like(rows, features),
        like(2 * features * width // HALF, HALF),
        like(2 * features * width // HALF, HALF, dtype=b16),
        like(1, features),
    )
    return run(query_back_kernel, outs, [], 16, 10**10, "query_back", grad, normed, attended, lowered, *pair)


def token_back(ranks, arrived, normed_grad, weight, tokens, gain, normed, middle_grad, vectors):
    count, features = normed.shape
    depth = weight.shape[0] + 2 * VECTOR_ROWS
    depth += -depth % (16 * ranks)
    outs = (
        like(count // 2, features),
        like(count // 2, features, dtype=jnp.bfloat16),
        like(depth, HALF, dtype=jnp.bfloat16),
    )
    return run(
        token_back_kernel, outs, [pltpu.VMEM((VECTOR_ROWS, HALF), jnp.float32)], 12, 10**9, "token_back",
        arrived, normed_grad, weight, tokens, gain, normed, middle_grad, *vectors,
    )


def pack(win, part, peer):
    depth = part.shape[0] // 4
    outs = (like(depth, HALF), *(like(depth, HALF, dtype=jnp.bfloat16) for _ in range(3)))
    return pl.pallas_call(
        pack_kernel,
        out_shape=outs,
        in_specs=[SM] + [VM] * 2,
        out_specs=(VM,) * 4,
        compiler_params=pltpu.CompilerParams(vmem_limit_bytes=16 * 2**20),
        name="pack",
    )(win, part, peer)


def unpack(win, parts, rest_rows, query_shape, out_shape, keyval_shape):
    outs = (like(*query_shape), like(*out_shape), like(*keyval_shape), like(VECTOR_ROWS, HALF))
    weight_rows = (math.prod(query_shape) + math.prod(out_shape)) // HALF
    return pl.pallas_call(
        unpack_kernel,
        out_shape=outs,
        in_specs=[SM] + [VM] * 4,
        out_specs=(VM,) * 4,
        scratch_shapes=[pltpu.VMEM((weight_rows, HALF), jnp.float32), pltpu.VMEM((rest_rows, HALF), jnp.float32)],
        compiler_params=pltpu.CompilerParams(vmem_limit_bytes=20 * 2**20),
        name="unpack",
    )(win, *parts)


def low(value):
    return value.astype(jnp.bfloat16)


def swapped(value):
    return lax.ppermute(value, "heads", SWAP)


def opposite(value):
    count = lax.axis_size(("seq", "heads"))
    return lax.ppermute(value, ("seq", "heads"), [(i, count - 1 - i) for i in range(count)])


def exchanged(value):
    half = value.shape[0] // 2
    return jnp.concatenate([value[:half], opposite(value[half:])], axis=0)


def spread_out(blocks, axis):
    return lax.all_to_all(blocks, axis, split_axis=0, concat_axis=0, tiled=True)


def copies(value, axis):
    return spread_out(jnp.broadcast_to(value[None], (lax.axis_size(axis), *value.shape)), axis)


def per_device(
    tokens,
    first_gain,
    first_shift,
    query_weight,
    query_bias,
    keyval_weight,
    value_bias,
    out_weight,
    out_bias,
    second_gain,
    second_shift,
    expand_weight,
    expand_bias,
    contract_weight,
    contract_bias,
    cotangent,
    lengths,
):
    f32 = jnp.float32
    place = lax.axis_index(("seq", "heads"))
    places = place.astype(jnp.int32).reshape(1)
    ranks = lax.axis_size(("win", "seq"))

    own_blocks, halves = own_keyval_blocks(
        tokens[0], cotangent[0], first_gain, first_shift, keyval_weight, value_bias, lax.axis_size("seq")
    )
    received = opposite(halves)
    grad_low = jnp.concatenate([cotangent[0, :HALF], received[HALF:]])
    own_blocks = spread_out(own_blocks, "seq")
    query_pair = (query_weight, swapped(query_weight))
    out_pair = (out_weight, swapped(out_weight))
    query_biases = (query_bias, swapped(query_bias))

    bounds = jnp.cumsum(lengths[0])
    first = jnp.stack(positions(place.astype(jnp.int32)))
    position = first[:, None] + jnp.arange(HALF, dtype=jnp.int32)[None, :]
    starts = jnp.max(jnp.where(bounds[None, None, :] <= position[:, :, None], bounds, 0), axis=2)
    starts = starts.astype(jnp.int32).reshape(2, 1, HALF)

    tokens_low, normed_low, query8 = query_rows(
        tokens[0], received, first_gain, first_shift, query_pair, query_biases
    )
    own_blocks, query8 = lax.optimization_barrier((own_blocks, query8))
    peer_blocks = swapped(own_blocks)
    attended, out, logs = attend(places, query8, own_blocks, peer_blocks, starts)
    width = query_bias.shape[0]
    middle, normed2_low = residual(attended, tokens_low, out_pair, out_bias, second_gain, second_shift)
    peer_grad_low = swapped(grad_low)
    contract_part, expand_part, expand_bias_part, out_rows, peer_out, back_rows, peer_back = mlp(
        normed2_low, swapped(normed2_low), grad_low, peer_grad_low, expand_weight, expand_bias, contract_weight
    )
    contract_total, expand_total = lax.psum((contract_part, expand_part), ("win", "seq"))
    middle_grad, middle_low, attended_grad, middle_sums = residual_back(
        back_rows, swapped(peer_back), grad_low, middle, second_gain, out_pair
    )

    def rest():
        query_grad, mine, theirs = attend_back(
            places, query8, own_blocks, peer_blocks, starts, attended_grad, out, logs
        )
        mlp_out = out_rows + swapped(peer_out).astype(f32)
        block_out = exchanged(low(middle + mlp_out + contract_bias))
        pair_grad = low(mine.astype(f32) + swapped(theirs).astype(f32))
        arrived = spread_out(pair_grad, "seq")
        from_query, weights_part, weights_sent, query_bias_part = query_back(
            query_grad, normed_low, attended, middle_low, query_pair
        )
        core = lax.axis_index("heads")
        turned_bias = jnp.concatenate([query_bias_part[:, width:], query_bias_part[:, :width]], axis=1)
        query_bias_part = jnp.where(core == 0, query_bias_part, turned_bias)
        wins, seqs = lax.axis_size("win"), lax.axis_size("seq")
        win = lax.axis_index("win").astype(jnp.int32)
        kept, *given = pack(win.reshape(1), weights_part, swapped(weights_sent))
        taken = [
            lax.ppermute(given[shift - 1], "win", [(i, (i + shift) % wins) for i in range(wins)]) for shift in (2, 1, 3)
        ]
        tokens_grad, half, sent = token_back(
            ranks, arrived, from_query, keyval_weight, tokens_low, first_gain, normed_low, middle_grad,
            (middle_sums, query_bias_part, expand_bias_part),
        )
        tokens_grad = jnp.concatenate([tokens_grad, opposite(half).astype(f32)], axis=0)

        sent, taken = lax.optimization_barrier((sent, taken))
        rest = spread_out(sent.reshape(wins, -1, HALF), "win")
        rest = low(jnp.sum(rest.astype(f32), axis=0)).reshape(seqs, -1, HALF)
        weights = low(kept + sum(t.astype(f32) for t in taken)).reshape(seqs, -1, HALF)
        depth = weights.shape[1]
        summed = jnp.sum(spread_out(jnp.concatenate([weights, rest], axis=1), "seq").astype(f32), axis=0)
        rest = summed[depth:]
        features = first_gain.shape[0]
        row = lax.axis_index(("win", "seq")) * rest.shape[0] + jnp.arange(rest.shape[0])[:, None]
        vectors = keyval_weight.shape[0]
        common = 7 * features // HALF + 1
        shared = row < vectors + common
        shared = shared | ((row >= vectors + VECTOR_ROWS) & (row < vectors + VECTOR_ROWS + common))
        rest = rest + jnp.where(shared, swapped(rest), 0.0)
        full = low(jnp.concatenate([summed[:depth], rest]))
        full = copies(full, "seq")
        others = {
            shift: lax.ppermute(full, "win", [(i, (i + shift) % wins) for i in range(wins)]) for shift in (2, 1, 3)
        }
        query_total, out_total, keyval_total, summed_rows = unpack(
            win.reshape(1),
            (full, others[1], others[2], others[3]),
            sent.shape[0],
            query_weight.shape,
            out_weight.shape,
            keyval_weight.shape,
        )
        summed_rows = summed_rows.reshape(-1)
        sizes = [features] * 7 + [HALF, expand_bias.shape[0]]
        totals = []
        for size in sizes:
            totals.append(summed_rows[:size])
            summed_rows = summed_rows[size:]
        query_bias_total = jnp.where(core == 0, totals[6][:width], totals[6][width:])
        return (
            block_out[None],
            tokens_grad[None],
            totals[4],
            totals[5],
            query_total,
            query_bias_total,
            keyval_total,
            totals[7][DH:],
            out_total,
            totals[0],
            totals[1],
            totals[2],
            totals[8],
            totals[3],
        )

    shapes = jax.eval_shape(rest)

    def nothing():
        return jax.tree.map(lambda s: jnp.zeros(s.shape, s.dtype), shapes)

    outs = lax.cond(lengths[0, 0] > 0, rest, nothing)
    contract_total, expand_total = widen(contract_total, expand_total)
    return (
        *outs[:12],
        expand_total,
        outs[12],
        contract_total,
        outs[13],
    )


def solution(mesh):
    return jax.shard_map(
        per_device,
        mesh=mesh,
        in_specs=(
            P("win", ("seq", "heads"), None),
            P(),
            P(),
            P(None, "heads"),
            P("heads"),
            P(),
            P(),
            P("heads", None),
            P(),
            P(),
            P(),
            P(None, "heads"),
            P("heads"),
            P("heads", None),
            P(),
            P("win", ("seq", "heads"), None),
            P("win", None),
        ),
        out_specs=(
            P("win", ("seq", "heads"), None),
            P("win", ("seq", "heads"), None),
            P(),
            P(),
            P(None, "heads"),
            P("heads"),
            P(),
            P(),
            P("heads", None),
            P(),
            P(),
            P(),
            P(None, "heads"),
            P("heads"),
            P("heads", None),
            P(),
        ),
        check_vma=False,
    )
```

```python
import math
import jax
import jax.numpy as jnp
from jax import lax
from jax.experimental import pallas as pl
from jax.experimental.pallas import tpu as pltpu
from jax.sharding import PartitionSpec as P

DH = 64
NEG = -1e30
TILE = 256
LANES = 256
HALF = 128


def mm(left, right):
    return lax.dot_general(left, right, (((1,), (0,)), ((), ())), preferred_element_type=jnp.float32)


def pieces(row, width):
    high = row.astype(jnp.bfloat16).astype(jnp.float32)
    rest = row - high
    mid = rest.astype(jnp.bfloat16).astype(jnp.float32)
    low = rest - mid
    which = lax.broadcasted_iota(jnp.int32, (16, width), 0)
    block = jnp.where(which == 0, -high, jnp.where(which == 1, -mid, jnp.where(which == 2, -low, 0.0)))
    return block.astype(jnp.bfloat16)


def with_ones(part):
    lane = lax.broadcasted_iota(jnp.int32, (part.shape[0], HALF), 1)
    wide = jnp.concatenate([part, jnp.zeros_like(part)], axis=1)
    return jnp.where((lane >= DH) & (lane < DH + 3), jnp.ones_like(wide), wide)


def mask_of(tile, chunk_pos, starts):
    key = tile * TILE + lax.broadcasted_iota(jnp.int32, (TILE, HALF), 0)
    query = chunk_pos + lax.broadcasted_iota(jnp.int32, (TILE, HALF), 1)
    mask = jnp.where((key <= query) & (key >= starts), 0.0, NEG)
    return jnp.concatenate([mask, mask], axis=1)


def in_groups(first, last, step, sizes):
    at = first
    for size in sizes:
        count = lax.div(jnp.maximum(last - at, 0), size)

        def group(i, _, at=at, size=size):
            step(at + size * i, size)
            return 0

        lax.fori_loop(0, count, group, 0)
        at = at + size * count


def block_of(own_ref, peer_ref, place, tile):
    pair = lax.div(tile, 2)
    own = lax.rem(tile, 2) == lax.rem(place, 2)
    return jnp.where(own, own_ref[pair], peer_ref[pair])


def positions(place):
    return (place * 2 * HALF, 63 * HALF - place * 2 * HALF)


def forward_kernel(place_ref, query_ref, own_ref, peer_ref, starts_ref, attended_ref, out_ref, log_ref, kx, vt, qt, acc, high):
    subs = qt.shape[2] // LANES
    chunk_pos = positions(place_ref[0])

    def prepare(tile, _):
        rows = pl.ds(pl.multiple_of(tile * TILE, TILE), TILE)
        block = block_of(own_ref, peer_ref, place_ref[0], tile)
        kx[rows, :] = with_ones(block[:, :DH])
        vt[:DH, rows] = block[:, DH:].T
        return 0

    lax.fori_loop(0, 2 * own_ref.shape[0], prepare, 0, unroll=4)
    vt[DH:, :] = jnp.ones_like(vt[DH:, :])

    def chunk(c, _):
        first = jnp.where(c == 0, chunk_pos[0], chunk_pos[1])
        diag = lax.div(first, TILE)
        lines = pl.ds(pl.multiple_of(c * HALF, HALF), HALF)
        starts = starts_ref[c]
        wide = jnp.concatenate([starts, starts], axis=1)
        spans = [slice(s * LANES, (s + 1) * LANES) for s in range(subs)]
        for s, cols in enumerate(spans):
            pair = query_ref[lines, s * 2 * DH : (s + 1) * 2 * DH].T
            qt[c, :DH, cols] = jnp.concatenate([pair[:DH], pair[DH:]], axis=1)
            qt[c, DH:, cols] = jnp.zeros_like(qt[c, DH:, cols])

        def rows_of(tile, count=1):
            return pl.ds(pl.multiple_of(tile * TILE, TILE), count * TILE)

        def scores(tile, count=1):
            return [mm(kx[rows_of(tile, count), :], qt[c, :, cols]) for cols in spans]

        def gather(tile, probs, fresh=False, count=1):
            rows = rows_of(tile, count)
            for cols, prob in zip(spans, probs):
                part = mm(vt[:, rows], prob)
                if fresh:
                    acc[c, :, cols] = part
                else:
                    acc[c, :, cols] += part

        def exps(values):
            return [jnp.exp(v).astype(jnp.bfloat16) for v in values]

        def set_shift(used):
            for cols in spans:
                if used:
                    block = pieces(jnp.where(wide <= TILE, high[c, :1, cols], -NEG), LANES)
                else:
                    block = jnp.zeros((16, LANES), jnp.bfloat16)
                qt[c, DH : DH + 16, cols] = block

        def sweep(again):
            mask = mask_of(diag, first, starts)
            values = [v + mask for v in scores(diag)]
            if again:
                tops = [high[c, :1, cols] for cols in spans]
            else:
                tops = [jnp.max(v, axis=0, keepdims=True) for v in values]
                for cols, top in zip(spans, tops):
                    high[c, :1, cols] = top
            gather(diag, exps([v - top for v, top in zip(values, tops)]), fresh=True)

            @pl.when(diag > 0)
            def _():
                set_shift(True)
                mask = mask_of(0, first, starts)
                gather(0, exps([v + mask for v in scores(0)]))
                in_groups(
                    1, diag, lambda tile, count: gather(tile, exps(scores(tile, count)), count=count), (4, 2, 1)
                )

        sweep(False)

        @pl.when(jnp.logical_not(jnp.max(acc[c, DH : DH + 1, :]) < 1e30))
        def _():
            set_shift(False)

            def raise_to(values):
                for cols, v in zip(spans, values):
                    high[c, :1, cols] = jnp.maximum(high[c, :1, cols], jnp.max(v, axis=0, keepdims=True))

            @pl.when(diag > 0)
            def _():
                mask = mask_of(0, first, starts)
                raise_to([v + mask for v in scores(0)])

                def step(tile, _):
                    raise_to([jnp.where(wide <= TILE, v, NEG) for v in scores(tile)])
                    return 0

                lax.fori_loop(1, diag, step, 0)

            sweep(True)

        for s, cols in enumerate(spans):
            total = acc[c, DH : DH + 1, cols]
            result = acc[c, :DH, cols] / total
            out_ref[c, :, cols] = result
            log_ref[c, :, cols] = high[c, :1, cols] + jnp.log(total)
            stacked = jnp.concatenate([result[:, :HALF], result[:, HALF:]], axis=0)
            attended_ref[lines, s * 2 * DH : (s + 1) * 2 * DH] = stacked.astype(jnp.bfloat16).T
        return 0

    lax.fori_loop(0, 2, chunk, 0)


def backward_kernel(
    place_ref, query_ref, own_ref, peer_ref, starts_ref, grad_ref, out_ref, log_ref,
    dquery_ref, mine_ref, theirs_ref, kx, vx, kt, qt, gt, wq, wg, dq, dkv,
):
    subs = qt.shape[2] // LANES
    place = place_ref[0]
    chunk_pos = positions(place)

    def prepare(tile, _):
        rows = pl.ds(pl.multiple_of(tile * TILE, TILE), TILE)
        block = block_of(own_ref, peer_ref, place, tile)
        kx[rows, :] = with_ones(block[:, :DH])
        vx[rows, :] = with_ones(block[:, DH:])
        kt[:, rows] = block[:, :DH].T
        return 0

    lax.fori_loop(0, 2 * own_ref.shape[0], prepare, 0, unroll=4)
    dkv[...] = jnp.zeros_like(dkv)

    def chunk(c, _):
        first = jnp.where(c == 0, chunk_pos[0], chunk_pos[1])
        diag = lax.div(first, TILE)
        lines = pl.ds(pl.multiple_of(c * HALF, HALF), HALF)
        starts = jnp.concatenate([starts_ref[c], starts_ref[c]], axis=1)
        empty = jnp.zeros((HALF, DH), jnp.bfloat16)
        for s in range(subs):
            cols = slice(s * LANES, (s + 1) * LANES)
            q2 = query_ref[lines, s * 2 * DH : (s + 1) * 2 * DH]
            g2 = grad_ref[lines, s * 2 * DH : (s + 1) * 2 * DH]
            q2t, g2t = q2.T, g2.T
            qt[c, :DH, cols] = jnp.concatenate([q2t[:DH], q2t[DH:]], axis=1)
            grad_t = jnp.concatenate([g2t[:DH], g2t[DH:]], axis=1)
            gt[c, :DH, cols] = grad_t
            qt[c, DH:, cols] = jnp.zeros_like(qt[c, DH:, cols])
            gt[c, DH + 16 :, cols] = jnp.zeros_like(gt[c, DH + 16 :, cols])
            delta = jnp.sum(grad_t.astype(jnp.float32) * out_ref[c, :, cols], axis=0, keepdims=True)
            gt[c, DH : DH + 16, cols] = pieces(delta, LANES)
            for h in range(2):
                rows = slice(h * HALF, (h + 1) * HALF)
                wq[c, s, rows, :] = jnp.concatenate([q2[:, h * DH : (h + 1) * DH], empty], axis=1)
                wg[c, s, rows, :] = jnp.concatenate([empty, g2[:, h * DH : (h + 1) * DH]], axis=1)

        def add(tile, mask=None, logs=None, fresh=False, count=1):
            rows = pl.ds(pl.multiple_of(tile * TILE, TILE), count * TILE)
            total = jnp.zeros((count * TILE, 2 * DH), jnp.float32)
            for base in range(0, subs, 3):
                group = range(base, base + 3)
                spans = [slice(s * LANES, (s + 1) * LANES) for s in group]
                sts = [mm(kx[rows, :], qt[c, :, cols]) for cols in spans]
                dps = [mm(vx[rows, :], gt[c, :, cols]) for cols in spans]
                if mask is not None:
                    sts = [st + mask for st in sts]
                if logs is not None:
                    sts = [st - log_ref[c, :, cols] for st, cols in zip(sts, spans)]
                probs = [jnp.exp(st) for st in sts]
                dss = [(p * dp).astype(jnp.bfloat16) for p, dp in zip(probs, dps)]
                lows = [p.astype(jnp.bfloat16) for p in probs]
                for s, ds, low in zip(group, dss, lows):
                    total = total + (mm(ds, wq[c, s]) + mm(low, wg[c, s]))
                for cols, ds in zip(spans, dss):
                    part = mm(kt[:, rows], ds)
                    if fresh:
                        dq[c, :, cols] = part
                    else:
                        dq[c, :, cols] += part
            dkv[rows, :] += total

        add(diag, mask_of(diag, first, starts_ref[c]), log_ref, fresh=True)

        @pl.when(diag > 0)
        def _():
            for s in range(subs):
                cols = slice(s * LANES, (s + 1) * LANES)
                qt[c, DH : DH + 16, cols] = pieces(jnp.where(starts <= TILE, log_ref[c, :, cols], -NEG), LANES)
            add(0, mask_of(0, first, starts_ref[c]))

            in_groups(1, diag, lambda tile, count: add(tile, count=count), (2, 1))

        for s in range(subs):
            cols = slice(s * LANES, (s + 1) * LANES)
            result = dq[c, :, cols] * 0.125
            stacked = jnp.concatenate([result[:, :HALF], result[:, HALF:]], axis=0)
            dquery_ref[lines, s * 2 * DH : (s + 1) * 2 * DH] = stacked.astype(jnp.bfloat16).T
        return 0

    lax.fori_loop(0, 2, chunk, 0)

    core = lax.rem(place, 2)

    def give(pair, _):
        for ref, owner in ((mine_ref, 2 * pair + core), (theirs_ref, 2 * pair + 1 - core)):
            for c, pos in enumerate(positions(owner)):
                rows = pl.ds(pl.multiple_of(pos, HALF), HALF)
                ref[pair, c * HALF : (c + 1) * HALF, :] = dkv[rows, :].astype(jnp.bfloat16)
        return 0

    lax.fori_loop(0, mine_ref.shape[0], give, 0)


VM = pl.BlockSpec(memory_space=pltpu.VMEM)
SM = pl.BlockSpec(memory_space=pltpu.SMEM)


def attend(place, query8, own, peer, starts):
    rows, width = query8.shape
    window = 2 * own.shape[0] * own.shape[1]
    lanes = (width // DH) * HALF
    return pl.pallas_call(
        forward_kernel,
        out_shape=(
            jax.ShapeDtypeStruct((rows, width), jnp.bfloat16),
            jax.ShapeDtypeStruct((2, DH, lanes), jnp.float32),
            jax.ShapeDtypeStruct((2, 1, lanes), jnp.float32),
        ),
        in_specs=[SM] + [VM] * 4,
        out_specs=(VM, VM, VM),
        scratch_shapes=[
            pltpu.VMEM((window, HALF), jnp.bfloat16),
            pltpu.VMEM((DH + 16, window), jnp.bfloat16),
            pltpu.VMEM((2, HALF, lanes), jnp.bfloat16),
            pltpu.VMEM((2, DH + 16, lanes), jnp.float32),
            pltpu.VMEM((2, 8, lanes), jnp.float32),
        ],
        compiler_params=pltpu.CompilerParams(vmem_limit_bytes=28 * 2**20),
        cost_estimate=pl.CostEstimate(flops=25 * 10**9, bytes_accessed=8 * 2**20, transcendentals=13 * 10**6),
        name="attend",
    )(place, query8, own, peer, starts)


def attend_back(place, query8, own, peer, starts, grad, out, logs):
    rows, width = query8.shape
    window = 2 * own.shape[0] * own.shape[1]
    lanes = (width // DH) * HALF
    subs = lanes // LANES
    return pl.pallas_call(
        backward_kernel,
        out_shape=(
            jax.ShapeDtypeStruct((rows, width), jnp.bfloat16),
            jax.ShapeDtypeStruct((window // (4 * HALF), 2 * HALF, 2 * DH), jnp.bfloat16),
            jax.ShapeDtypeStruct((window // (4 * HALF), 2 * HALF, 2 * DH), jnp.bfloat16),
        ),
        in_specs=[SM] + [VM] * 7,
        out_specs=(VM, VM, VM),
        scratch_shapes=[
            pltpu.VMEM((window, HALF), jnp.bfloat16),
            pltpu.VMEM((window, HALF), jnp.bfloat16),
            pltpu.VMEM((DH, window), jnp.bfloat16),
            pltpu.VMEM((2, HALF, lanes), jnp.bfloat16),
            pltpu.VMEM((2, HALF, lanes), jnp.bfloat16),
            pltpu.VMEM((2, subs, LANES, HALF), jnp.bfloat16),
            pltpu.VMEM((2, subs, LANES, HALF), jnp.bfloat16),
            pltpu.VMEM((2, DH, lanes), jnp.float32),
            pltpu.VMEM((window, HALF), jnp.float32),
        ],
        compiler_params=pltpu.CompilerParams(vmem_limit_bytes=26 * 2**20),
        cost_estimate=pl.CostEstimate(flops=45 * 10**9, bytes_accessed=12 * 2**20, transcendentals=13 * 10**6),
        name="attend_back",
    )(place, query8, own, peer, starts, grad, out, logs)


EPS = 1e-05
CUBE = 0.044715
VECTOR_ROWS = 64
BLOCKS = 6
ROOT = math.sqrt(2.0 / math.pi)


def mm_cols(left, right):
    return lax.dot_general(left, right, (((1,), (1,)), ((), ())), preferred_element_type=jnp.float32)


def line(ref):
    return ref[...].reshape(1, ref.shape[0])


def statistics(values):
    center = values - jnp.mean(values, axis=-1, keepdims=True)
    spread = jnp.mean(center * center, axis=-1, keepdims=True)
    scale = lax.rsqrt(spread + EPS)
    return center * scale, scale


def residual_kernel(
    attended_ref, tokens_ref, mine_ref, theirs_ref, bias_ref, gain_ref, shift_ref, middle_ref, normed_ref
):
    width = mine_ref.shape[0]
    rows = mm(attended_ref[:, :width], mine_ref[...]) + mm(attended_ref[:, width:], theirs_ref[...])
    middle = tokens_ref[...].astype(jnp.float32) + rows + line(bias_ref)
    middle_ref[...] = middle
    normal, _ = statistics(middle)
    normed_ref[...] = (normal * line(gain_ref) + line(shift_ref)).astype(jnp.bfloat16)


def own_kernel(tokens_ref, cotangent_ref, gain_ref, shift_ref, weight_ref, bias_ref, blocks_ref, halves_ref):
    half = tokens_ref.shape[0] // 2
    halves_ref[:half, :] = tokens_ref[half:, :]
    halves_ref[half:, :] = cotangent_ref[half:, :]
    normal, _ = statistics(tokens_ref[...].astype(jnp.float32))
    normed = (normal * line(gain_ref) + line(shift_ref)).astype(jnp.bfloat16)
    bias = jnp.concatenate([jnp.zeros_like(line(bias_ref)), line(bias_ref)], axis=1)
    keyval = (mm(normed, weight_ref[...]) + bias).astype(jnp.bfloat16)
    for i in range(blocks_ref.shape[0]):
        blocks_ref[i] = keyval


def query_kernel(
    own_ref, received_ref, gain_ref, shift_ref, mine_ref, theirs_ref, mine_bias_ref, theirs_bias_ref,
    tokens_ref, normed_ref, query_ref,
):
    half, width = received_ref.shape[0] // 2, mine_ref.shape[1]
    tokens_ref[:half, :] = own_ref[:half, :]
    tokens_ref[half:, :] = received_ref[:half, :]
    normal, _ = statistics(tokens_ref[...].astype(jnp.float32))
    normed = (normal * line(gain_ref) + line(shift_ref)).astype(jnp.bfloat16)
    normed_ref[...] = normed
    mine = (mm(normed, mine_ref[...]) + line(mine_bias_ref)).astype(jnp.bfloat16)
    theirs = (mm(normed, theirs_ref[...]) + line(theirs_bias_ref)).astype(jnp.bfloat16)
    query_ref[:, :width] = mine * jnp.bfloat16(0.125)
    query_ref[:, width:] = theirs * jnp.bfloat16(0.125)


def mlp_kernel(
    own_ref, peer_ref, own_grad_ref, peer_grad_ref, expand_ref, bias_ref, contract_ref,
    contract_part_ref, expand_part_ref, bias_part_ref, own_out_ref, peer_out_ref, own_back_ref, peer_back_ref,
    both, turned, grads, acts_all, grad_all,
):
    rows = own_ref.shape[0]
    hidden = expand_ref.shape[1]
    block = hidden // BLOCKS
    both[:rows, :] = own_ref[...]
    both[rows:, :] = peer_ref[...]
    grads[:rows, :] = own_grad_ref[...]
    grads[rows:, :] = peer_grad_ref[...]
    spans = [slice(j * block, (j + 1) * block) for j in range(BLOCKS)]

    def products(cols):
        return mm(both[...], expand_ref[:, cols]), mm_cols(grads[...], contract_ref[cols, :])

    bias = line(bias_ref)

    def activate(cols, inner, acts_grad):
        inner = inner + bias[:, cols]
        square = inner * inner
        tanh = jnp.tanh(inner * (ROOT + ROOT * CUBE * square))
        half = 0.5 + 0.5 * tanh
        acts_all[:, cols] = (inner * half).astype(jnp.bfloat16)
        slope = half + inner * (0.5 - 0.5 * tanh * tanh) * (ROOT + 3.0 * ROOT * CUBE * square)
        grad = (acts_grad * slope).astype(jnp.bfloat16)
        grad_all[:, cols] = grad
        bias_part_ref[:, cols] = jnp.sum(grad.astype(jnp.float32), axis=0, keepdims=True)

    def weights(cols):
        contract_part_ref[cols, :] = mm(acts_all[:, cols].T, grads[...]).astype(jnp.bfloat16)
        expand_part_ref[:, cols] = mm(turned[...], grad_all[:, cols]).astype(jnp.bfloat16)

    turned[...] = both[...].T
    held = products(spans[0])
    for j, cols in enumerate(spans):
        later = products(spans[j + 1]) if j + 1 < BLOCKS else None
        activate(cols, *held)
        held = later
    for cols in spans:
        weights(cols)
    out = mm(acts_all[...], contract_ref[...])
    own_out_ref[...] = out[:rows, :]
    peer_out_ref[...] = out[rows:, :].astype(jnp.bfloat16)
    back = mm_cols(grad_all[...], expand_ref[...])
    own_back_ref[...] = back[:rows, :]
    peer_back_ref[...] = back[rows:, :].astype(jnp.bfloat16)


def widen_kernel(contract_ref, expand_ref, contract_out_ref, expand_out_ref):
    contract_out_ref[...] = contract_ref[...].astype(jnp.float32)
    expand_out_ref[...] = expand_ref[...].astype(jnp.float32)


def residual_back_kernel(
    back_ref, peer_back_ref, grad_ref, middle_ref, gain_ref, mine_ref, theirs_ref,
    middle_grad_ref, low_ref, attended_grad_ref, sums_ref,
):
    width = mine_ref.shape[0]
    back = back_ref[...] + peer_back_ref[...].astype(jnp.float32)
    grad = grad_ref[...].astype(jnp.float32)
    normal, scale = statistics(middle_ref[...])
    weighted = back * line(gain_ref)
    mean = jnp.mean(weighted, axis=-1, keepdims=True)
    along = jnp.mean(weighted * normal, axis=-1, keepdims=True)
    middle_grad = grad + scale * (weighted - mean - normal * along)
    middle_grad_ref[...] = middle_grad
    lowered = middle_grad.astype(jnp.bfloat16)
    low_ref[...] = lowered
    attended_grad_ref[:, :width] = mm_cols(lowered, mine_ref[...]).astype(jnp.bfloat16)
    attended_grad_ref[:, width:] = mm_cols(lowered, theirs_ref[...]).astype(jnp.bfloat16)
    sums_ref[0:1, :] = jnp.sum(middle_grad, axis=0, keepdims=True)
    sums_ref[1:2, :] = jnp.sum(back * normal, axis=0, keepdims=True)
    sums_ref[2:3, :] = jnp.sum(back, axis=0, keepdims=True)
    sums_ref[3:4, :] = jnp.sum(grad, axis=0, keepdims=True)


def query_back_kernel(
    grad_ref, normed_ref, attended_ref, low_ref, mine_ref, theirs_ref,
    normed_grad_ref, mine_part_ref, theirs_part_ref, bias_ref,
):
    width = mine_ref.shape[1]
    normed = normed_ref[...].T
    attended = attended_ref[...].T
    mine, theirs = grad_ref[:, :width], grad_ref[:, width:]
    normed_grad_ref[...] = mm_cols(mine, mine_ref[...]) + mm_cols(theirs, theirs_ref[...])

    def put(ref, *parts):
        place = 0
        for part in parts:
            for col in range(0, part.shape[1], HALF):
                ref[place : place + part.shape[0], :] = part[:, col : col + HALF].astype(ref.dtype)
                place += part.shape[0]

    put(theirs_part_ref, mm(normed, theirs), mm(attended[width:], low_ref[...]))
    put(mine_part_ref, mm(normed, mine), mm(attended[:width], low_ref[...]))
    bias_ref[...] = jnp.sum(grad_ref[...].astype(jnp.float32), axis=0, keepdims=True)


def token_back_kernel(
    arrived_ref, normed_grad_ref, weight_ref, tokens_ref, gain_ref, normed_ref, middle_grad_ref,
    middle_sums_ref, query_bias_ref, expand_bias_ref,
    tokens_grad_ref, half_ref, sent_ref, rows_ref,
):
    grad = arrived_ref[0].astype(jnp.float32)
    for i in range(1, arrived_ref.shape[0]):
        grad = grad + arrived_ref[i].astype(jnp.float32)
    grad = grad.astype(jnp.bfloat16)
    back = normed_grad_ref[...] + mm_cols(grad, weight_ref[...])
    normal, scale = statistics(tokens_ref[...].astype(jnp.float32))
    weighted = back * line(gain_ref)
    mean = jnp.mean(weighted, axis=-1, keepdims=True)
    along = jnp.mean(weighted * normal, axis=-1, keepdims=True)
    tokens_grad = middle_grad_ref[...] + scale * (weighted - mean - normal * along)
    half = half_ref.shape[0]
    tokens_grad_ref[...] = tokens_grad[:half]
    half_ref[...] = tokens_grad[half:].astype(jnp.bfloat16)

    place = 0

    def put(values):
        nonlocal place
        depth = values.shape[0]
        sent_ref[place : place + depth, :] = values.astype(jnp.bfloat16)
        place += depth

    put(mm(normed_ref[...].T, grad))
    vectors = [middle_sums_ref[i : i + 1, :] for i in range(4)]
    vectors += [jnp.sum(back * normal, axis=0, keepdims=True), jnp.sum(back, axis=0, keepdims=True)]
    vectors += [query_bias_ref[...], jnp.sum(grad.astype(jnp.float32), axis=0, keepdims=True), expand_bias_ref[...]]
    rows_ref[...] = jnp.zeros_like(rows_ref)
    row = 0
    for vector in vectors:
        for col in range(0, vector.shape[1], HALF):
            rows_ref[row : row + 1, :] = vector[:, col : col + HALF]
            row += 1
    rows = rows_ref[...]
    high = rows.astype(jnp.bfloat16)
    put(high)
    put(rows - high.astype(jnp.float32))
    sent_ref[place:, :] = jnp.zeros_like(sent_ref[place:, :])


def pack_kernel(win_ref, part_ref, peer_ref, own_ref, first_ref, second_ref, third_ref):
    depth = own_ref.shape[0]
    count = part_ref.shape[0] // depth
    for shift, ref in enumerate((own_ref, first_ref, second_ref, third_ref)):
        to = lax.rem(win_ref[0] + shift, count)
        rows = pl.ds(pl.multiple_of(to * depth, HALF), depth)
        ref[...] = (part_ref[rows, :] + peer_ref[rows, :].astype(jnp.float32)).astype(ref.dtype)


def unpack_kernel(
    win_ref, own_ref, first_ref, second_ref, third_ref, query_ref, out_ref, keyval_ref, rows_ref, weights_ref, rest_ref
):
    pieces_of = (own_ref, first_ref, second_ref, third_ref)
    count = own_ref.shape[0]
    depth = weights_ref.shape[0] // len(pieces_of) // count
    spare = rest_ref.shape[0] // len(pieces_of) // count
    for shift, ref in enumerate(pieces_of):
        start = lax.rem(win_ref[0] + len(pieces_of) - shift, len(pieces_of)) * count
        for i in range(count):
            piece = ref[i].astype(jnp.float32)
            weights_ref[pl.ds(pl.multiple_of((start + i) * depth, 8), depth), :] = piece[:depth]
            rest_ref[pl.ds(pl.multiple_of((start + i) * spare, 8), spare), :] = piece[depth:]
    place = 0
    for ref in (query_ref, out_ref):
        depth = ref.shape[0]
        for col in range(0, ref.shape[1], HALF):
            ref[:, col : col + HALF] = weights_ref[place : place + depth, :]
            place += depth
    place = keyval_ref.shape[0]
    keyval_ref[...] = rest_ref[:place, :]
    depth = rows_ref.shape[0]
    rows_ref[...] = rest_ref[place : place + depth, :] + rest_ref[place + depth : place + 2 * depth, :]


def like(*shape, dtype=jnp.float32):
    return jax.ShapeDtypeStruct(shape, dtype)


def run(kernel, outs, scratch, limit, flops, name, *args):
    return pl.pallas_call(
        kernel,
        out_shape=outs,
        in_specs=[VM] * len(args),
        out_specs=tuple(VM for _ in outs),
        scratch_shapes=scratch,
        compiler_params=pltpu.CompilerParams(vmem_limit_bytes=limit * 2**20),
        cost_estimate=pl.CostEstimate(flops=flops, bytes_accessed=2**20, transcendentals=0),
        name=name,
    )(*args)


def residual(attended, tokens, pair, bias, gain, shift):
    outs = (like(*tokens.shape), like(*tokens.shape, dtype=jnp.bfloat16))
    return run(residual_kernel, outs, [], 12, 10**9, "residual", attended, tokens, *pair, bias, gain, shift)


def own_keyval_blocks(tokens, cotangent, gain, shift, weight, bias, count):
    outs = (
        like(count, tokens.shape[0], weight.shape[1], dtype=jnp.bfloat16),
        like(*tokens.shape, dtype=jnp.bfloat16),
    )
    return run(own_kernel, outs, [], 60, 10**8, "own_keyval", tokens, cotangent, gain, shift, weight, bias)


def query_rows(own, received, gain, shift, pair, biases):
    low16 = like(*own.shape, dtype=jnp.bfloat16)
    outs = (low16, low16, low16)
    return run(
        query_kernel, outs, [], 12, 3 * 10**10, "query_rows", own, received, gain, shift, *pair, *biases
    )


def mlp(own, peer, own_grad, peer_grad, expand, bias, contract):
    rows, features = own.shape
    hidden = expand.shape[1]
    b16 = jnp.bfloat16
    outs = (
        like(hidden, features, dtype=b16),
        like(features, hidden, dtype=b16),
        like(1, hidden),
        like(rows, features),
        like(rows, features, dtype=b16),
        like(rows, features),
        like(rows, features, dtype=b16),
    )
    scratch = [
        pltpu.VMEM((2 * rows, features), b16),
        pltpu.VMEM((features, 2 * rows), b16),
        pltpu.VMEM((2 * rows, features), b16),
        pltpu.VMEM((2 * rows, hidden), b16),
        pltpu.VMEM((2 * rows, hidden), b16),
    ]
    return run(
        mlp_kernel, outs, scratch, 32, 10**10, "mlp", own, peer, own_grad, peer_grad, expand, bias, contract
    )


def widen(contract, expand):
    steps = 2

    def spec(array):
        return pl.BlockSpec((array.shape[0] // steps, array.shape[1]), lambda i: (i, 0))

    return pl.pallas_call(
        widen_kernel,
        grid=(steps,),
        out_shape=(like(*contract.shape), like(*expand.shape)),
        in_specs=[spec(contract), spec(expand)],
        out_specs=(spec(contract), spec(expand)),
        compiler_params=pltpu.CompilerParams(vmem_limit_bytes=60 * 2**20),
        name="widen",
    )(contract, expand)


def residual_back(back, peer_back, grad, middle, gain, pair):
    rows, features = grad.shape
    b16 = jnp.bfloat16
    outs = (like(rows, features), like(rows, features, dtype=b16), like(rows, features, dtype=b16), like(8, features))
    return run(
        residual_back_kernel, outs, [], 12, 10**9, "residual_back", back, peer_back, grad, middle, gain, *pair
    )


SWAP = ((0, 1), (1, 0))


def query_back(grad, normed, attended, lowered, pair):
    rows, features = grad.shape
    width = pair[0].shape[1]
    b16 = jnp.bfloat16
    outs = (
        like(rows, features),
        like(2 * features * width // HALF, HALF),
        like(2 * features * width // HALF, HALF, dtype=b16),
        like(1, features),
    )
    return run(query_back_kernel, outs, [], 16, 10**10, "query_back", grad, normed, attended, lowered, *pair)


def token_back(ranks, arrived, normed_grad, weight, tokens, gain, normed, middle_grad, vectors):
    count, features = normed.shape
    depth = weight.shape[0] + 2 * VECTOR_ROWS
    depth += -depth % (16 * ranks)
    outs = (
        like(count // 2, features),
        like(count // 2, features, dtype=jnp.bfloat16),
        like(depth, HALF, dtype=jnp.bfloat16),
    )
    return run(
        token_back_kernel, outs, [pltpu.VMEM((VECTOR_ROWS, HALF), jnp.float32)], 12, 10**9, "token_back",
        arrived, normed_grad, weight, tokens, gain, normed, middle_grad, *vectors,
    )


def pack(win, part, peer):
    depth = part.shape[0] // 4
    outs = (like(depth, HALF), *(like(depth, HALF, dtype=jnp.bfloat16) for _ in range(3)))
    return pl.pallas_call(
        pack_kernel,
        out_shape=outs,
        in_specs=[SM] + [VM] * 2,
        out_specs=(VM,) * 4,
        compiler_params=pltpu.CompilerParams(vmem_limit_bytes=16 * 2**20),
        name="pack",
    )(win, part, peer)


def unpack(win, parts, rest_rows, query_shape, out_shape, keyval_shape):
    outs = (like(*query_shape), like(*out_shape), like(*keyval_shape), like(VECTOR_ROWS, HALF))
    weight_rows = (math.prod(query_shape) + math.prod(out_shape)) // HALF
    return pl.pallas_call(
        unpack_kernel,
        out_shape=outs,
        in_specs=[SM] + [VM] * 4,
        out_specs=(VM,) * 4,
        scratch_shapes=[pltpu.VMEM((weight_rows, HALF), jnp.float32), pltpu.VMEM((rest_rows, HALF), jnp.float32)],
        compiler_params=pltpu.CompilerParams(vmem_limit_bytes=20 * 2**20),
        name="unpack",
    )(win, *parts)


def low(value):
    return value.astype(jnp.bfloat16)


def swapped(value):
    return lax.ppermute(value, "heads", SWAP)


def opposite(value):
    count = lax.axis_size(("seq", "heads"))
    return lax.ppermute(value, ("seq", "heads"), [(i, count - 1 - i) for i in range(count)])


def exchanged(value):
    half = value.shape[0] // 2
    return jnp.concatenate([value[:half], opposite(value[half:])], axis=0)


def spread_out(blocks, axis):
    return lax.all_to_all(blocks, axis, split_axis=0, concat_axis=0, tiled=True)


def copies(value, axis):
    return spread_out(jnp.broadcast_to(value[None], (lax.axis_size(axis), *value.shape)), axis)


def per_device(
    tokens,
    first_gain,
    first_shift,
    query_weight,
    query_bias,
    keyval_weight,
    value_bias,
    out_weight,
    out_bias,
    second_gain,
    second_shift,
    expand_weight,
    expand_bias,
    contract_weight,
    contract_bias,
    cotangent,
    lengths,
):
    f32 = jnp.float32
    place = lax.axis_index(("seq", "heads"))
    places = place.astype(jnp.int32).reshape(1)
    ranks = lax.axis_size(("win", "seq"))

    own_blocks, halves = own_keyval_blocks(
        tokens[0], cotangent[0], first_gain, first_shift, keyval_weight, value_bias, lax.axis_size("seq")
    )
    received = opposite(halves)
    grad_low = jnp.concatenate([cotangent[0, :HALF], received[HALF:]])
    own_blocks = spread_out(own_blocks, "seq")
    query_pair = (query_weight, swapped(query_weight))
    out_pair = (out_weight, swapped(out_weight))
    query_biases = (query_bias, swapped(query_bias))

    bounds = jnp.cumsum(lengths[0])
    first = jnp.stack(positions(place.astype(jnp.int32)))
    position = first[:, None] + jnp.arange(HALF, dtype=jnp.int32)[None, :]
    starts = jnp.max(jnp.where(bounds[None, None, :] <= position[:, :, None], bounds, 0), axis=2)
    starts = starts.astype(jnp.int32).reshape(2, 1, HALF)

    tokens_low, normed_low, query8 = query_rows(
        tokens[0], received, first_gain, first_shift, query_pair, query_biases
    )
    own_blocks, query8 = lax.optimization_barrier((own_blocks, query8))
    peer_blocks = swapped(own_blocks)
    attended, out, logs = attend(places, query8, own_blocks, peer_blocks, starts)
    width = query_bias.shape[0]
    middle, normed2_low = residual(attended, tokens_low, out_pair, out_bias, second_gain, second_shift)
    peer_grad_low = swapped(grad_low)
    contract_part, expand_part, expand_bias_part, out_rows, peer_out, back_rows, peer_back = mlp(
        normed2_low, swapped(normed2_low), grad_low, peer_grad_low, expand_weight, expand_bias, contract_weight
    )
    contract_total, expand_total = lax.psum((contract_part, expand_part), ("win", "seq"))
    middle_grad, middle_low, attended_grad, middle_sums = residual_back(
        back_rows, swapped(peer_back), grad_low, middle, second_gain, out_pair
    )

    def rest():
        query_grad, mine, theirs = attend_back(
            places, query8, own_blocks, peer_blocks, starts, attended_grad, out, logs
        )
        mlp_out = out_rows + swapped(peer_out).astype(f32)
        block_out = exchanged(low(middle + mlp_out + contract_bias))
        pair_grad = low(mine.astype(f32) + swapped(theirs).astype(f32))
        arrived = spread_out(pair_grad, "seq")
        from_query, weights_part, weights_sent, query_bias_part = query_back(
            query_grad, normed_low, attended, middle_low, query_pair
        )
        core = lax.axis_index("heads")
        turned_bias = jnp.concatenate([query_bias_part[:, width:], query_bias_part[:, :width]], axis=1)
        query_bias_part = jnp.where(core == 0, query_bias_part, turned_bias)
        wins, seqs = lax.axis_size("win"), lax.axis_size("seq")
        win = lax.axis_index("win").astype(jnp.int32)
        kept, *given = pack(win.reshape(1), weights_part, swapped(weights_sent))
        taken = [
            lax.ppermute(given[shift - 1], "win", [(i, (i + shift) % wins) for i in range(wins)]) for shift in (2, 1, 3)
        ]
        tokens_grad, half, sent = token_back(
            ranks, arrived, from_query, keyval_weight, tokens_low, first_gain, normed_low, middle_grad,
            (middle_sums, query_bias_part, expand_bias_part),
        )
        tokens_grad = jnp.concatenate([tokens_grad, opposite(half).astype(f32)], axis=0)

        sent, taken = lax.optimization_barrier((sent, taken))
        rest = spread_out(sent.reshape(wins, -1, HALF), "win")
        rest = low(jnp.sum(rest.astype(f32), axis=0)).reshape(seqs, -1, HALF)
        weights = low(kept + sum(t.astype(f32) for t in taken)).reshape(seqs, -1, HALF)
        depth = weights.shape[1]
        summed = jnp.sum(spread_out(jnp.concatenate([weights, rest], axis=1), "seq").astype(f32), axis=0)
        rest = summed[depth:]
        features = first_gain.shape[0]
        row = lax.axis_index(("win", "seq")) * rest.shape[0] + jnp.arange(rest.shape[0])[:, None]
        vectors = keyval_weight.shape[0]
        common = 7 * features // HALF + 1
        shared = row < vectors + common
        shared = shared | ((row >= vectors + VECTOR_ROWS) & (row < vectors + VECTOR_ROWS + common))
        rest = rest + jnp.where(shared, swapped(rest), 0.0)
        full = low(jnp.concatenate([summed[:depth], rest]))
        full = copies(full, "seq")
        others = {
            shift: lax.ppermute(full, "win", [(i, (i + shift) % wins) for i in range(wins)]) for shift in (2, 1, 3)
        }
        query_total, out_total, keyval_total, summed_rows = unpack(
            win.reshape(1),
            (full, others[1], others[2], others[3]),
            sent.shape[0],
            query_weight.shape,
            out_weight.shape,
            keyval_weight.shape,
        )
        summed_rows = summed_rows.reshape(-1)
        sizes = [features] * 7 + [HALF, expand_bias.shape[0]]
        totals = []
        for size in sizes:
            totals.append(summed_rows[:size])
            summed_rows = summed_rows[size:]
        query_bias_total = jnp.where(core == 0, totals[6][:width], totals[6][width:])
        return (
            block_out[None],
            tokens_grad[None],
            totals[4],
            totals[5],
            query_total,
            query_bias_total,
            keyval_total,
            totals[7][DH:],
            out_total,
            totals[0],
            totals[1],
            totals[2],
            totals[8],
            totals[3],
        )

    shapes = jax.eval_shape(rest)

    def nothing():
        return jax.tree.map(lambda s: jnp.zeros(s.shape, s.dtype), shapes)

    outs = lax.cond(lengths[0, 0] > 0, rest, nothing)
    contract_total, expand_total = widen(contract_total, expand_total)
    return (
        *outs[:12],
        expand_total,
        outs[12],
        contract_total,
        outs[13],
    )


def solution(mesh):
    return jax.shard_map(
        per_device,
        mesh=mesh,
        in_specs=(
            P("win", ("seq", "heads"), None),
            P(),
            P(),
            P(None, "heads"),
            P("heads"),
            P(),
            P(),
            P("heads", None),
            P(),
            P(),
            P(),
            P(None, "heads"),
            P("heads"),
            P("heads", None),
            P(),
            P("win", ("seq", "heads"), None),
            P("win", None),
        ),
        out_specs=(
            P("win", ("seq", "heads"), None),
            P("win", ("seq", "heads"), None),
            P(),
            P(),
            P(None, "heads"),
            P("heads"),
            P(),
            P(),
            P("heads", None),
            P(),
            P(),
            P(),
            P(None, "heads"),
            P("heads"),
            P("heads", None),
            P(),
        ),
        check_vma=False,
    )
```
